32 devices in a mesh: orb: 8 (over z, x), seg: 4 (over y, core).
Axes of the slice: x: 2, y: 2, z: 4, core: 2. Of those that a mesh axis runs over, the one named last changes fastest.
Arguments:
- coeffs: bfloat16 [64, 8192, 128], P('orb', 'seg'), as said below
- seg_count: int32 [4], P('seg'), may hold values from 1 to 2048, 4096 in all
- seg_lines: int32 [4, 2048], P('seg'), may hold values from 0 to 4095, as said below
- potential: float32 [128, 128, 128], P('seg'), may hold values from -1.5 to 0.5
Outputs:
- rotated_orbitals: bfloat16 [64, 8192, 128], P('orb', 'seg')
- rotated_applied: bfloat16 [64, 8192, 128], P('orb', 'seg')
- rotated_hamiltonian: float32 [64, 64], replicated
The draws below stay inside these ranges and needn't reach their ends.
Inputs may be any that keep to these rules, and one draw needn't show every extreme that they name: `seg_count`: the counts of the 4 regions sum to 4096. `seg_lines`: within one region the entries are distinct. `coeffs`: only the live slots are read.
All inputs are finite; a program needn't handle non-finite values. No bound on the sum of `seg_count` on one device may be relied on, other than what follows from the above.
Results may differ from the reference program's by a relative error of at most 0.0013.
The reference program's roundings to bfloat16 on the way count: a program that leaves them out, or rounds other values in their place, can miss the bound.
Values may be sent and summed in bfloat16 or wider, within the bound.
No kernel may reach another device: no remote copies, remote signals or barrier semaphores. Data moves between devices by JAX's collectives and lax.ppermute only.
A program may use at most 128 MiB of HBM per device.

```python
import math
import jax
import jax.numpy as jnp
import numpy as np
from jax import lax

NORB = 64
CX = 32
NY = 128
NZ = 128
SWEEPS = 6
SEGMAX = 2048
SLOTS = 8192
NX = 128
N_SEG = 4


def draw_coeffs(key, part):
    key = jax.random.fold_in(key, 11)
    noise_key, row_key = jax.random.split(key, 2)
    noise = jax.random.normal(noise_key, (NORB, SLOTS, NZ), jnp.float32)
    row_scale = jnp.exp(jax.random.uniform(row_key, (1, SLOTS, 1), jnp.float32, math.log(0.3), math.log(3.0)))
    mixed = noise + 0.6 * jnp.roll(noise, -1, axis=0)
    return (mixed * row_scale).astype(jnp.bfloat16)


def draw_seg_lines(key, part):
    key = jax.random.fold_in(key, 23)
    region_keys = jax.random.split(key, N_SEG)

    def one_region(region_key):
        first_key, second_key = jax.random.split(region_key)
        order = jax.random.permutation(first_key, SEGMAX)
        parity = jax.random.randint(second_key, (SEGMAX,), 0, 2)
        parity = jnp.where(order == 0, 0, jnp.where(order == SEGMAX - 1, 1, parity))
        return (2 * order + parity).astype(jnp.int32)
    return jax.vmap(one_region)(region_keys)


def block_levels(rng, extent, cuts, low, high):
    loudness, own = 1.0, jax.random.fold_in(rng, 6)
    for position, parts in cuts:
        steps = jnp.exp(jax.random.uniform(jax.random.fold_in(own, position), (parts,), jnp.float32, low / len(cuts), high / len(cuts)))
        loudness = loudness * jnp.repeat(steps, extent[position] // parts).reshape([-1 if axis == position else 1 for axis in range(len(extent))])
    return loudness


def split_up(amount, total, limit, skew):
    weights = [(1 << 20) // math.isqrt(standing ** skew) + 1 for standing in range(2, amount + 1)]
    surplus, counts = total - limit - (amount - 1), [1] * (amount - 1)
    while surplus > 0:
        movable = [i for i in range(amount - 1) if counts[i] < limit]
        mass, remaining = sum([weights[i] for i in movable]), surplus
        for i in movable:
            more = min(limit - counts[i], max(1, remaining * weights[i] // mass), surplus)
            counts[i] = counts[i] + more
            surplus = surplus - more
    return np.array([limit] + counts)


def uneven_parts(rng, amount, total, reach, skew):
    if amount == 2:
        one = jax.random.randint(rng, (), max(1, total - reach), min(reach, total - 1) + 1)
        return jnp.stack([one, total - one])
    tallies = jnp.asarray(split_up(amount, total, reach, skew), jnp.int32)
    twos = (amount - 1) // 2
    donor, sink = tallies[1:1 + 2 * twos:2], tallies[2:2 + 2 * twos:2]
    margin = jnp.minimum(donor - 1, reach - sink)
    moved = jax.random.randint(jax.random.fold_in(rng, 1), (twos,), 0, 1 << 20) % (margin + 1)
    tallies = tallies.at[1:1 + 2 * twos:2].set(donor - moved).at[2:2 + 2 * twos:2].set(sink + moved)
    return tallies[jax.random.permutation(jax.random.fold_in(rng, 2), amount)]


def setup_inputs(seed: int = 0) -> dict:
    streams_of = jax.random.split(jax.random.key(seed), 5)
    coeffs = draw_coeffs(jax.random.fold_in(streams_of[4], 71), 0)
    seg_count = uneven_parts(streams_of[1], N_SEG, N_SEG * SEGMAX // 2, SEGMAX, 2).astype(jnp.int32)
    seg_lines = draw_seg_lines(jax.random.fold_in(streams_of[4], 71), 0)
    potential = jnp.clip(-1.5 + 2.0 * jax.random.uniform(streams_of[3], (NX, NY, NZ), jnp.float32) ** block_levels(streams_of[3], (NX, NY, NZ), ((0, 4),), -0.2, 0.2), -1.5, 0.5)
    return dict(coeffs=coeffs, seg_count=seg_count, seg_lines=seg_lines, potential=potential)


RADIUS = 7
KINETIC = -0.5 / 2.25

def filter_taps():
    offsets = jnp.arange(-RADIUS, RADIUS + 1)
    safe_k = jnp.where(offsets == 0, 1, offsets).astype(jnp.float32)
    signs = jnp.where(offsets % 2 == 0, -1.0, 1.0).astype(jnp.float32)
    values = jnp.where(offsets == 0, -math.pi * math.pi / 3.0, 2.0 * signs / (safe_k * safe_k))
    return values.astype(jnp.float32).astype(jnp.bfloat16)

def band_table(n_in, n_out, shift):
    weights = filter_taps().astype(jnp.float32)
    offsets = jnp.arange(-RADIUS, RADIUS + 1)
    spread = jnp.arange(n_in)[:, None] - jnp.arange(n_out)[None, :] - shift
    table = lax.optimization_barrier(jnp.sum(jnp.where(spread[:, :, None] == offsets[None, None, :], weights[None, None, :], jnp.zeros((), jnp.float32)), axis=2))
    return table.astype(jnp.bfloat16)

def inverse_root(intersection):
    high = lax.Precision.HIGHEST
    norm_scale = jnp.sqrt(jnp.sum(intersection * intersection) + 1e-06)
    identity = jnp.eye(intersection.shape[0], dtype=jnp.float32)
    upper = intersection / norm_scale
    lower = identity
    for sweep_id in range(SWEEPS):
        middle = 0.5 * (3.0 * identity - jnp.dot(lower, upper, precision=high))
        upper = jnp.dot(upper, middle, precision=high)
        lower = jnp.dot(middle, lower, precision=high)
    return lower / jnp.sqrt(norm_scale)

def reference(coeffs, seg_count, seg_lines, potential):
    live_slots = (jnp.arange(SEGMAX)[None, :] < seg_count[:, None]).reshape(-1)
    line_index = (jnp.arange(N_SEG)[:, None] * (CX * NY) + seg_lines).reshape(-1).astype(jnp.int32)
    weights = filter_taps().astype(jnp.float32)
    band_y = band_table(NY, NY, 0)
    band_z = band_table(NZ, NZ, 0)

    def apply_one(orbital):
        kept_rows = jnp.where(live_slots[:, None], orbital, jnp.zeros((), jnp.bfloat16))
        line_rows = jnp.zeros((NX * NY, NZ), jnp.bfloat16).at[line_index].set(kept_rows)
        grid_cells = line_rows.reshape(NX, NY, NZ)
        padded = jnp.pad(grid_cells, ((RADIUS, RADIUS), (0, 0), (0, 0))).astype(jnp.float32)
        sweep_x = jnp.zeros((NX, NY, NZ), jnp.float32)
        for shift_at in range(2 * RADIUS + 1):
            sweep_x = sweep_x + weights[shift_at] * padded[shift_at:shift_at + NX]
        sweep_z = jnp.dot(line_rows, band_z, preferred_element_type=jnp.float32).reshape(NX, NY, NZ)
        flipped = jnp.swapaxes(grid_cells, 1, 2).reshape(NX * NZ, NY)
        sweep_y = jnp.swapaxes(jnp.dot(flipped, band_y, preferred_element_type=jnp.float32).reshape(NX, NZ, NY), 1, 2)
        applied = KINETIC * (sweep_x + sweep_y + sweep_z) + potential * grid_cells.astype(jnp.float32)
        picked = applied.reshape(NX * NY, NZ)[line_index]
        applied_rows = jnp.where(live_slots[:, None], picked, jnp.zeros((), jnp.float32)).astype(jnp.bfloat16)
        return (kept_rows, applied_rows)
    orbitals, applied_rows = lax.map(apply_one, coeffs)
    flat_orbitals = orbitals.reshape(NORB, SLOTS * NZ)
    flat_applied = applied_rows.reshape(NORB, SLOTS * NZ)
    weight_sum = 2.0 / (SLOTS * NZ)
    intersection = jnp.dot(flat_orbitals, flat_orbitals.T, preferred_element_type=jnp.float32) * weight_sum
    hamiltonian = jnp.dot(flat_orbitals, flat_applied.T, preferred_element_type=jnp.float32) * weight_sum
    rotation = inverse_root(intersection)
    rotation_half = rotation.astype(jnp.bfloat16)
    rotated_orbitals = jnp.dot(rotation_half.T, flat_orbitals, preferred_element_type=jnp.float32).astype(jnp.bfloat16).reshape(NORB, SLOTS, NZ)
    rotated_applied = jnp.dot(rotation_half.T, flat_applied, preferred_element_type=jnp.float32).astype(jnp.bfloat16).reshape(NORB, SLOTS, NZ)
    high = lax.Precision.HIGHEST
    rotated_hamiltonian = jnp.dot(jnp.dot(rotation.T, hamiltonian, precision=high), rotation, precision=high)
    return (rotated_orbitals, rotated_applied, rotated_hamiltonian)
```

```python
import functools
import math

import jax
import jax.numpy as jnp
import ml_dtypes
import numpy as np
from jax import lax
from jax.experimental import pallas as pl
from jax.experimental.pallas import tpu as pltpu
from jax.sharding import PartitionSpec as P

SWEEPS = 6
RADIUS = 7
KINETIC = -0.5 / 2.25
TILE = 256
GROUP = 8
PITCH_PAD = 16
VMEM = 60 * 1024 * 1024


def tap_values():
    exact = [-math.pi * math.pi / 3.0]
    exact += [2.0 * (1.0 if k % 2 else -1.0) / (k * k) for k in range(1, RADIUS + 1)]
    return [float(np.float32(v).astype(ml_dtypes.bfloat16)) for v in exact]


TAPS = tap_values()


def band_matrix(n):
    table = np.zeros((n, n), np.float32)
    for i in range(n):
        for j in range(n):
            if abs(i - j) <= RADIUS:
                table[i, j] = TAPS[abs(i - j)]
    return table.astype(ml_dtypes.bfloat16)


def inverse_root(intersection):
    high = lax.Precision.HIGHEST
    norm_scale = jnp.sqrt(jnp.sum(intersection * intersection) + 1e-06)
    identity = jnp.eye(intersection.shape[0], dtype=jnp.float32)
    upper = intersection / norm_scale
    lower = identity
    for sweep_id in range(SWEEPS):
        middle = 0.5 * (3.0 * identity - jnp.dot(lower, upper, precision=high))
        upper = jnp.dot(upper, middle, precision=high)
        lower = jnp.dot(middle, lower, precision=high)
    return lower / jnp.sqrt(norm_scale)


def swapped(value, axis, distance):
    size = lax.axis_size(axis)
    return lax.ppermute(value, axis, [(i, i ^ distance) for i in range(size)])


def bits(axis):
    size = lax.axis_size(axis)
    return [1 << b for b in range(size.bit_length() - 1)]


def total(value):
    for axis in ("seg", "orb"):
        for distance in bits(axis):
            value = value + swapped(value, axis, distance)
    return value


def pack_kernel(edge_lines, grid_lines, count_ref, lines_ref, coeffs_ref, rows_ref, edge_ref):
    step = pl.program_id(0)
    count = count_ref[0]
    base = step * TILE
    live = count - base
    dump = 2 * edge_lines

    @pl.when(step == 0)
    def _():
        edge_ref[...] = jnp.zeros_like(edge_ref)

    @pl.when(live > 0)
    def _():
        tile = jnp.swapaxes(coeffs_ref[...].astype(jnp.float32), 0, 1)
        row = lax.broadcasted_iota(jnp.int32, tile.shape, 0)
        rows_ref[...] = jnp.where(row < live, tile, 0.0).astype(jnp.bfloat16)

        @pl.loop(0, TILE // GROUP)
        def _(group):
            for u in range(GROUP):
                j = group * GROUP + u
                line = lines_ref[base + j]
                tail = line - (grid_lines - 2 * edge_lines)
                place = jnp.where(line < edge_lines, line, jnp.where(tail >= edge_lines, tail, dump))
                place = jnp.where(j < live, place, dump)
                edge_ref[place] = rows_ref[j]

    @pl.when(live <= 0)
    def _():
        rows_ref[...] = jnp.zeros_like(rows_ref)


def pack(coeffs, seg_count, lines, grid_lines, cells_y, rows_out):
    orbs, slot_count, depth = coeffs.shape
    edge_lines = RADIUS * cells_y
    last = slot_count // TILE - 1
    return pl.pallas_call(
        functools.partial(pack_kernel, edge_lines, grid_lines),
        grid=(rows_out // TILE,),
        in_specs=[
            pl.BlockSpec(memory_space=pltpu.SMEM),
            pl.BlockSpec(memory_space=pltpu.SMEM),
            pl.BlockSpec((orbs, TILE, depth), lambda i: (0, jnp.minimum(i, last), 0)),
        ],
        out_specs=[
            pl.BlockSpec((TILE, orbs, depth), lambda i: (i, 0, 0)),
            pl.BlockSpec((2 * edge_lines + 8, orbs, depth), lambda i: (0, 0, 0)),
        ],
        out_shape=[
            jax.ShapeDtypeStruct((rows_out, orbs, depth), jnp.bfloat16),
            jax.ShapeDtypeStruct((2 * edge_lines + 8, orbs, depth), jnp.bfloat16),
        ],
        compiler_params=pltpu.CompilerParams(vmem_limit_bytes=VMEM),
        cost_estimate=pl.CostEstimate(flops=0, bytes_accessed=14 << 20, transcendentals=0),
        name="pack_slots",
    )(seg_count, lines, coeffs)


def apply_kernel(
    cells_x,
    cells_y,
    count_ref,
    lines_ref,
    rows_ref,
    low_ref,
    high_ref,
    potential_ref,
    band_ref,
    applied_ref,
    grid_ref,
    zsum_ref,
):
    step = pl.program_id(0)
    pitch = cells_y + PITCH_PAD
    count = count_ref[0]
    base = step * TILE
    live = jnp.minimum(count - base, TILE)
    shift = cells_y.bit_length() - 1

    def place_of(line):
        return line + lax.shift_right_logical(line, shift) * PITCH_PAD + (RADIUS * pitch + RADIUS)

    @pl.when(step == 0)
    def _():
        @pl.loop(0, grid_ref.shape[0] // 16)
        def _(block):
            grid_ref[pl.ds(block * 16, 16)] = jnp.zeros((16,) + grid_ref.shape[1:], jnp.float32)

        for plane in range(RADIUS):
            for source, at in ((low_ref, plane), (high_ref, plane + RADIUS + cells_x)):

                @pl.loop(0, cells_y // 16)
                def _(block, source=source, at=at, plane=plane):
                    grid_ref[pl.ds(at * pitch + RADIUS + block * 16, 16)] = source[
                        pl.ds(plane * cells_y + block * 16, 16)
                    ].astype(jnp.float32)

        @pl.loop(0, lax.div(count + GROUP - 1, GROUP))
        def _(group):
            for u in range(GROUP):
                j = group * GROUP + u
                place = jnp.where(j < count, place_of(lines_ref[j]), grid_ref.shape[0] - 1)
                grid_ref[place] = rows_ref[j].astype(jnp.float32)

    applied_ref[...] = jnp.zeros_like(applied_ref)

    @pl.when(live > 0)
    def _():
        tile = rows_ref[pl.ds(base, TILE)].astype(jnp.float32)
        flat = tile.reshape(TILE * tile.shape[1], tile.shape[2]).astype(jnp.bfloat16)
        zsum = jnp.dot(flat, band_ref[...], preferred_element_type=jnp.float32)
        zsum_ref[...] = (KINETIC * zsum).reshape(zsum_ref.shape)

        @pl.loop(0, lax.div(live + GROUP - 1, GROUP))
        def _(group):
            for u in range(GROUP):
                j = group * GROUP + u
                line = lines_ref[base + j]
                at = place_of(line)
                center = grid_ref[at]
                value = zsum_ref[j] + center * (
                    potential_ref[pl.ds(line, 1), :] + (2.0 * KINETIC * TAPS[0])
                )
                for k in range(1, RADIUS + 1):
                    near = (grid_ref[at - k] + grid_ref[at + k]) + (
                        grid_ref[at - k * pitch] + grid_ref[at + k * pitch]
                    )
                    value = value + (KINETIC * TAPS[k]) * near
                applied_ref[j] = jnp.where(j < live, value, 0.0).astype(jnp.bfloat16)


def apply_rows(rows, seg_count, lines, low, high, potential):
    rows_out, orbs, depth = rows.shape
    cells_x, cells_y, _ = potential.shape
    slot_count = lines.shape[0]
    edge_lines = RADIUS * cells_y
    pitch = cells_y + PITCH_PAD
    grid_rows = (cells_x + 2 * RADIUS) * pitch + 16
    once = pl.Buffered(1)
    whole = lambda i: (0, 0, 0)
    return pl.pallas_call(
        functools.partial(apply_kernel, cells_x, cells_y),
        grid=(rows_out // TILE,),
        in_specs=[
            pl.BlockSpec(memory_space=pltpu.SMEM),
            pl.BlockSpec(memory_space=pltpu.SMEM),
            pl.BlockSpec((slot_count, orbs, depth), whole, pipeline_mode=once),
            pl.BlockSpec((edge_lines, orbs, depth), whole, pipeline_mode=once),
            pl.BlockSpec((edge_lines, orbs, depth), whole, pipeline_mode=once),
            pl.BlockSpec((cells_x * cells_y, depth), lambda i: (0, 0), pipeline_mode=once),
            pl.BlockSpec((depth, depth), lambda i: (0, 0), pipeline_mode=once),
        ],
        out_specs=pl.BlockSpec((TILE, orbs, depth), lambda i: (i, 0, 0)),
        out_shape=jax.ShapeDtypeStruct((rows_out, orbs, depth), jnp.bfloat16),
        scratch_shapes=[
            pltpu.VMEM((grid_rows, orbs, depth), jnp.float32),
            pltpu.VMEM((TILE, orbs, depth), jnp.float32),
        ],
        compiler_params=pltpu.CompilerParams(vmem_limit_bytes=VMEM),
        cost_estimate=pl.CostEstimate(flops=2 << 30, bytes_accessed=60 << 20, transcendentals=0),
        name="apply_rows",
    )(
        seg_count,
        lines,
        rows,
        low,
        high,
        potential.reshape(cells_x * cells_y, depth),
        jnp.asarray(band_matrix(depth)),
    )


def unpack_kernel(rows_ref, out_ref):
    tile = jnp.swapaxes(rows_ref[...].astype(jnp.float32), 0, 1)
    out_ref[...] = tile.astype(jnp.bfloat16)


def unpack(rows, slot_count):
    _, orbs, depth = rows.shape
    return pl.pallas_call(
        unpack_kernel,
        grid=(slot_count // TILE,),
        in_specs=[pl.BlockSpec((TILE, orbs, depth), lambda i: (i, 0, 0))],
        out_specs=pl.BlockSpec((orbs, TILE, depth), lambda i: (0, i, 0)),
        out_shape=jax.ShapeDtypeStruct((orbs, slot_count, depth), jnp.bfloat16),
        compiler_params=pltpu.CompilerParams(vmem_limit_bytes=VMEM),
        cost_estimate=pl.CostEstimate(flops=0, bytes_accessed=8 << 20, transcendentals=0),
        name="unpack_slots",
    )(rows)


def body(coeffs, seg_count, seg_lines, potential):
    orbs, slot_count, depth = coeffs.shape
    cells_x, cells_y, _ = potential.shape
    n_orb, n_seg = lax.axis_size("orb"), lax.axis_size("seg")
    lines = seg_lines[0]
    move = slot_count // 2
    padded = slot_count + move
    edge_lines = RADIUS * cells_y
    weight_sum = 2.0 / (n_seg * slot_count * depth)

    partner_count = swapped(seg_count, "seg", 1)
    both = seg_count + partner_count
    core = lax.rem(lax.axis_index("seg"), 2)
    share = (both[0] + 1 - core) // 2
    own = jnp.minimum(seg_count[0], share)
    most = (both + 1) // 2
    for distance in bits("seg")[1:]:
        most = jnp.maximum(most, swapped(most, "seg", distance))

    rows, edges = pack(coeffs, seg_count, lines, cells_x * cells_y, cells_y, padded)

    def balance(value, start):
        sent = lax.dynamic_slice_in_dim(value, start, move, axis=0)
        return lax.dynamic_update_slice_in_dim(value, swapped(sent, "seg", 1), own, axis=0)

    def rest(used, operands):
        rows, edges = operands
        part = used // n_orb
        ends = n_seg - 1

        def spread(value):
            return lax.all_to_all(value[:used], "orb", split_axis=0, concat_axis=0, tiled=True).reshape(
                n_orb, part, orbs, depth
            )

        def collect(value):
            value = lax.all_to_all(
                value.reshape(n_orb * part, orbs, depth), "orb", split_axis=0, concat_axis=0, tiled=True
            )
            value = jnp.pad(value, ((0, padded - used), (0, 0), (0, 0)))
            return unpack(balance(value, own), slot_count)

        slot_orbitals = spread(balance(rows, share))
        low = lax.ppermute(
            edges[edge_lines : 2 * edge_lines], "seg", [(i, i + 1) for i in range(ends)]
        )
        high = lax.ppermute(edges[:edge_lines], "seg", [(i + 1, i) for i in range(ends)])
        applied = apply_rows(rows, seg_count, lines, low, high, potential)
        slot_applied = spread(balance(applied, share))

        def gram(left, right):
            return jnp.einsum("asoz,bspz->aobp", left, right, preferred_element_type=jnp.float32).reshape(
                n_orb * orbs, n_orb * orbs
            )

        intersection = total(gram(slot_orbitals, slot_orbitals)) * weight_sum
        rotation = inverse_root(intersection)
        half = rotation.astype(jnp.bfloat16).reshape(n_orb, orbs, n_orb, orbs)

        def turn(value):
            return jnp.einsum("aobp,asoz->bspz", half, value, preferred_element_type=jnp.float32).astype(
                jnp.bfloat16
            )

        rotated_orbitals = collect(turn(slot_orbitals))
        rotated_applied = collect(turn(slot_applied))
        hamiltonian = total(gram(slot_orbitals, slot_applied)) * weight_sum
        high_p = lax.Precision.HIGHEST
        rotated_hamiltonian = jnp.dot(
            jnp.dot(rotation.T, hamiltonian, precision=high_p), rotation, precision=high_p
        )
        return rotated_orbitals, rotated_applied, rotated_hamiltonian

    first = slot_count // 2
    grain = slot_count // 8
    classes = [first + grain * (i + 1) for i in range(4)]
    chosen = jnp.clip((most[0] - first + grain - 1) // grain - 1, 0, len(classes) - 1)
    return lax.switch(chosen, [functools.partial(rest, used) for used in classes], (rows, edges))


def solution(mesh):
    in_specs = (P("orb", "seg", None), P("seg"), P("seg", None), P("seg", None, None))
    out_specs = (P("orb", "seg", None), P("orb", "seg", None), P())
    return jax.shard_map(body, mesh=mesh, in_specs=in_specs, out_specs=out_specs, check_vma=False)
```

```python
import functools
import math

import jax
import jax.numpy as jnp
import ml_dtypes
import numpy as np
from jax import lax
from jax.experimental import pallas as pl
from jax.experimental.pallas import tpu as pltpu
from jax.sharding import PartitionSpec as P

SWEEPS = 6
RADIUS = 7
KINETIC = -0.5 / 2.25
TILE = 256
GROUP = 8
PITCH_PAD = 16
VMEM = 60 * 1024 * 1024


def tap_values():
    exact = [-math.pi * math.pi / 3.0]
    exact += [2.0 * (1.0 if k % 2 else -1.0) / (k * k) for k in range(1, RADIUS + 1)]
    return [float(np.float32(v).astype(ml_dtypes.bfloat16)) for v in exact]


TAPS = tap_values()


def band_matrix(n):
    table = np.zeros((n, n), np.float32)
    for i in range(n):
        for j in range(n):
            if abs(i - j) <= RADIUS:
                table[i, j] = TAPS[abs(i - j)]
    return table.astype(ml_dtypes.bfloat16)


def inverse_root(intersection):
    high = lax.Precision.HIGHEST
    norm_scale = jnp.sqrt(jnp.sum(intersection * intersection) + 1e-06)
    identity = jnp.eye(intersection.shape[0], dtype=jnp.float32)
    upper = intersection / norm_scale
    lower = identity
    for sweep_id in range(SWEEPS):
        middle = 0.5 * (3.0 * identity - jnp.dot(lower, upper, precision=high))
        upper = jnp.dot(upper, middle, precision=high)
        lower = jnp.dot(middle, lower, precision=high)
    return lower / jnp.sqrt(norm_scale)


def swapped(value, axis, distance):
    size = lax.axis_size(axis)
    return lax.ppermute(value, axis, [(i, i ^ distance) for i in range(size)])


def bits(axis):
    size = lax.axis_size(axis)
    return [1 << b for b in range(size.bit_length() - 1)]


def total(value):
    for axis in ("seg", "orb"):
        for distance in bits(axis):
            value = value + swapped(value, axis, distance)
    return value


def call(kernel, name, cost, **kwargs):
    flops, megabytes = cost
    return pl.pallas_call(
        kernel,
        name=name,
        compiler_params=pltpu.CompilerParams(vmem_limit_bytes=VMEM),
        cost_estimate=pl.CostEstimate(
            flops=flops, bytes_accessed=megabytes << 20, transcendentals=0
        ),
        **kwargs,
    )


def smem():
    return pl.BlockSpec(memory_space=pltpu.SMEM)


def untouched():
    return pl.BlockSpec(memory_space=pl.ANY)


def pack_kernel(first_turned, count_ref, coeffs_ref, rows_ref, turned_ref):
    step = pl.program_id(0)
    tile_rows = rows_ref.shape[0]
    live = count_ref[0] - step * tile_rows
    tile = jnp.swapaxes(coeffs_ref[...].astype(jnp.float32), 0, 1)
    row = lax.broadcasted_iota(jnp.int32, tile.shape, 0)
    rows_ref[...] = jnp.where(row < live, tile, 0.0).astype(jnp.bfloat16)

    @pl.when(step >= first_turned)
    def _():
        for j in range(tile_rows):
            turned_ref[tile_rows - 1 - j] = rows_ref[j]


def pack(coeffs, seg_count):
    orbs, slot_count, depth = coeffs.shape
    steps = slot_count // TILE
    half = steps // 2
    return call(
        functools.partial(pack_kernel, half),
        "pack_slots",
        (0, 10),
        grid=(steps,),
        in_specs=[smem(), pl.BlockSpec((orbs, TILE, depth), lambda i: (0, i, 0))],
        out_specs=[
            pl.BlockSpec((TILE, orbs, depth), lambda i: (i, 0, 0)),
            pl.BlockSpec(
                (TILE, orbs, depth), lambda i: (jnp.minimum(steps - 1 - i, half - 1), 0, 0)
            ),
        ],
        out_shape=[
            jax.ShapeDtypeStruct((slot_count, orbs, depth), jnp.bfloat16),
            jax.ShapeDtypeStruct((slot_count // 2, orbs, depth), jnp.bfloat16),
        ],
    )(seg_count, coeffs)


def merge(rows, received, seg_count, used, order=None):
    slot_count, orbs, depth = rows.shape
    if used == slot_count:
        return rows
    free = (used - received.shape[0]) // TILE
    assert free * TILE == used - received.shape[0]

    def kernel(count_ref, own_ref, other_ref, order_ref, out_ref):
        step = pl.program_id(0)
        live = count_ref[0] - step * TILE
        row = lax.broadcasted_iota(jnp.int32, out_ref.shape, 0)

        @pl.when(step < free)
        def _():
            out_ref[...] = own_ref[...]

        @pl.when(step >= free)
        def _():
            own, other = own_ref[...].astype(jnp.float32), other_ref[...].astype(jnp.float32)
            out_ref[...] = jnp.where(row < live, own, other).astype(jnp.bfloat16)

    return call(
        kernel,
        "merge_rows",
        (0, 8),
        grid=(used // TILE,),
        in_specs=[
            smem(),
            pl.BlockSpec((TILE, orbs, depth), lambda i: (i, 0, 0)),
            pl.BlockSpec((TILE, orbs, depth), lambda i: (jnp.maximum(i - free, 0), 0, 0)),
            untouched(),
        ],
        out_specs=pl.BlockSpec((TILE, orbs, depth), lambda i: (i, 0, 0)),
        out_shape=jax.ShapeDtypeStruct((used, orbs, depth), jnp.bfloat16),
    )(seg_count, rows, received, rows if order is None else order)


def edge_kernel(edge_lines, grid_lines, count_ref, lines_ref, rows_ref, order_ref, edge_ref):
    count = count_ref[0]
    dump = 2 * edge_lines

    @pl.loop(0, edge_ref.shape[0] // 8)
    def _(block):
        edge_ref[pl.ds(block * 8, 8)] = jnp.zeros((8,) + edge_ref.shape[1:], edge_ref.dtype)

    @pl.loop(0, lax.div(count + GROUP - 1, GROUP))
    def _(group):
        for u in range(GROUP):
            j = group * GROUP + u
            line = lines_ref[j]
            tail = line - (grid_lines - 2 * edge_lines)
            place = jnp.where(line < edge_lines, line, jnp.where(tail >= edge_lines, tail, dump))
            place = jnp.where(j < count, place, dump)
            edge_ref[place] = rows_ref[j]


def edges_of(rows, seg_count, lines, order, grid_lines, cells_y):
    slot_count, orbs, depth = rows.shape
    edge_lines = RADIUS * cells_y
    return call(
        functools.partial(edge_kernel, edge_lines, grid_lines),
        "edge_planes",
        (0, 8),
        in_specs=[smem(), smem(), pl.BlockSpec(memory_space=pltpu.VMEM), untouched()],
        out_specs=pl.BlockSpec(memory_space=pltpu.VMEM),
        out_shape=jax.ShapeDtypeStruct((2 * edge_lines + 8, orbs, depth), jnp.bfloat16),
    )(seg_count, lines, rows, order)


def apply_kernel(
    cells_x,
    cells_y,
    count_ref,
    lines_ref,
    rows_ref,
    low_ref,
    high_ref,
    potential_ref,
    band_ref,
    applied_ref,
    turned_ref,
    grid_ref,
    zsum_ref,
):
    step = pl.program_id(0)
    pitch = cells_y + PITCH_PAD
    count = count_ref[0]
    base = step * TILE
    live = jnp.minimum(count - base, TILE)
    shift = cells_y.bit_length() - 1

    def place_of(line):
        return line + lax.shift_right_logical(line, shift) * PITCH_PAD + (RADIUS * pitch + RADIUS)

    @pl.when(step == 0)
    def _():
        @pl.loop(0, grid_ref.shape[0] // 16)
        def _(block):
            grid_ref[pl.ds(block * 16, 16)] = jnp.zeros((16,) + grid_ref.shape[1:], jnp.float32)

        for plane in range(RADIUS):
            for source, at in ((low_ref, plane), (high_ref, plane + RADIUS + cells_x)):

                @pl.loop(0, cells_y // 16)
                def _(block, source=source, at=at, plane=plane):
                    grid_ref[pl.ds(at * pitch + RADIUS + block * 16, 16)] = source[
                        pl.ds(plane * cells_y + block * 16, 16)
                    ].astype(jnp.float32)

        @pl.loop(0, lax.div(count + GROUP - 1, GROUP))
        def _(group):
            for u in range(GROUP):
                j = group * GROUP + u
                place = jnp.where(j < count, place_of(lines_ref[j]), grid_ref.shape[0] - 1)
                grid_ref[place] = rows_ref[j].astype(jnp.float32)

    applied_ref[...] = jnp.zeros_like(applied_ref)

    @pl.when(live > 0)
    def _():
        tile = rows_ref[pl.ds(base, TILE)].astype(jnp.float32)
        flat = tile.reshape(TILE * tile.shape[1], tile.shape[2]).astype(jnp.bfloat16)
        zsum = jnp.dot(flat, band_ref[...], preferred_element_type=jnp.float32)
        zsum_ref[...] = (KINETIC * zsum).reshape(zsum_ref.shape)

        @pl.loop(0, lax.div(live + GROUP - 1, GROUP))
        def _(group):
            for u in range(GROUP):
                j = group * GROUP + u
                line = lines_ref[base + j]
                at = place_of(line)
                center = grid_ref[at]
                value = zsum_ref[j] + center * (
                    potential_ref[pl.ds(line, 1), :] + (2.0 * KINETIC * TAPS[0])
                )
                for k in range(1, RADIUS + 1):
                    near = (grid_ref[at - k] + grid_ref[at + k]) + (
                        grid_ref[at - k * pitch] + grid_ref[at + k * pitch]
                    )
                    value = value + (KINETIC * TAPS[k]) * near
                applied_ref[j] = jnp.where(j < live, value, 0.0).astype(jnp.bfloat16)

    @pl.when(step >= pl.num_programs(0) // 2)
    def _():
        for j in range(TILE):
            turned_ref[TILE - 1 - j] = applied_ref[j]


def apply_rows(rows, seg_count, lines, low, high, potential):
    slot_count, orbs, depth = rows.shape
    cells_x, cells_y, _ = potential.shape
    edge_lines = RADIUS * cells_y
    grid_rows = (cells_x + 2 * RADIUS) * (cells_y + PITCH_PAD) + 16
    once = pl.Buffered(1)
    whole = lambda i: (0, 0, 0)
    steps = slot_count // TILE
    half = steps // 2
    return call(
        functools.partial(apply_kernel, cells_x, cells_y),
        "apply_rows",
        (2 << 30, 80),
        grid=(steps,),
        in_specs=[
            smem(),
            smem(),
            pl.BlockSpec((slot_count, orbs, depth), whole, pipeline_mode=once),
            pl.BlockSpec((edge_lines, orbs, depth), whole, pipeline_mode=once),
            pl.BlockSpec((edge_lines, orbs, depth), whole, pipeline_mode=once),
            pl.BlockSpec((cells_x * cells_y, depth), lambda i: (0, 0), pipeline_mode=once),
            pl.BlockSpec((depth, depth), lambda i: (0, 0), pipeline_mode=once),
        ],
        out_specs=[
            pl.BlockSpec((TILE, orbs, depth), lambda i: (i, 0, 0)),
            pl.BlockSpec(
                (TILE, orbs, depth), lambda i: (jnp.minimum(steps - 1 - i, half - 1), 0, 0)
            ),
        ],
        out_shape=[
            jax.ShapeDtypeStruct((slot_count, orbs, depth), jnp.bfloat16),
            jax.ShapeDtypeStruct((slot_count // 2, orbs, depth), jnp.bfloat16),
        ],
        scratch_shapes=[
            pltpu.VMEM((grid_rows, orbs, depth), jnp.float32),
            pltpu.VMEM((TILE, orbs, depth), jnp.float32),
        ],
    )(
        seg_count,
        lines,
        rows,
        low,
        high,
        potential.reshape(cells_x * cells_y, depth),
        jnp.asarray(band_matrix(depth)),
    )


def unpack(rows, returned, seg_count, slot_count, order):
    used, orbs, depth = rows.shape
    kept = used // TILE
    steps = slot_count // TILE

    def kernel(count_ref, rows_ref, returned_ref, order_ref, out_ref, turned_ref):
        step = pl.program_id(0)
        live = count_ref[0] - step * TILE
        row = lax.broadcasted_iota(jnp.int32, rows_ref.shape, 0)

        def put(tile):
            tile = jnp.where(row < live, tile.astype(jnp.float32), 0.0)
            out_ref[...] = jnp.swapaxes(tile, 0, 1).astype(jnp.bfloat16)

        @pl.when(step < kept)
        def _():
            put(rows_ref[...])

        @pl.when(step >= kept)
        def _():
            for j in range(TILE):
                turned_ref[j] = returned_ref[TILE - 1 - j]
            put(turned_ref[...])

    return call(
        kernel,
        "unpack_slots",
        (0, 10),
        grid=(steps,),
        in_specs=[
            smem(),
            pl.BlockSpec((TILE, orbs, depth), lambda i: (jnp.minimum(i, kept - 1), 0, 0)),
            pl.BlockSpec(
                (TILE, orbs, depth),
                lambda i: (jnp.clip(steps - 1 - i, 0, max(steps - kept - 1, 0)), 0, 0),
            ),
            untouched(),
        ],
        out_specs=pl.BlockSpec((orbs, TILE, depth), lambda i: (0, i, 0)),
        out_shape=jax.ShapeDtypeStruct((orbs, slot_count, depth), jnp.bfloat16),
        scratch_shapes=[pltpu.VMEM((TILE, orbs, depth), jnp.bfloat16)],
    )(seg_count, rows, returned, order)


def body(coeffs, seg_count, seg_lines, potential):
    orbs, slot_count, depth = coeffs.shape
    cells_x, cells_y, _ = potential.shape
    n_orb, n_seg = lax.axis_size("orb"), lax.axis_size("seg")
    ends = n_seg - 1
    norb = n_orb * orbs
    lines = seg_lines[0]
    edge_lines = RADIUS * cells_y
    weight_sum = 2.0 / (n_seg * slot_count * depth)

    most = seg_count + swapped(seg_count, "seg", 1)
    for distance in bits("seg")[1:]:
        most = jnp.maximum(most, swapped(most, "seg", distance))
    rows, turned = pack(coeffs, seg_count)

    def rest(used, operands):
        rows, turned = operands
        moved = slot_count - used

        def spread(value):
            value = lax.all_to_all(value, "orb", split_axis=0, concat_axis=0, tiled=True)
            return value.reshape(n_orb, used // n_orb, orbs, depth)

        def to_partner(value, turned, order=None):
            if not moved:
                return value
            received = swapped(turned[:moved], "seg", 1)
            return merge(value, received, seg_count, used, order)

        def collect(value, order):
            value = value.reshape(used, orbs, depth)
            value = lax.all_to_all(value, "orb", split_axis=0, concat_axis=0, tiled=True)
            returned = swapped(value[used - moved :], "seg", 1) if moved else value
            return unpack(value, returned, seg_count, slot_count, order)

        def gram(left, right):
            product = jnp.einsum("asoz,bspz->aobp", left, right, preferred_element_type=jnp.float32)
            return product.reshape(norb, norb)

        merged = to_partner(rows, turned)
        slot_orbitals = spread(merged)

        edges = edges_of(rows, seg_count, lines, merged, cells_x * cells_y, cells_y)
        low = lax.ppermute(
            edges[edge_lines : 2 * edge_lines], "seg", [(i, i + 1) for i in range(ends)]
        )
        high = lax.ppermute(edges[:edge_lines], "seg", [(i + 1, i) for i in range(ends)])
        applied, turned_applied = apply_rows(rows, seg_count, lines, low, high, potential)
        slot_applied = spread(to_partner(applied, turned_applied, slot_orbitals))

        intersection = total(gram(slot_orbitals, slot_orbitals)) * weight_sum
        rotation = inverse_root(intersection)
        half = rotation.astype(jnp.bfloat16).reshape(n_orb, orbs, n_orb, orbs)

        def turn(value):
            return jnp.einsum(
                "aobp,asoz->bspz", half, value, preferred_element_type=jnp.float32
            ).astype(jnp.bfloat16)

        rotated_orbitals = collect(turn(slot_orbitals), half)
        hamiltonian = total(gram(slot_orbitals, slot_applied)) * weight_sum
        precise = lax.Precision.HIGHEST
        rotated_hamiltonian = jnp.dot(
            jnp.dot(rotation.T, hamiltonian, precision=precise), rotation, precision=precise
        )
        slot_turned, rotated_hamiltonian = lax.optimization_barrier(
            (turn(slot_applied), rotated_hamiltonian)
        )
        rotated_applied = collect(slot_turned, rotated_orbitals)
        return rotated_orbitals, rotated_applied, rotated_hamiltonian

    first = slot_count // 2
    classes = [first + TILE * (i + 1) for i in range((slot_count - first) // TILE)]
    chosen = jnp.clip(((most[0] + 1) // 2 - first + TILE - 1) // TILE - 1, 0, len(classes) - 1)
    return lax.switch(chosen, [functools.partial(rest, used) for used in classes], (rows, turned))


def solution(mesh):
    in_specs = (P("orb", "seg", None), P("seg"), P("seg", None), P("seg", None, None))
    out_specs = (P("orb", "seg", None), P("orb", "seg", None), P())
    return jax.shard_map(body, mesh=mesh, in_specs=in_specs, out_specs=out_specs, check_vma=False)
```

```python
import functools
import math

import jax
import jax.numpy as jnp
import ml_dtypes
import numpy as np
from jax import lax
from jax.experimental import pallas as pl
from jax.experimental.pallas import tpu as pltpu
from jax.sharding import PartitionSpec as P

SWEEPS = 6
RADIUS = 7
KINETIC = -0.5 / 2.25
TILE = 256
BIG = 512
GROUP = 8
PITCH_PAD = 16
VMEM = 60 * 1024 * 1024


def tap_values():
    exact = [-math.pi * math.pi / 3.0]
    exact += [2.0 * (1.0 if k % 2 else -1.0) / (k * k) for k in range(1, RADIUS + 1)]
    return [float(np.float32(v).astype(ml_dtypes.bfloat16)) for v in exact]


TAPS = tap_values()


def band_matrix(n):
    table = np.zeros((n, n), np.float32)
    for i in range(n):
        for j in range(n):
            if abs(i - j) <= RADIUS:
                table[i, j] = TAPS[abs(i - j)]
    return table.astype(ml_dtypes.bfloat16)


def inverse_root(intersection):
    high = lax.Precision.HIGHEST
    norm_scale = jnp.sqrt(jnp.sum(intersection * intersection) + 1e-06)
    identity = jnp.eye(intersection.shape[0], dtype=jnp.float32)
    upper = intersection / norm_scale
    lower = identity
    for sweep_id in range(SWEEPS):
        middle = 0.5 * (3.0 * identity - jnp.dot(lower, upper, precision=high))
        upper = jnp.dot(upper, middle, precision=high)
        lower = jnp.dot(middle, lower, precision=high)
    return lower / jnp.sqrt(norm_scale)


def swapped(value, axis, distance):
    size = lax.axis_size(axis)
    return lax.ppermute(value, axis, [(i, i ^ distance) for i in range(size)])


def bits(axis):
    size = lax.axis_size(axis)
    return [1 << b for b in range(size.bit_length() - 1)]


def total(value):
    for axis in ("seg", "orb"):
        for distance in bits(axis):
            value = value + swapped(value, axis, distance)
    return value


def call(kernel, name, cost, **kwargs):
    flops, megabytes = cost
    return pl.pallas_call(
        kernel,
        name=name,
        compiler_params=pltpu.CompilerParams(vmem_limit_bytes=VMEM),
        cost_estimate=pl.CostEstimate(
            flops=flops, bytes_accessed=megabytes << 20, transcendentals=0
        ),
        **kwargs,
    )


def smem():
    return pl.BlockSpec(memory_space=pltpu.SMEM)


def untouched():
    return pl.BlockSpec(memory_space=pl.ANY)


def whole_vmem(pieces=1):
    return pl.BlockSpec(memory_space=pltpu.VMEM)


def pack_kernel(first_turned, count_ref, coeffs_ref, rows_ref, turned_ref):
    step = pl.program_id(0)
    tile_rows = rows_ref.shape[0]
    live = count_ref[0] - step * tile_rows
    tile = jnp.swapaxes(coeffs_ref[...].astype(jnp.float32), 0, 1)
    row = lax.broadcasted_iota(jnp.int32, tile.shape, 0)
    rows_ref[...] = jnp.where(row < live, tile, 0.0).astype(jnp.bfloat16)

    @pl.when(step >= first_turned)
    def _():
        for j in range(tile_rows):
            turned_ref[tile_rows - 1 - j] = rows_ref[j]


def pack(coeffs, seg_count):
    orbs, slot_count, depth = coeffs.shape
    steps = slot_count // BIG
    half = steps // 2
    return call(
        functools.partial(pack_kernel, half),
        "pack_slots",
        (0, 10),
        grid=(steps,),
        in_specs=[smem(), pl.BlockSpec((orbs, BIG, depth), lambda i: (0, i, 0))],
        out_specs=[
            pl.BlockSpec((BIG, orbs, depth), lambda i: (i, 0, 0)),
            pl.BlockSpec(
                (BIG, orbs, depth), lambda i: (jnp.minimum(steps - 1 - i, half - 1), 0, 0)
            ),
        ],
        out_shape=[
            jax.ShapeDtypeStruct((slot_count, orbs, depth), jnp.bfloat16),
            jax.ShapeDtypeStruct((slot_count // 2, orbs, depth), jnp.bfloat16),
        ],
    )(seg_count, coeffs)


def merge(rows, received, seg_count, used, order=None):
    slot_count, orbs, depth = rows.shape
    if used == slot_count:
        return rows
    moved = received.shape[0]
    tile_rows = math.gcd(used - moved, moved)
    free = (used - moved) // tile_rows

    def kernel(count_ref, own_ref, other_ref, order_ref, out_ref):
        live = count_ref[0] - (pl.program_id(0) + free) * tile_rows
        row = lax.broadcasted_iota(jnp.int32, out_ref.shape, 0)
        own, other = own_ref[...].astype(jnp.float32), other_ref[...].astype(jnp.float32)
        out_ref[...] = jnp.where(row < live, own, other).astype(jnp.bfloat16)

    kept = rows[:used]
    return call(
        kernel,
        "merge_rows",
        (0, 4),
        grid=(moved // tile_rows,),
        in_specs=[
            smem(),
            pl.BlockSpec((tile_rows, orbs, depth), lambda i: (i + free, 0, 0)),
            pl.BlockSpec((tile_rows, orbs, depth), lambda i: (i, 0, 0)),
            untouched(),
        ],
        out_specs=pl.BlockSpec((tile_rows, orbs, depth), lambda i: (i + free, 0, 0)),
        out_shape=jax.ShapeDtypeStruct((used, orbs, depth), jnp.bfloat16),
        input_output_aliases={1: 0},
    )(seg_count, kept, received, received if order is None else order)


def edge_kernel(count_ref, place_ref, rows_ref, order_ref, edge_ref):
    count = count_ref[0]

    @pl.loop(0, edge_ref.shape[0] // 8)
    def _(block):
        edge_ref[pl.ds(block * 8, 8)] = jnp.zeros((8,) + edge_ref.shape[1:], edge_ref.dtype)

    @pl.loop(0, lax.div(count + GROUP - 1, GROUP))
    def _(group):
        for u in range(GROUP):
            j = group * GROUP + u
            edge_ref[place_ref[j]] = rows_ref[j]


def edges_of(rows, seg_count, places, order, edge_lines):
    _, orbs, depth = rows.shape
    return call(
        edge_kernel,
        "edge_planes",
        (0, 8),
        in_specs=[smem(), smem(), whole_vmem(), untouched()],
        out_specs=whole_vmem(),
        out_shape=jax.ShapeDtypeStruct((2 * edge_lines + 8, orbs, depth), jnp.bfloat16),
    )(seg_count, places, rows, order)


def apply_kernel(
    cells_x,
    cells_y,
    count_ref,
    lines_ref,
    place_ref,
    rows_ref,
    low_ref,
    high_ref,
    potential_ref,
    band_ref,
    applied_ref,
    turned_ref,
    grid_ref,
    zsum_ref,
):
    step = pl.program_id(0)
    pitch = cells_y + PITCH_PAD
    count = count_ref[0]
    base = step * TILE
    live = jnp.minimum(count - base, TILE)
    reach = RADIUS * pitch

    @pl.when(step == 0)
    def _():
        @pl.loop(0, grid_ref.shape[0] // 16)
        def _(block):
            grid_ref[pl.ds(block * 16, 16)] = jnp.zeros((16,) + grid_ref.shape[1:], jnp.float32)

        for plane in range(RADIUS):
            for source, at in ((low_ref, plane), (high_ref, plane + RADIUS + cells_x)):

                @pl.loop(0, cells_y // 16)
                def _(block, source=source, at=at, plane=plane):
                    grid_ref[pl.ds(at * pitch + RADIUS + block * 16, 16)] = source[
                        pl.ds(plane * cells_y + block * 16, 16)
                    ].astype(jnp.float32)

        @pl.loop(0, lax.div(count + GROUP - 1, GROUP))
        def _(group):
            for u in range(GROUP):
                j = group * GROUP + u
                grid_ref[place_ref[j] + reach] = rows_ref[j].astype(jnp.float32)

    applied_ref[...] = jnp.zeros_like(applied_ref)

    @pl.when(live > 0)
    def _():
        tile = rows_ref[pl.ds(base, TILE)].astype(jnp.float32)
        flat = tile.reshape(TILE * tile.shape[1], tile.shape[2]).astype(jnp.bfloat16)
        zsum = jnp.dot(flat, band_ref[...], preferred_element_type=jnp.float32)
        zsum_ref[...] = (KINETIC * zsum).reshape(zsum_ref.shape)

        @pl.loop(0, lax.div(live + GROUP - 1, GROUP))
        def _(group):
            for u in range(GROUP):
                j = group * GROUP + u
                line = lines_ref[base + j]
                near = grid_ref.at[pl.ds(place_ref[base + j], 2 * reach + 1)]
                value = zsum_ref[j] + near[reach] * (
                    potential_ref[pl.ds(line, 1), :] + (2.0 * KINETIC * TAPS[0])
                )
                for k in range(1, RADIUS + 1):
                    pair = near[reach - k] + near[reach + k]
                    pair = pair + (near[reach - k * pitch] + near[reach + k * pitch])
                    value = value + (KINETIC * TAPS[k]) * pair
                applied_ref[j] = jnp.where(j < live, value, 0.0).astype(jnp.bfloat16)

    @pl.when(step >= pl.num_programs(0) // 2)
    def _():
        for j in range(TILE):
            turned_ref[TILE - 1 - j] = applied_ref[j]


def apply_rows(rows, seg_count, lines, places, low, high, potential):
    slot_count, orbs, depth = rows.shape
    cells_x, cells_y, _ = potential.shape
    edge_lines = RADIUS * cells_y
    grid_rows = (cells_x + 2 * RADIUS) * (cells_y + PITCH_PAD)
    once = pl.Buffered(1)
    whole = lambda i: (0, 0, 0)
    steps = slot_count // TILE
    half = steps // 2
    return call(
        functools.partial(apply_kernel, cells_x, cells_y),
        "apply_rows",
        (2 << 30, 80),
        grid=(steps,),
        in_specs=[
            smem(),
            smem(),
            smem(),
            pl.BlockSpec((slot_count, orbs, depth), whole, pipeline_mode=once),
            pl.BlockSpec((edge_lines, orbs, depth), whole, pipeline_mode=once),
            pl.BlockSpec((edge_lines, orbs, depth), whole, pipeline_mode=once),
            pl.BlockSpec((cells_x * cells_y, depth), lambda i: (0, 0), pipeline_mode=once),
            pl.BlockSpec((depth, depth), lambda i: (0, 0), pipeline_mode=once),
        ],
        out_specs=[
            pl.BlockSpec((TILE, orbs, depth), lambda i: (i, 0, 0)),
            pl.BlockSpec(
                (TILE, orbs, depth), lambda i: (jnp.minimum(steps - 1 - i, half - 1), 0, 0)
            ),
        ],
        out_shape=[
            jax.ShapeDtypeStruct((slot_count, orbs, depth), jnp.bfloat16),
            jax.ShapeDtypeStruct((slot_count // 2, orbs, depth), jnp.bfloat16),
        ],
        scratch_shapes=[
            pltpu.VMEM((grid_rows, orbs, depth), jnp.float32),
            pltpu.VMEM((TILE, orbs, depth), jnp.float32),
        ],
    )(
        seg_count,
        lines,
        places,
        rows,
        low,
        high,
        potential.reshape(cells_x * cells_y, depth),
        jnp.asarray(band_matrix(depth)),
    )


def tail_rows(rows, moved, order):
    used, orbs, depth = rows.shape

    def kernel(rows_ref, order_ref, out_ref, tail_ref, sem):
        copy = pltpu.make_async_copy(rows_ref.at[pl.ds(used - moved, moved)], tail_ref, sem)
        copy.start()
        copy.wait()

        @pl.loop(0, moved // 16)
        def _(block):
            for u in range(16):
                out_ref[moved - 1 - (block * 16 + u)] = tail_ref[block * 16 + u]

    return call(
        kernel,
        "tail_rows",
        (0, 4),
        in_specs=[untouched(), untouched()],
        out_specs=whole_vmem(),
        out_shape=jax.ShapeDtypeStruct((moved, orbs, depth), jnp.bfloat16),
        scratch_shapes=[pltpu.VMEM((moved, orbs, depth), jnp.bfloat16), pltpu.SemaphoreType.DMA],
    )(rows, order)


def unpack(rows, returned, seg_count, slot_count):
    used, orbs, depth = rows.shape
    steps = slot_count // BIG
    pieces = BIG // TILE
    kept = used // TILE

    def kernel(count_ref, rows_ref, returned_ref, out_ref):
        step = pl.program_id(0)
        for piece in range(pieces):
            block = step * pieces + piece
            live = count_ref[0] - block * TILE

            def put(tile, live=live, piece=piece):
                row = lax.broadcasted_iota(jnp.int32, tile.shape, 0)
                tile = jnp.where(row < live, tile.astype(jnp.float32), 0.0)
                out_ref[:, pl.ds(piece * TILE, TILE), :] = jnp.swapaxes(tile, 0, 1).astype(
                    jnp.bfloat16
                )

            @pl.when(block < kept)
            def _():
                put(rows_ref[pl.ds(block * TILE, TILE)])

            if kept * TILE < slot_count:

                @pl.when(block >= kept)
                def _():
                    put(returned_ref[pl.ds((block - kept) * TILE, TILE)])

    return call(
        kernel,
        "unpack_slots",
        (0, 10),
        grid=(steps,),
        in_specs=[smem(), whole_vmem(), whole_vmem()],
        out_specs=pl.BlockSpec((orbs, BIG, depth), lambda i: (0, i, 0)),
        out_shape=jax.ShapeDtypeStruct((orbs, slot_count, depth), jnp.bfloat16),
    )(seg_count, rows, returned)


def body(coeffs, seg_count, seg_lines, potential):
    orbs, slot_count, depth = coeffs.shape
    cells_x, cells_y, _ = potential.shape
    n_orb, n_seg = lax.axis_size("orb"), lax.axis_size("seg")
    ends = n_seg - 1
    norb = n_orb * orbs
    lines = seg_lines[0]
    edge_lines = RADIUS * cells_y
    weight_sum = 2.0 / (n_seg * slot_count * depth)

    most = seg_count + swapped(seg_count, "seg", 1)
    for distance in bits("seg")[1:]:
        most = jnp.maximum(most, swapped(most, "seg", distance))
    rows, turned = pack(coeffs, seg_count)
    live = jnp.arange(slot_count) < seg_count[0]
    tail = lines - (cells_x * cells_y - 2 * edge_lines)
    on_edge = jnp.where(lines < edge_lines, lines, jnp.where(tail >= edge_lines, tail, 2 * edge_lines))
    on_edge = jnp.where(live, on_edge, 2 * edge_lines)
    dump = cells_y + 2 * RADIUS
    places = lines + (lines // cells_y) * PITCH_PAD + RADIUS
    places = jnp.where(live, places, dump)

    def rest(used, operands):
        rows, turned, on_edge, places = operands
        moved = slot_count - used

        def spread(value):
            value = lax.all_to_all(value, "orb", split_axis=0, concat_axis=0, tiled=True)
            return value.reshape(n_orb, used // n_orb, orbs, depth)

        def to_partner(value, turned, order=None):
            if not moved:
                return value
            received = swapped(turned[:moved], "seg", 1)
            return merge(value, received, seg_count, used, order)

        def collect(value, order):
            value = value.reshape(used, orbs, depth)
            value = lax.all_to_all(value, "orb", split_axis=0, concat_axis=0, tiled=True)
            returned = swapped(tail_rows(value, moved, order), "seg", 1) if moved else value
            return unpack(value, returned, seg_count, slot_count)

        def gram(left, right):
            product = jnp.einsum("asoz,bspz->aobp", left, right, preferred_element_type=jnp.float32)
            return product.reshape(norb, norb)

        merged = to_partner(rows, turned)
        slot_orbitals = spread(merged)

        edges = edges_of(rows, seg_count, on_edge, merged, edge_lines)
        low = lax.ppermute(
            edges[edge_lines : 2 * edge_lines], "seg", [(i, i + 1) for i in range(ends)]
        )
        high = lax.ppermute(edges[:edge_lines], "seg", [(i + 1, i) for i in range(ends)])
        applied, turned_applied = apply_rows(rows, seg_count, lines, places, low, high, potential)
        slot_applied = spread(to_partner(applied, turned_applied, slot_orbitals))

        intersection = total(gram(slot_orbitals, slot_orbitals)) * weight_sum
        rotation = inverse_root(intersection)
        half = rotation.astype(jnp.bfloat16).reshape(n_orb, orbs, n_orb, orbs)

        def turn(value):
            return jnp.einsum(
                "aobp,asoz->bspz", half, value, preferred_element_type=jnp.float32
            ).astype(jnp.bfloat16)

        rotated_orbitals = collect(turn(slot_orbitals), half)
        hamiltonian = total(gram(slot_orbitals, slot_applied)) * weight_sum
        precise = lax.Precision.HIGHEST
        rotated_hamiltonian = jnp.dot(
            jnp.dot(rotation.T, hamiltonian, precision=precise), rotation, precision=precise
        )
        slot_turned, rotated_hamiltonian = lax.optimization_barrier(
            (turn(slot_applied), rotated_hamiltonian)
        )
        rotated_applied = collect(slot_turned, rotated_orbitals)
        return rotated_orbitals, rotated_applied, rotated_hamiltonian

    first = slot_count // 2
    classes = [first + TILE * (i + 1) for i in range((slot_count - first) // TILE)]
    chosen = jnp.clip(((most[0] + 1) // 2 - first + TILE - 1) // TILE - 1, 0, len(classes) - 1)
    return lax.switch(chosen, [functools.partial(rest, used) for used in classes], (rows, turned, on_edge, places))


def solution(mesh):
    in_specs = (P("orb", "seg", None), P("seg"), P("seg", None), P("seg", None, None))
    out_specs = (P("orb", "seg", None), P("orb", "seg", None), P())
    return jax.shard_map(body, mesh=mesh, in_specs=in_specs, out_specs=out_specs, check_vma=False)
```

```python
import functools
import math

import jax
import jax.numpy as jnp
import ml_dtypes
import numpy as np
from jax import lax
from jax.experimental import pallas as pl
from jax.experimental.pallas import tpu as pltpu
from jax.sharding import PartitionSpec as P

SWEEPS = 6
RADIUS = 7
KINETIC = -0.5 / 2.25
TILE = 128
APPLY_TILE = 256
BIG = 512
GROUP = 8
PITCH_PAD = 16
VMEM = 60 * 1024 * 1024


def tap_values():
    exact = [-math.pi * math.pi / 3.0]
    exact += [2.0 * (1.0 if k % 2 else -1.0) / (k * k) for k in range(1, RADIUS + 1)]
    return [float(np.float32(v).astype(ml_dtypes.bfloat16)) for v in exact]


TAPS = tap_values()


def band_matrix(n):
    table = np.zeros((n, n), np.float32)
    for i in range(n):
        for j in range(n):
            if abs(i - j) <= RADIUS:
                table[i, j] = TAPS[abs(i - j)]
    return table.astype(ml_dtypes.bfloat16)


def inverse_root(intersection):
    high = lax.Precision.HIGHEST
    norm_scale = jnp.sqrt(jnp.sum(intersection * intersection) + 1e-06)
    identity = jnp.eye(intersection.shape[0], dtype=jnp.float32)
    upper = intersection / norm_scale
    lower = identity
    for sweep_id in range(SWEEPS):
        middle = 0.5 * (3.0 * identity - jnp.dot(lower, upper, precision=high))
        upper = jnp.dot(upper, middle, precision=high)
        lower = jnp.dot(middle, lower, precision=high)
    return lower / jnp.sqrt(norm_scale)


def swapped(value, axis, distance):
    size = lax.axis_size(axis)
    return lax.ppermute(value, axis, [(i, i ^ distance) for i in range(size)])


def bits(axis):
    size = lax.axis_size(axis)
    return [1 << b for b in range(size.bit_length() - 1)]


def total(value):
    for axis in ("seg", "orb"):
        left = bits(axis)
        while left:
            if len(left) > 1:
                one, two = left.pop(), left.pop()
                near = swapped(value, axis, one)
                far, both = swapped(value, axis, two), swapped(value, axis, one | two)
                value = (value + near) + (far + both)
            else:
                value = value + swapped(value, axis, left.pop())
    return value


def call(kernel, name, cost, **kwargs):
    flops, megabytes = cost
    return pl.pallas_call(
        kernel,
        name=name,
        compiler_params=pltpu.CompilerParams(vmem_limit_bytes=VMEM),
        cost_estimate=pl.CostEstimate(
            flops=flops, bytes_accessed=megabytes << 20, transcendentals=0
        ),
        **kwargs,
    )


def smem():
    return pl.BlockSpec(memory_space=pltpu.SMEM)


def untouched():
    return pl.BlockSpec(memory_space=pl.ANY)


def whole_vmem(pieces=1):
    return pl.BlockSpec(memory_space=pltpu.VMEM)


def pack_kernel(first_turned, count_ref, coeffs_ref, rows_ref, turned_ref):
    step = pl.program_id(0)
    tile_rows = rows_ref.shape[0]
    live = count_ref[0] - step * tile_rows
    tile = jnp.swapaxes(coeffs_ref[...].astype(jnp.float32), 0, 1)
    row = lax.broadcasted_iota(jnp.int32, tile.shape, 0)
    rows_ref[...] = jnp.where(row < live, tile, 0.0).astype(jnp.bfloat16)

    @pl.when(step >= first_turned)
    def _():
        for j in range(tile_rows):
            turned_ref[tile_rows - 1 - j] = rows_ref[j]


def pack(coeffs, seg_count):
    orbs, slot_count, depth = coeffs.shape
    steps = slot_count // BIG
    half = steps // 2
    return call(
        functools.partial(pack_kernel, half),
        "pack_slots",
        (0, 10),
        grid=(steps,),
        in_specs=[smem(), pl.BlockSpec((orbs, BIG, depth), lambda i: (0, i, 0))],
        out_specs=[
            pl.BlockSpec((BIG, orbs, depth), lambda i: (i, 0, 0)),
            pl.BlockSpec(
                (BIG, orbs, depth), lambda i: (jnp.minimum(steps - 1 - i, half - 1), 0, 0)
            ),
        ],
        out_shape=[
            jax.ShapeDtypeStruct((slot_count, orbs, depth), jnp.bfloat16),
            jax.ShapeDtypeStruct((slot_count // 2, orbs, depth), jnp.bfloat16),
        ],
    )(seg_count, coeffs)


def merge(rows, received, seg_count, used, order=None):
    slot_count, orbs, depth = rows.shape
    if used == slot_count:
        return rows
    moved = received.shape[0]
    first = used - moved

    def kernel(count_ref, own_ref, other_ref, order_ref, out_ref, tail_ref, sem_in, sem_out):
        load = pltpu.make_async_copy(own_ref.at[pl.ds(first, moved)], tail_ref, sem_in)
        load.start()
        load.wait()

        @pl.loop(0, moved // TILE)
        def _(block):
            at = pl.ds(block * TILE, TILE)
            live = count_ref[0] - (first + block * TILE)
            row = lax.broadcasted_iota(jnp.int32, (TILE, orbs, depth), 0)
            own, other = tail_ref[at].astype(jnp.float32), other_ref[at].astype(jnp.float32)
            tail_ref[at] = jnp.where(row < live, own, other).astype(jnp.bfloat16)

        store = pltpu.make_async_copy(tail_ref, out_ref.at[pl.ds(first, moved)], sem_out)
        store.start()
        store.wait()

    return call(
        kernel,
        "merge_rows",
        (0, 4),
        in_specs=[smem(), untouched(), whole_vmem(), untouched()],
        out_specs=untouched(),
        out_shape=jax.ShapeDtypeStruct((used, orbs, depth), jnp.bfloat16),
        scratch_shapes=[
            pltpu.VMEM((moved, orbs, depth), jnp.bfloat16),
            pltpu.SemaphoreType.DMA,
            pltpu.SemaphoreType.DMA,
        ],
        input_output_aliases={1: 0},
    )(seg_count, rows[:used], received, received if order is None else order)


def edge_kernel(count_ref, place_ref, rows_ref, order_ref, edge_ref):
    count = count_ref[0]

    @pl.loop(0, edge_ref.shape[0] // 8)
    def _(block):
        edge_ref[pl.ds(block * 8, 8)] = jnp.zeros((8,) + edge_ref.shape[1:], edge_ref.dtype)

    @pl.loop(0, lax.div(count + GROUP - 1, GROUP))
    def _(group):
        for u in range(GROUP):
            j = group * GROUP + u
            edge_ref[place_ref[j]] = rows_ref[j]


def edges_of(rows, seg_count, places, order, edge_lines):
    _, orbs, depth = rows.shape
    return call(
        edge_kernel,
        "edge_planes",
        (0, 8),
        in_specs=[smem(), smem(), whole_vmem(), untouched()],
        out_specs=whole_vmem(),
        out_shape=jax.ShapeDtypeStruct((2 * edge_lines + 8, orbs, depth), jnp.bfloat16),
    )(seg_count, places, rows, order)


def apply_kernel(
    cells_x,
    cells_y,
    count_ref,
    lines_ref,
    place_ref,
    rows_ref,
    low_ref,
    high_ref,
    potential_ref,
    band_ref,
    applied_ref,
    turned_ref,
    grid_ref,
    zsum_ref,
):
    step = pl.program_id(0)
    pitch = cells_y + PITCH_PAD
    count = count_ref[0]
    base = step * APPLY_TILE
    live = jnp.minimum(count - base, APPLY_TILE)
    reach = RADIUS * pitch

    @pl.when(step == 0)
    def _():
        @pl.loop(0, grid_ref.shape[0] // 16)
        def _(block):
            grid_ref[pl.ds(block * 16, 16)] = jnp.zeros((16,) + grid_ref.shape[1:], jnp.float32)

        for plane in range(RADIUS):
            for source, at in ((low_ref, plane), (high_ref, plane + RADIUS + cells_x)):

                @pl.loop(0, cells_y // 16)
                def _(block, source=source, at=at, plane=plane):
                    grid_ref[pl.ds(at * pitch + RADIUS + block * 16, 16)] = source[
                        pl.ds(plane * cells_y + block * 16, 16)
                    ].astype(jnp.float32)

        @pl.loop(0, lax.div(count + GROUP - 1, GROUP))
        def _(group):
            first = group * GROUP
            tiles = [(place_ref[first + u], rows_ref[first + u]) for u in range(GROUP)]
            for place, tile in tiles:
                grid_ref[place + reach] = tile.astype(jnp.float32)

    applied_ref[...] = jnp.zeros_like(applied_ref)

    @pl.when(live > 0)
    def _():
        tile = rows_ref[pl.ds(base, APPLY_TILE)].astype(jnp.float32)
        flat = tile.reshape(APPLY_TILE * tile.shape[1], tile.shape[2]).astype(jnp.bfloat16)
        zsum = jnp.dot(flat, band_ref[...], preferred_element_type=jnp.float32)
        zsum_ref[...] = (KINETIC * zsum).reshape(zsum_ref.shape)

        @pl.loop(0, lax.div(live + GROUP - 1, GROUP))
        def _(group):
            values = []
            for u in range(GROUP):
                j = group * GROUP + u
                line = lines_ref[base + j]
                near = grid_ref.at[pl.ds(place_ref[base + j], 2 * reach + 1)]
                terms = [
                    near[reach] * (potential_ref[pl.ds(line, 1), :] + (2.0 * KINETIC * TAPS[0]))
                ]
                for k in range(1, RADIUS + 1):
                    pair = near[reach - k] + near[reach + k]
                    pair = pair + (near[reach - k * pitch] + near[reach + k * pitch])
                    terms.append((KINETIC * TAPS[k]) * pair)
                while len(terms) > 1:
                    terms = [p + q for p, q in zip(terms[::2], terms[1::2])]
                value = terms[0] + zsum_ref[j]
                values.append(jnp.where(j < live, value, 0.0).astype(jnp.bfloat16))
            for u in range(GROUP):
                applied_ref[group * GROUP + u] = values[u]

    @pl.when(step >= pl.num_programs(0) // 2)
    def _():
        for j in range(APPLY_TILE):
            turned_ref[APPLY_TILE - 1 - j] = applied_ref[j]


def apply_rows(rows, seg_count, lines, places, low, high, potential):
    slot_count, orbs, depth = rows.shape
    cells_x, cells_y, _ = potential.shape
    edge_lines = RADIUS * cells_y
    grid_rows = (cells_x + 2 * RADIUS) * (cells_y + PITCH_PAD)
    once = pl.Buffered(1)
    whole = lambda i: (0, 0, 0)
    steps = slot_count // APPLY_TILE
    half = steps // 2
    return call(
        functools.partial(apply_kernel, cells_x, cells_y),
        "apply_rows",
        (2 << 30, 80),
        grid=(steps,),
        in_specs=[
            smem(),
            smem(),
            smem(),
            pl.BlockSpec((slot_count, orbs, depth), whole, pipeline_mode=once),
            pl.BlockSpec((edge_lines, orbs, depth), whole, pipeline_mode=once),
            pl.BlockSpec((edge_lines, orbs, depth), whole, pipeline_mode=once),
            pl.BlockSpec((cells_x * cells_y, depth), lambda i: (0, 0), pipeline_mode=once),
            pl.BlockSpec((depth, depth), lambda i: (0, 0), pipeline_mode=once),
        ],
        out_specs=[
            pl.BlockSpec((APPLY_TILE, orbs, depth), lambda i: (i, 0, 0)),
            pl.BlockSpec(
                (APPLY_TILE, orbs, depth), lambda i: (jnp.minimum(steps - 1 - i, half - 1), 0, 0)
            ),
        ],
        out_shape=[
            jax.ShapeDtypeStruct((slot_count, orbs, depth), jnp.bfloat16),
            jax.ShapeDtypeStruct((slot_count // 2, orbs, depth), jnp.bfloat16),
        ],
        scratch_shapes=[
            pltpu.VMEM((grid_rows, orbs, depth), jnp.float32),
            pltpu.VMEM((APPLY_TILE, orbs, depth), jnp.float32),
        ],
    )(
        seg_count,
        lines,
        places,
        rows,
        low,
        high,
        potential.reshape(cells_x * cells_y, depth),
        jnp.asarray(band_matrix(depth)),
    )


def tail_rows(rows, moved, order):
    used, orbs, depth = rows.shape

    def kernel(rows_ref, *refs):
        out_ref, tail_ref, sem = refs[-3:]
        copy = pltpu.make_async_copy(rows_ref.at[pl.ds(used - moved, moved)], tail_ref, sem)
        copy.start()
        copy.wait()

        @pl.loop(0, moved // 16)
        def _(block):
            for u in range(16):
                out_ref[moved - 1 - (block * 16 + u)] = tail_ref[block * 16 + u]

    return call(
        kernel,
        "tail_rows",
        (0, 4),
        in_specs=[untouched()] * (1 + len(order)),
        out_specs=whole_vmem(),
        out_shape=jax.ShapeDtypeStruct((moved, orbs, depth), jnp.bfloat16),
        scratch_shapes=[pltpu.VMEM((moved, orbs, depth), jnp.bfloat16), pltpu.SemaphoreType.DMA],
    )(rows, *order)


def unpack(rows, returned, seg_count, slot_count):
    used, orbs, depth = rows.shape
    steps = slot_count // BIG
    pieces = BIG // TILE
    kept = used // TILE

    def kernel(count_ref, rows_ref, returned_ref, out_ref):
        step = pl.program_id(0)
        for piece in range(pieces):
            block = step * pieces + piece
            live = count_ref[0] - block * TILE

            def put(tile, live=live, piece=piece):
                row = lax.broadcasted_iota(jnp.int32, tile.shape, 0)
                tile = jnp.where(row < live, tile.astype(jnp.float32), 0.0)
                out_ref[:, pl.ds(piece * TILE, TILE), :] = jnp.swapaxes(tile, 0, 1).astype(
                    jnp.bfloat16
                )

            @pl.when(block < kept)
            def _():
                put(rows_ref[pl.ds(block * TILE, TILE)])

            if kept * TILE < slot_count:

                @pl.when(block >= kept)
                def _():
                    put(returned_ref[pl.ds((block - kept) * TILE, TILE)])

    return call(
        kernel,
        "unpack_slots",
        (0, 10),
        grid=(steps,),
        in_specs=[smem(), whole_vmem(), whole_vmem()],
        out_specs=pl.BlockSpec((orbs, BIG, depth), lambda i: (0, i, 0)),
        out_shape=jax.ShapeDtypeStruct((orbs, slot_count, depth), jnp.bfloat16),
    )(seg_count, rows, returned)


def stacked(ref, start, depth):
    value = ref[:, pl.ds(start, GROUP)].astype(jnp.float32)
    norb = value.shape[0] * value.shape[2]
    tiles = [value[:, u].reshape(norb, depth) for u in range(GROUP)]
    return jnp.concatenate(tiles, axis=1).astype(jnp.bfloat16)


def gram(left, right):
    parts, slots, orbs, depth = left.shape
    norb = parts * orbs
    if orbs % 8 or slots % GROUP:
        product = jnp.einsum("asoz,bspz->aobp", left, right, preferred_element_type=jnp.float32)
        return product.reshape(norb, norb)
    same = left is right

    def kernel(*refs):
        out_ref = refs[-1]
        out_ref[...] = jnp.zeros_like(out_ref)

        @pl.loop(0, slots // GROUP)
        def _(block):
            one = stacked(refs[0], block * GROUP, depth)
            two = one if same else stacked(refs[1], block * GROUP, depth)
            out_ref[...] += lax.dot_general(
                one, two, (((1,), (1,)), ((), ())), preferred_element_type=jnp.float32
            )

    given = (left,) if same else (left, right)
    return call(
        kernel,
        "gram",
        (1 << 28, 4 * len(given)),
        in_specs=[whole_vmem()] * len(given),
        out_specs=whole_vmem(),
        out_shape=jax.ShapeDtypeStruct((norb, norb), jnp.float32),
    )(*given)


def turn(half, value):
    parts, slots, orbs, depth = value.shape
    norb = parts * orbs
    if orbs % 8 or slots % GROUP:
        blocks = half.reshape(parts, orbs, parts, orbs)
        turned = jnp.einsum("aobp,asoz->bspz", blocks, value, preferred_element_type=jnp.float32)
        return turned.astype(jnp.bfloat16)

    def kernel(half_ref, value_ref, out_ref):
        @pl.loop(0, slots // GROUP)
        def _(block):
            rows = stacked(value_ref, block * GROUP, depth)
            product = jnp.dot(half_ref[...], rows, preferred_element_type=jnp.float32)
            for u in range(GROUP):
                tile = product[:, u * depth : (u + 1) * depth].reshape(parts, orbs, depth)
                out_ref[:, block * GROUP + u] = tile.astype(jnp.bfloat16)

    return call(
        kernel,
        "turn_rows",
        (1 << 28, 8),
        in_specs=[whole_vmem(), whole_vmem()],
        out_specs=whole_vmem(),
        out_shape=jax.ShapeDtypeStruct(value.shape, jnp.bfloat16),
    )(half.T, value)


def body(coeffs, seg_count, seg_lines, potential):
    orbs, slot_count, depth = coeffs.shape
    cells_x, cells_y, _ = potential.shape
    n_orb, n_seg = lax.axis_size("orb"), lax.axis_size("seg")
    ends = n_seg - 1
    norb = n_orb * orbs
    lines = seg_lines[0]
    edge_lines = RADIUS * cells_y
    weight_sum = 2.0 / (n_seg * slot_count * depth)

    most = seg_count + swapped(seg_count, "seg", 1)
    for distance in bits("seg")[1:]:
        most = jnp.maximum(most, swapped(most, "seg", distance))
    rows, turned = pack(coeffs, seg_count)
    live = jnp.arange(slot_count) < seg_count[0]
    tail = lines - (cells_x * cells_y - 2 * edge_lines)
    on_edge = jnp.where(lines < edge_lines, lines, jnp.where(tail >= edge_lines, tail, 2 * edge_lines))
    on_edge = jnp.where(live, on_edge, 2 * edge_lines)
    dump = cells_y + 2 * RADIUS
    places = lines + (lines // cells_y) * PITCH_PAD + RADIUS
    places = jnp.where(live, places, dump)

    def rest(used, operands):
        rows, turned, on_edge, places = operands
        moved = slot_count - used

        def spread(value):
            value = lax.all_to_all(value, "orb", split_axis=0, concat_axis=0, tiled=True)
            return value.reshape(n_orb, used // n_orb, orbs, depth)

        def to_partner(value, turned, order=None):
            if not moved:
                return value
            received = swapped(turned[:moved], "seg", 1)
            return merge(value, received, seg_count, used, order)

        def collect(value, order):
            value = value.reshape(used, orbs, depth)
            value = lax.all_to_all(value, "orb", split_axis=0, concat_axis=0, tiled=True)
            returned = swapped(tail_rows(value, moved, order), "seg", 1) if moved else value
            return unpack(value, returned, seg_count, slot_count)

        merged = to_partner(rows, turned)
        slot_orbitals = spread(merged)

        edges = edges_of(rows, seg_count, on_edge, merged, edge_lines)
        low = lax.ppermute(
            edges[edge_lines : 2 * edge_lines], "seg", [(i, i + 1) for i in range(ends)]
        )
        high = lax.ppermute(edges[:edge_lines], "seg", [(i + 1, i) for i in range(ends)])
        applied, turned_applied = apply_rows(rows, seg_count, lines, places, low, high, potential)
        slot_applied = spread(to_partner(applied, turned_applied, slot_orbitals))

        intersection = total(gram(slot_orbitals, slot_orbitals)) * weight_sum
        rotation = inverse_root(intersection)
        half = rotation.astype(jnp.bfloat16)
        rotated_orbitals = collect(turn(half, slot_orbitals), (half,))
        hamiltonian = total(gram(slot_orbitals, slot_applied)) * weight_sum
        precise = lax.Precision.HIGHEST
        rotated_hamiltonian = jnp.dot(
            jnp.dot(rotation.T, hamiltonian, precision=precise), rotation, precision=precise
        )
        rotated_applied = collect(
            turn(half, slot_applied), (rotated_orbitals, rotated_hamiltonian)
        )
        return rotated_orbitals, rotated_applied, rotated_hamiltonian

    first = slot_count // 2
    classes = [first + TILE * (i + 1) for i in range((slot_count - first) // TILE)]
    chosen = jnp.clip(((most[0] + 1) // 2 - first + TILE - 1) // TILE - 1, 0, len(classes) - 1)
    return lax.switch(chosen, [functools.partial(rest, used) for used in classes], (rows, turned, on_edge, places))


def solution(mesh):
    in_specs = (P("orb", "seg", None), P("seg"), P("seg", None), P("seg", None, None))
    out_specs = (P("orb", "seg", None), P("orb", "seg", None), P())
    return jax.shard_map(body, mesh=mesh, in_specs=in_specs, out_specs=out_specs, check_vma=False)
```

```python
import functools
import math

import jax
import jax.numpy as jnp
import ml_dtypes
import numpy as np
from jax import lax
from jax.experimental import pallas as pl
from jax.experimental.pallas import tpu as pltpu
from jax.sharding import PartitionSpec as P

SWEEPS = 6
RADIUS = 7
KINETIC = -0.5 / 2.25
TILE = 128
APPLY_TILE = 256
BIG = 512
GROUP = 8
SLOTS = 16
PITCH_PAD = 16
VMEM = 60 * 1024 * 1024


def tap_values():
    exact = [-math.pi * math.pi / 3.0]
    exact += [2.0 * (1.0 if k % 2 else -1.0) / (k * k) for k in range(1, RADIUS + 1)]
    return [float(np.float32(v).astype(ml_dtypes.bfloat16)) for v in exact]


TAPS = tap_values()


def band_matrix(n):
    table = np.zeros((n, n), np.float32)
    for i in range(n):
        for j in range(n):
            if abs(i - j) <= RADIUS:
                table[i, j] = TAPS[abs(i - j)]
    return table.astype(ml_dtypes.bfloat16)


def inverse_root(intersection):
    high = lax.Precision.HIGHEST
    norm_scale = jnp.sqrt(jnp.sum(intersection * intersection) + 1e-06)
    identity = jnp.eye(intersection.shape[0], dtype=jnp.float32)
    upper = intersection / norm_scale
    lower = identity
    for sweep_id in range(SWEEPS):
        middle = 0.5 * (3.0 * identity - jnp.dot(lower, upper, precision=high))
        upper = jnp.dot(upper, middle, precision=high)
        lower = jnp.dot(middle, lower, precision=high)
    return lower / jnp.sqrt(norm_scale)


def swapped(value, axis, distance):
    size = lax.axis_size(axis)
    return lax.ppermute(value, axis, [(i, i ^ distance) for i in range(size)])


def bits(axis):
    size = lax.axis_size(axis)
    return [1 << b for b in range(size.bit_length() - 1)]


def total(value):
    for axis in ("seg", "orb"):
        left = bits(axis)
        while left:
            if len(left) > 1:
                one, two = left.pop(), left.pop()
                near = swapped(value, axis, one)
                far, both = swapped(value, axis, two), swapped(value, axis, one | two)
                value = (value + near) + (far + both)
            else:
                value = value + swapped(value, axis, left.pop())
    return value


def call(kernel, name, cost, **kwargs):
    flops, megabytes = cost
    return pl.pallas_call(
        kernel,
        name=name,
        compiler_params=pltpu.CompilerParams(vmem_limit_bytes=VMEM),
        cost_estimate=pl.CostEstimate(
            flops=flops, bytes_accessed=megabytes << 20, transcendentals=0
        ),
        **kwargs,
    )


def smem():
    return pl.BlockSpec(memory_space=pltpu.SMEM)


def untouched():
    return pl.BlockSpec(memory_space=pl.ANY)


def whole_vmem(pieces=1):
    return pl.BlockSpec(memory_space=pltpu.VMEM)


def pack_kernel(first_turned, count_ref, coeffs_ref, rows_ref, turned_ref):
    step = pl.program_id(0)
    tile_rows = rows_ref.shape[0]
    live = count_ref[0] - step * tile_rows
    tile = jnp.swapaxes(coeffs_ref[...].astype(jnp.float32), 0, 1)
    row = lax.broadcasted_iota(jnp.int32, tile.shape, 0)
    rows_ref[...] = jnp.where(row < live, tile, 0.0).astype(jnp.bfloat16)

    @pl.when(step >= first_turned)
    def _():
        for j in range(tile_rows):
            turned_ref[tile_rows - 1 - j] = rows_ref[j]


def pack(coeffs, seg_count):
    orbs, slot_count, depth = coeffs.shape
    steps = slot_count // BIG
    half = steps // 2
    return call(
        functools.partial(pack_kernel, half),
        "pack_slots",
        (0, 10),
        grid=(steps,),
        in_specs=[smem(), pl.BlockSpec((orbs, BIG, depth), lambda i: (0, i, 0))],
        out_specs=[
            pl.BlockSpec((BIG, orbs, depth), lambda i: (i, 0, 0)),
            pl.BlockSpec(
                (BIG, orbs, depth), lambda i: (jnp.minimum(steps - 1 - i, half - 1), 0, 0)
            ),
        ],
        out_shape=[
            jax.ShapeDtypeStruct((slot_count, orbs, depth), jnp.bfloat16),
            jax.ShapeDtypeStruct((slot_count // 2, orbs, depth), jnp.bfloat16),
        ],
    )(seg_count, coeffs)


def merge(rows, received, seg_count, used, order=None):
    slot_count, orbs, depth = rows.shape
    if used == slot_count:
        return rows
    moved = received.shape[0]
    first = used - moved

    def kernel(count_ref, own_ref, other_ref, order_ref, out_ref, tail_ref, sem_in, sem_out):
        load = pltpu.make_async_copy(own_ref.at[pl.ds(first, moved)], tail_ref, sem_in)
        load.start()
        load.wait()

        @pl.loop(0, moved // TILE)
        def _(block):
            at = pl.ds(block * TILE, TILE)
            live = count_ref[0] - (first + block * TILE)
            row = lax.broadcasted_iota(jnp.int32, (TILE, orbs, depth), 0)
            own, other = tail_ref[at].astype(jnp.float32), other_ref[at].astype(jnp.float32)
            tail_ref[at] = jnp.where(row < live, own, other).astype(jnp.bfloat16)

        store = pltpu.make_async_copy(tail_ref, out_ref.at[pl.ds(first, moved)], sem_out)
        store.start()
        store.wait()

    return call(
        kernel,
        "merge_rows",
        (0, 4),
        in_specs=[smem(), untouched(), whole_vmem(), untouched()],
        out_specs=untouched(),
        out_shape=jax.ShapeDtypeStruct((used, orbs, depth), jnp.bfloat16),
        scratch_shapes=[
            pltpu.VMEM((moved, orbs, depth), jnp.bfloat16),
            pltpu.SemaphoreType.DMA,
            pltpu.SemaphoreType.DMA,
        ],
        input_output_aliases={1: 0},
    )(seg_count, rows[:used], received, received if order is None else order)


def edge_kernel(count_ref, place_ref, rows_ref, order_ref, edge_ref):
    count = count_ref[0]

    @pl.loop(0, edge_ref.shape[0] // 8)
    def _(block):
        edge_ref[pl.ds(block * 8, 8)] = jnp.zeros((8,) + edge_ref.shape[1:], edge_ref.dtype)

    @pl.loop(0, lax.div(count + GROUP - 1, GROUP))
    def _(group):
        for u in range(GROUP):
            j = group * GROUP + u
            edge_ref[place_ref[j]] = rows_ref[j]


def edges_of(rows, seg_count, places, order, edge_lines):
    _, orbs, depth = rows.shape
    return call(
        edge_kernel,
        "edge_planes",
        (0, 8),
        in_specs=[smem(), smem(), whole_vmem(), untouched()],
        out_specs=whole_vmem(),
        out_shape=jax.ShapeDtypeStruct((2 * edge_lines + 8, orbs, depth), jnp.bfloat16),
    )(seg_count, places, rows, order)


def apply_kernel(
    cells_x,
    cells_y,
    count_ref,
    lines_ref,
    place_ref,
    rows_ref,
    low_ref,
    high_ref,
    potential_ref,
    band_ref,
    order_ref,
    applied_ref,
    turned_ref,
    grid_ref,
    zsum_ref,
):
    step = pl.program_id(0)
    pitch = cells_y + PITCH_PAD
    count = count_ref[0]
    base = step * APPLY_TILE
    live = jnp.minimum(count - base, APPLY_TILE)
    reach = RADIUS * pitch

    @pl.when(step == 0)
    def _():
        @pl.loop(0, grid_ref.shape[0] // 16)
        def _(block):
            grid_ref[pl.ds(block * 16, 16)] = jnp.zeros((16,) + grid_ref.shape[1:], jnp.float32)

        for plane in range(RADIUS):
            for source, at in ((low_ref, plane), (high_ref, plane + RADIUS + cells_x)):

                @pl.loop(0, cells_y // 16)
                def _(block, source=source, at=at, plane=plane):
                    grid_ref[pl.ds(at * pitch + RADIUS + block * 16, 16)] = source[
                        pl.ds(plane * cells_y + block * 16, 16)
                    ].astype(jnp.float32)

        @pl.loop(0, lax.div(count + GROUP - 1, GROUP))
        def _(group):
            first = group * GROUP
            tiles = [(place_ref[first + u], rows_ref[first + u]) for u in range(GROUP)]
            for place, tile in tiles:
                grid_ref[place + reach] = tile.astype(jnp.float32)

    applied_ref[...] = jnp.zeros_like(applied_ref)

    @pl.when(live > 0)
    def _():
        tile = rows_ref[pl.ds(base, APPLY_TILE)].astype(jnp.float32)
        flat = tile.reshape(APPLY_TILE * tile.shape[1], tile.shape[2]).astype(jnp.bfloat16)
        zsum = jnp.dot(flat, band_ref[...], preferred_element_type=jnp.float32)
        zsum_ref[...] = (KINETIC * zsum).reshape(zsum_ref.shape)

        @pl.loop(0, lax.div(live + GROUP - 1, GROUP))
        def _(group):
            values = []
            for u in range(GROUP):
                j = group * GROUP + u
                line = lines_ref[base + j]
                near = grid_ref.at[pl.ds(place_ref[base + j], 2 * reach + 1)]
                terms = [
                    near[reach] * (potential_ref[pl.ds(line, 1), :] + (2.0 * KINETIC * TAPS[0]))
                ]
                for k in range(1, RADIUS + 1):
                    pair = near[reach - k] + near[reach + k]
                    pair = pair + (near[reach - k * pitch] + near[reach + k * pitch])
                    terms.append((KINETIC * TAPS[k]) * pair)
                while len(terms) > 1:
                    terms = [p + q for p, q in zip(terms[::2], terms[1::2])]
                value = terms[0] + zsum_ref[j]
                values.append(jnp.where(j < live, value, 0.0).astype(jnp.bfloat16))
            for u in range(GROUP):
                applied_ref[group * GROUP + u] = values[u]

    @pl.when(step >= pl.num_programs(0) // 2)
    def _():
        for j in range(APPLY_TILE):
            turned_ref[APPLY_TILE - 1 - j] = applied_ref[j]


def apply_rows(rows, seg_count, lines, places, low, high, potential, order):
    slot_count, orbs, depth = rows.shape
    cells_x, cells_y, _ = potential.shape
    edge_lines = RADIUS * cells_y
    grid_rows = (cells_x + 2 * RADIUS) * (cells_y + PITCH_PAD)
    once = pl.Buffered(1)
    whole = lambda i: (0, 0, 0)
    steps = slot_count // APPLY_TILE
    half = steps // 2
    return call(
        functools.partial(apply_kernel, cells_x, cells_y),
        "apply_rows",
        (2 << 30, 80),
        grid=(steps,),
        in_specs=[
            smem(),
            smem(),
            smem(),
            pl.BlockSpec((slot_count, orbs, depth), whole, pipeline_mode=once),
            pl.BlockSpec((edge_lines, orbs, depth), whole, pipeline_mode=once),
            pl.BlockSpec((edge_lines, orbs, depth), whole, pipeline_mode=once),
            pl.BlockSpec((cells_x * cells_y, depth), lambda i: (0, 0), pipeline_mode=once),
            pl.BlockSpec((depth, depth), lambda i: (0, 0), pipeline_mode=once),
            untouched(),
        ],
        out_specs=[
            pl.BlockSpec((APPLY_TILE, orbs, depth), lambda i: (i, 0, 0)),
            pl.BlockSpec(
                (APPLY_TILE, orbs, depth), lambda i: (jnp.minimum(steps - 1 - i, half - 1), 0, 0)
            ),
        ],
        out_shape=[
            jax.ShapeDtypeStruct((slot_count, orbs, depth), jnp.bfloat16),
            jax.ShapeDtypeStruct((slot_count // 2, orbs, depth), jnp.bfloat16),
        ],
        scratch_shapes=[
            pltpu.VMEM((grid_rows, orbs, depth), jnp.float32),
            pltpu.VMEM((APPLY_TILE, orbs, depth), jnp.float32),
        ],
    )(
        seg_count,
        lines,
        places,
        rows,
        low,
        high,
        potential.reshape(cells_x * cells_y, depth),
        jnp.asarray(band_matrix(depth)),
        order,
    )


def tail_rows(rows, moved, order):
    used, orbs, depth = rows.shape

    def kernel(rows_ref, *refs):
        out_ref, tail_ref, sem = refs[-3:]
        copy = pltpu.make_async_copy(rows_ref.at[pl.ds(used - moved, moved)], tail_ref, sem)
        copy.start()
        copy.wait()

        @pl.loop(0, moved // 16)
        def _(block):
            for u in range(16):
                out_ref[moved - 1 - (block * 16 + u)] = tail_ref[block * 16 + u]

    return call(
        kernel,
        "tail_rows",
        (0, 4),
        in_specs=[untouched()] * (1 + len(order)),
        out_specs=whole_vmem(),
        out_shape=jax.ShapeDtypeStruct((moved, orbs, depth), jnp.bfloat16),
        scratch_shapes=[pltpu.VMEM((moved, orbs, depth), jnp.bfloat16), pltpu.SemaphoreType.DMA],
    )(rows, *order)


def unpack(rows, returned, seg_count, slot_count):
    used, orbs, depth = rows.shape
    steps = slot_count // BIG
    pieces = BIG // TILE
    kept = used // TILE

    def kernel(count_ref, rows_ref, returned_ref, out_ref):
        step = pl.program_id(0)
        for piece in range(pieces):
            block = step * pieces + piece
            live = count_ref[0] - block * TILE

            def put(tile, live=live, piece=piece):
                row = lax.broadcasted_iota(jnp.int32, tile.shape, 0)
                tile = jnp.where(row < live, tile.astype(jnp.float32), 0.0)
                out_ref[:, pl.ds(piece * TILE, TILE), :] = jnp.swapaxes(tile, 0, 1).astype(
                    jnp.bfloat16
                )

            @pl.when(block < kept)
            def _():
                put(rows_ref[pl.ds(block * TILE, TILE)])

            if kept * TILE < slot_count:

                @pl.when(block >= kept)
                def _():
                    put(returned_ref[pl.ds((block - kept) * TILE, TILE)])

    return call(
        kernel,
        "unpack_slots",
        (0, 10),
        grid=(steps,),
        in_specs=[smem(), whole_vmem(), whole_vmem()],
        out_specs=pl.BlockSpec((orbs, BIG, depth), lambda i: (0, i, 0)),
        out_shape=jax.ShapeDtypeStruct((orbs, slot_count, depth), jnp.bfloat16),
    )(seg_count, rows, returned)


def stacked(ref, start, depth):
    value = ref[:, pl.ds(start, SLOTS)].astype(jnp.float32)
    norb = value.shape[0] * value.shape[2]
    tiles = [value[:, u].reshape(norb, depth) for u in range(SLOTS)]
    return jnp.concatenate(tiles, axis=1).astype(jnp.bfloat16)


def gram(left, right, order):
    parts, slots, orbs, depth = left.shape
    norb = parts * orbs
    if orbs % 8 or slots % SLOTS:
        product = jnp.einsum("asoz,bspz->aobp", left, right, preferred_element_type=jnp.float32)
        return product.reshape(norb, norb)
    same = left is right

    def kernel(*refs):
        out_ref = refs[-1]
        out_ref[...] = jnp.zeros_like(out_ref)

        @pl.loop(0, slots // SLOTS)
        def _(block):
            one = stacked(refs[0], block * SLOTS, depth)
            two = one if same else stacked(refs[1], block * SLOTS, depth)
            out_ref[...] += lax.dot_general(
                one, two, (((1,), (1,)), ((), ())), preferred_element_type=jnp.float32
            )

    given = (left,) if same else (left, right)
    return call(
        kernel,
        "gram",
        (1 << 28, 4 * len(given)),
        in_specs=[whole_vmem()] * len(given) + [untouched()],
        out_specs=whole_vmem(),
        out_shape=jax.ShapeDtypeStruct((norb, norb), jnp.float32),
    )(*given, order)


def turn(half, value):
    parts, slots, orbs, depth = value.shape
    norb = parts * orbs
    if orbs % 8 or slots % SLOTS:
        blocks = half.reshape(parts, orbs, parts, orbs)
        turned = jnp.einsum("aobp,asoz->bspz", blocks, value, preferred_element_type=jnp.float32)
        return turned.astype(jnp.bfloat16)

    def kernel(half_ref, value_ref, out_ref):
        @pl.loop(0, slots // SLOTS)
        def _(block):
            rows = stacked(value_ref, block * SLOTS, depth)
            product = jnp.dot(half_ref[...], rows, preferred_element_type=jnp.float32)
            for u in range(SLOTS):
                tile = product[:, u * depth : (u + 1) * depth].reshape(parts, orbs, depth)
                out_ref[:, block * SLOTS + u] = tile.astype(jnp.bfloat16)

    return call(
        kernel,
        "turn_rows",
        (1 << 28, 8),
        in_specs=[whole_vmem(), whole_vmem()],
        out_specs=whole_vmem(),
        out_shape=jax.ShapeDtypeStruct(value.shape, jnp.bfloat16),
    )(half.T, value)


def body(coeffs, seg_count, seg_lines, potential):
    orbs, slot_count, depth = coeffs.shape
    cells_x, cells_y, _ = potential.shape
    n_orb, n_seg = lax.axis_size("orb"), lax.axis_size("seg")
    ends = n_seg - 1
    norb = n_orb * orbs
    lines = seg_lines[0]
    edge_lines = RADIUS * cells_y
    weight_sum = 2.0 / (n_seg * slot_count * depth)

    most = seg_count + swapped(seg_count, "seg", 1)
    for distance in bits("seg")[1:]:
        most = jnp.maximum(most, swapped(most, "seg", distance))
    rows, turned = pack(coeffs, seg_count)
    live = jnp.arange(slot_count) < seg_count[0]
    tail = lines - (cells_x * cells_y - 2 * edge_lines)
    on_edge = jnp.where(lines < edge_lines, lines, jnp.where(tail >= edge_lines, tail, 2 * edge_lines))
    on_edge = jnp.where(live, on_edge, 2 * edge_lines)
    dump = cells_y + 2 * RADIUS
    places = lines + (lines // cells_y) * PITCH_PAD + RADIUS
    places = jnp.where(live, places, dump)

    def rest(used, operands):
        rows, turned, on_edge, places = operands
        moved = slot_count - used

        def spread(value):
            value = lax.all_to_all(value, "orb", split_axis=0, concat_axis=0, tiled=True)
            return value.reshape(n_orb, used // n_orb, orbs, depth)

        def to_partner(value, turned, order=None):
            if not moved:
                return value
            received = swapped(turned[:moved], "seg", 1)
            return merge(value, received, seg_count, used, order)

        def collect(value, order):
            value = value.reshape(used, orbs, depth)
            value = lax.all_to_all(value, "orb", split_axis=0, concat_axis=0, tiled=True)
            returned = swapped(tail_rows(value, moved, order), "seg", 1) if moved else value
            return unpack(value, returned, seg_count, slot_count)

        merged = to_partner(rows, turned)
        slot_orbitals = spread(merged)

        edges = edges_of(rows, seg_count, on_edge, merged, edge_lines)
        low = lax.ppermute(
            edges[edge_lines : 2 * edge_lines], "seg", [(i, i + 1) for i in range(ends)]
        )
        high = lax.ppermute(edges[:edge_lines], "seg", [(i + 1, i) for i in range(ends)])
        intersection = total(gram(slot_orbitals, slot_orbitals, edges)) * weight_sum
        rotation = inverse_root(intersection)
        half = rotation.astype(jnp.bfloat16)
        turned_orbitals = turn(half, slot_orbitals)

        applied, reversed_applied = apply_rows(
            rows, seg_count, lines, places, low, high, potential, turned_orbitals
        )
        rotated_orbitals = collect(turned_orbitals, (half,))
        slot_applied = spread(to_partner(applied, reversed_applied))

        turned_applied = turn(half, slot_applied)
        hamiltonian = total(gram(slot_orbitals, slot_applied, turned_applied)) * weight_sum
        precise = lax.Precision.HIGHEST
        rotated_hamiltonian = jnp.dot(
            jnp.dot(rotation.T, hamiltonian, precision=precise), rotation, precision=precise
        )
        rotated_applied = collect(turned_applied, (rotated_orbitals, rotated_hamiltonian))
        return rotated_orbitals, rotated_applied, rotated_hamiltonian

    first = slot_count // 2
    classes = [first + TILE * (i + 1) for i in range((slot_count - first) // TILE)]
    chosen = jnp.clip(((most[0] + 1) // 2 - first + TILE - 1) // TILE - 1, 0, len(classes) - 1)
    return lax.switch(chosen, [functools.partial(rest, used) for used in classes], (rows, turned, on_edge, places))


def solution(mesh):
    in_specs = (P("orb", "seg", None), P("seg"), P("seg", None), P("seg", None, None))
    out_specs = (P("orb", "seg", None), P("orb", "seg", None), P())
    return jax.shard_map(body, mesh=mesh, in_specs=in_specs, out_specs=out_specs, check_vma=False)
```

```python
import functools
import math

import jax
import jax.numpy as jnp
import ml_dtypes
import numpy as np
from jax import lax
from jax.experimental import pallas as pl
from jax.experimental.pallas import tpu as pltpu
from jax.sharding import PartitionSpec as P

SWEEPS = 6
RADIUS = 7
KINETIC = -0.5 / 2.25
TILE = 128
APPLY_TILE = 256
BIG = 512
GROUP = 8
SLOTS = 16
PITCH_PAD = 16
VMEM = 60 * 1024 * 1024


def tap_values():
    exact = [-math.pi * math.pi / 3.0]
    exact += [2.0 * (1.0 if k % 2 else -1.0) / (k * k) for k in range(1, RADIUS + 1)]
    return [float(np.float32(v).astype(ml_dtypes.bfloat16)) for v in exact]


TAPS = tap_values()


def band_matrix(n):
    table = np.zeros((n, n), np.float32)
    for i in range(n):
        for j in range(n):
            if abs(i - j) <= RADIUS:
                table[i, j] = TAPS[abs(i - j)]
    return table.astype(ml_dtypes.bfloat16)


def inverse_root(intersection):
    high = lax.Precision.HIGHEST
    norm_scale = jnp.sqrt(jnp.sum(intersection * intersection) + 1e-06)
    identity = jnp.eye(intersection.shape[0], dtype=jnp.float32)
    upper = intersection / norm_scale
    lower = identity
    for sweep_id in range(SWEEPS):
        middle = 0.5 * (3.0 * identity - jnp.dot(lower, upper, precision=high))
        upper = jnp.dot(upper, middle, precision=high)
        lower = jnp.dot(middle, lower, precision=high)
    return lower / jnp.sqrt(norm_scale)


def swapped(value, axis, distance):
    size = lax.axis_size(axis)
    return lax.ppermute(value, axis, [(i, i ^ distance) for i in range(size)])


def bits(axis):
    size = lax.axis_size(axis)
    return [1 << b for b in range(size.bit_length() - 1)]


def total(value, at_once):
    for axis in ("seg", "orb"):
        left = bits(axis)
        while left:
            now, left = left[-at_once:], left[:-at_once]
            masks = [0]
            for bit in now:
                masks += [mask | bit for mask in masks]
            terms = [swapped(value, axis, mask) if mask else value for mask in masks]
            while len(terms) > 1:
                terms = [p + q for p, q in zip(terms[::2], terms[1::2])]
            value = terms[0]
    return value


def call(kernel, name, cost, **kwargs):
    flops, megabytes = cost
    return pl.pallas_call(
        kernel,
        name=name,
        compiler_params=pltpu.CompilerParams(vmem_limit_bytes=VMEM),
        cost_estimate=pl.CostEstimate(
            flops=flops, bytes_accessed=megabytes << 20, transcendentals=0
        ),
        **kwargs,
    )


def smem():
    return pl.BlockSpec(memory_space=pltpu.SMEM)


def untouched():
    return pl.BlockSpec(memory_space=pl.ANY)


def whole_vmem(pieces=1):
    return pl.BlockSpec(memory_space=pltpu.VMEM)


def pack_kernel(first_turned, count_ref, coeffs_ref, rows_ref, turned_ref):
    step = pl.program_id(0)
    tile_rows = rows_ref.shape[0]
    live = count_ref[0] - step * tile_rows
    tile = jnp.swapaxes(coeffs_ref[...].astype(jnp.float32), 0, 1)
    row = lax.broadcasted_iota(jnp.int32, tile.shape, 0)
    rows_ref[...] = jnp.where(row < live, tile, 0.0).astype(jnp.bfloat16)

    @pl.when(step >= first_turned)
    def _():
        for j in range(tile_rows):
            turned_ref[tile_rows - 1 - j] = rows_ref[j]


def pack(coeffs, seg_count):
    orbs, slot_count, depth = coeffs.shape
    steps = slot_count // BIG
    half = steps // 2
    return call(
        functools.partial(pack_kernel, half),
        "pack_slots",
        (0, 10),
        grid=(steps,),
        in_specs=[smem(), pl.BlockSpec((orbs, BIG, depth), lambda i: (0, i, 0))],
        out_specs=[
            pl.BlockSpec((BIG, orbs, depth), lambda i: (i, 0, 0)),
            pl.BlockSpec(
                (BIG, orbs, depth), lambda i: (jnp.minimum(steps - 1 - i, half - 1), 0, 0)
            ),
        ],
        out_shape=[
            jax.ShapeDtypeStruct((slot_count, orbs, depth), jnp.bfloat16),
            jax.ShapeDtypeStruct((slot_count // 2, orbs, depth), jnp.bfloat16),
        ],
    )(seg_count, coeffs)


def merge(rows, received, seg_count, used, order=None):
    slot_count, orbs, depth = rows.shape
    if used == slot_count:
        return rows
    moved = received.shape[0]
    first = used - moved

    def kernel(count_ref, own_ref, other_ref, order_ref, out_ref, tail_ref, sem_in, sem_out):
        load = pltpu.make_async_copy(own_ref.at[pl.ds(first, moved)], tail_ref, sem_in)
        load.start()
        load.wait()

        @pl.loop(0, moved // TILE)
        def _(block):
            at = pl.ds(block * TILE, TILE)
            live = count_ref[0] - (first + block * TILE)
            row = lax.broadcasted_iota(jnp.int32, (TILE, orbs, depth), 0)
            own, other = tail_ref[at].astype(jnp.float32), other_ref[at].astype(jnp.float32)
            tail_ref[at] = jnp.where(row < live, own, other).astype(jnp.bfloat16)

        store = pltpu.make_async_copy(tail_ref, out_ref.at[pl.ds(first, moved)], sem_out)
        store.start()
        store.wait()

    return call(
        kernel,
        "merge_rows",
        (0, 4),
        in_specs=[smem(), untouched(), whole_vmem(), untouched()],
        out_specs=untouched(),
        out_shape=jax.ShapeDtypeStruct((used, orbs, depth), jnp.bfloat16),
        scratch_shapes=[
            pltpu.VMEM((moved, orbs, depth), jnp.bfloat16),
            pltpu.SemaphoreType.DMA,
            pltpu.SemaphoreType.DMA,
        ],
        input_output_aliases={1: 0},
    )(seg_count, rows[:used], received, received if order is None else order)


def edge_kernel(count_ref, place_ref, rows_ref, order_ref, edge_ref):
    count = count_ref[0]

    @pl.loop(0, edge_ref.shape[0] // 8)
    def _(block):
        edge_ref[pl.ds(block * 8, 8)] = jnp.zeros((8,) + edge_ref.shape[1:], edge_ref.dtype)

    @pl.loop(0, lax.div(count + GROUP - 1, GROUP))
    def _(group):
        for u in range(GROUP):
            j = group * GROUP + u
            edge_ref[place_ref[j]] = rows_ref[j]


def edges_of(rows, seg_count, places, order, edge_lines):
    _, orbs, depth = rows.shape
    return call(
        edge_kernel,
        "edge_planes",
        (0, 8),
        in_specs=[smem(), smem(), whole_vmem(), untouched()],
        out_specs=whole_vmem(),
        out_shape=jax.ShapeDtypeStruct((2 * edge_lines + 8, orbs, depth), jnp.bfloat16),
    )(seg_count, places, rows, order)


def apply_kernel(
    cells_x,
    cells_y,
    count_ref,
    lines_ref,
    place_ref,
    rows_ref,
    low_ref,
    high_ref,
    potential_ref,
    band_ref,
    order_ref,
    applied_ref,
    turned_ref,
    grid_ref,
    zsum_ref,
):
    step = pl.program_id(0)
    pitch = cells_y + PITCH_PAD
    count = count_ref[0]
    base = step * APPLY_TILE
    live = jnp.minimum(count - base, APPLY_TILE)
    reach = RADIUS * pitch

    @pl.when(step == 0)
    def _():
        @pl.loop(0, grid_ref.shape[0] // 16)
        def _(block):
            grid_ref[pl.ds(block * 16, 16)] = jnp.zeros((16,) + grid_ref.shape[1:], jnp.float32)

        for plane in range(RADIUS):
            for source, at in ((low_ref, plane), (high_ref, plane + RADIUS + cells_x)):

                @pl.loop(0, cells_y // 16)
                def _(block, source=source, at=at, plane=plane):
                    grid_ref[pl.ds(at * pitch + RADIUS + block * 16, 16)] = source[
                        pl.ds(plane * cells_y + block * 16, 16)
                    ].astype(jnp.float32)

        @pl.loop(0, lax.div(count + GROUP - 1, GROUP))
        def _(group):
            first = group * GROUP
            tiles = [(place_ref[first + u], rows_ref[first + u]) for u in range(GROUP)]
            for place, tile in tiles:
                grid_ref[place + reach] = tile.astype(jnp.float32)

    applied_ref[...] = jnp.zeros_like(applied_ref)

    @pl.when(live > 0)
    def _():
        tile = rows_ref[pl.ds(base, APPLY_TILE)].astype(jnp.float32)
        flat = tile.reshape(APPLY_TILE * tile.shape[1], tile.shape[2]).astype(jnp.bfloat16)
        zsum = jnp.dot(flat, band_ref[...], preferred_element_type=jnp.float32)
        zsum_ref[...] = (KINETIC * zsum).reshape(zsum_ref.shape)

        @pl.loop(0, lax.div(live + GROUP - 1, GROUP))
        def _(group):
            values = []
            for u in range(GROUP):
                j = group * GROUP + u
                line = lines_ref[base + j]
                near = grid_ref.at[pl.ds(place_ref[base + j], 2 * reach + 1)]
                terms = [
                    near[reach] * (potential_ref[pl.ds(line, 1), :] + (2.0 * KINETIC * TAPS[0]))
                ]
                for k in range(1, RADIUS + 1):
                    pair = near[reach - k] + near[reach + k]
                    pair = pair + (near[reach - k * pitch] + near[reach + k * pitch])
                    terms.append((KINETIC * TAPS[k]) * pair)
                while len(terms) > 1:
                    terms = [p + q for p, q in zip(terms[::2], terms[1::2])]
                value = terms[0] + zsum_ref[j]
                values.append(jnp.where(j < live, value, 0.0).astype(jnp.bfloat16))
            for u in range(GROUP):
                applied_ref[group * GROUP + u] = values[u]

    @pl.when(step >= pl.num_programs(0) // 2)
    def _():
        for j in range(APPLY_TILE):
            turned_ref[APPLY_TILE - 1 - j] = applied_ref[j]


def apply_rows(rows, seg_count, lines, places, low, high, potential, order):
    slot_count, orbs, depth = rows.shape
    cells_x, cells_y, _ = potential.shape
    edge_lines = RADIUS * cells_y
    grid_rows = (cells_x + 2 * RADIUS) * (cells_y + PITCH_PAD)
    once = pl.Buffered(1)
    whole = lambda i: (0, 0, 0)
    steps = slot_count // APPLY_TILE
    half = steps // 2
    return call(
        functools.partial(apply_kernel, cells_x, cells_y),
        "apply_rows",
        (2 << 30, 80),
        grid=(steps,),
        in_specs=[
            smem(),
            smem(),
            smem(),
            pl.BlockSpec((slot_count, orbs, depth), whole, pipeline_mode=once),
            pl.BlockSpec((edge_lines, orbs, depth), whole, pipeline_mode=once),
            pl.BlockSpec((edge_lines, orbs, depth), whole, pipeline_mode=once),
            pl.BlockSpec((cells_x * cells_y, depth), lambda i: (0, 0), pipeline_mode=once),
            pl.BlockSpec((depth, depth), lambda i: (0, 0), pipeline_mode=once),
            untouched(),
        ],
        out_specs=[
            pl.BlockSpec((APPLY_TILE, orbs, depth), lambda i: (i, 0, 0)),
            pl.BlockSpec(
                (APPLY_TILE, orbs, depth), lambda i: (jnp.minimum(steps - 1 - i, half - 1), 0, 0)
            ),
        ],
        out_shape=[
            jax.ShapeDtypeStruct((slot_count, orbs, depth), jnp.bfloat16),
            jax.ShapeDtypeStruct((slot_count // 2, orbs, depth), jnp.bfloat16),
        ],
        scratch_shapes=[
            pltpu.VMEM((grid_rows, orbs, depth), jnp.float32),
            pltpu.VMEM((APPLY_TILE, orbs, depth), jnp.float32),
        ],
    )(
        seg_count,
        lines,
        places,
        rows,
        low,
        high,
        potential.reshape(cells_x * cells_y, depth),
        jnp.asarray(band_matrix(depth)),
        order,
    )


def tail_rows(rows, moved, order):
    used, orbs, depth = rows.shape

    def kernel(rows_ref, *refs):
        out_ref, tail_ref, sem = refs[-3:]
        copy = pltpu.make_async_copy(rows_ref.at[pl.ds(used - moved, moved)], tail_ref, sem)
        copy.start()
        copy.wait()

        @pl.loop(0, moved // 16)
        def _(block):
            for u in range(16):
                out_ref[moved - 1 - (block * 16 + u)] = tail_ref[block * 16 + u]

    return call(
        kernel,
        "tail_rows",
        (0, 4),
        in_specs=[untouched()] * (1 + len(order)),
        out_specs=whole_vmem(),
        out_shape=jax.ShapeDtypeStruct((moved, orbs, depth), jnp.bfloat16),
        scratch_shapes=[pltpu.VMEM((moved, orbs, depth), jnp.bfloat16), pltpu.SemaphoreType.DMA],
    )(rows, *order)


def unpack(rows, returned, seg_count, slot_count):
    used, orbs, depth = rows.shape
    steps = slot_count // BIG
    pieces = BIG // TILE
    kept = used // TILE

    def kernel(count_ref, rows_ref, returned_ref, out_ref):
        step = pl.program_id(0)
        for piece in range(pieces):
            block = step * pieces + piece
            live = count_ref[0] - block * TILE

            def put(tile, live=live, piece=piece):
                row = lax.broadcasted_iota(jnp.int32, tile.shape, 0)
                tile = jnp.where(row < live, tile.astype(jnp.float32), 0.0)
                out_ref[:, pl.ds(piece * TILE, TILE), :] = jnp.swapaxes(tile, 0, 1).astype(
                    jnp.bfloat16
                )

            @pl.when(block < kept)
            def _():
                put(rows_ref[pl.ds(block * TILE, TILE)])

            if kept * TILE < slot_count:

                @pl.when(block >= kept)
                def _():
                    put(returned_ref[pl.ds((block - kept) * TILE, TILE)])

    return call(
        kernel,
        "unpack_slots",
        (0, 10),
        grid=(steps,),
        in_specs=[smem(), whole_vmem(), whole_vmem()],
        out_specs=pl.BlockSpec((orbs, BIG, depth), lambda i: (0, i, 0)),
        out_shape=jax.ShapeDtypeStruct((orbs, slot_count, depth), jnp.bfloat16),
    )(seg_count, rows, returned)


def stacked(ref, start, depth):
    value = ref[:, pl.ds(start, SLOTS)].astype(jnp.float32)
    norb = value.shape[0] * value.shape[2]
    tiles = [value[:, u].reshape(norb, depth) for u in range(SLOTS)]
    return jnp.concatenate(tiles, axis=1).astype(jnp.bfloat16)


def gram(left, right, order):
    parts, slots, orbs, depth = left.shape
    norb = parts * orbs
    if orbs % 8 or slots % SLOTS:
        product = jnp.einsum("asoz,bspz->aobp", left, right, preferred_element_type=jnp.float32)
        return product.reshape(norb, norb)
    same = left is right

    def kernel(*refs):
        out_ref = refs[-1]
        out_ref[...] = jnp.zeros_like(out_ref)

        @pl.loop(0, slots // SLOTS)
        def _(block):
            one = stacked(refs[0], block * SLOTS, depth)
            two = one if same else stacked(refs[1], block * SLOTS, depth)
            out_ref[...] += lax.dot_general(
                one, two, (((1,), (1,)), ((), ())), preferred_element_type=jnp.float32
            )

    given = (left,) if same else (left, right)
    return call(
        kernel,
        "gram",
        (1 << 28, 4 * len(given)),
        in_specs=[whole_vmem()] * len(given) + [untouched()] * len(order),
        out_specs=whole_vmem(),
        out_shape=jax.ShapeDtypeStruct((norb, norb), jnp.float32),
    )(*given, *order)


def turn(half, value, order):
    parts, slots, orbs, depth = value.shape
    norb = parts * orbs
    if orbs % 8 or slots % SLOTS:
        blocks = half.reshape(parts, orbs, parts, orbs)
        turned = jnp.einsum("aobp,asoz->bspz", blocks, value, preferred_element_type=jnp.float32)
        return turned.astype(jnp.bfloat16)

    def kernel(half_ref, value_ref, order_ref, out_ref):
        @pl.loop(0, slots // SLOTS)
        def _(block):
            rows = stacked(value_ref, block * SLOTS, depth)
            product = jnp.dot(half_ref[...], rows, preferred_element_type=jnp.float32)
            for u in range(SLOTS):
                tile = product[:, u * depth : (u + 1) * depth].reshape(parts, orbs, depth)
                out_ref[:, block * SLOTS + u] = tile.astype(jnp.bfloat16)

    return call(
        kernel,
        "turn_rows",
        (1 << 28, 8),
        in_specs=[whole_vmem(), whole_vmem(), untouched()],
        out_specs=whole_vmem(),
        out_shape=jax.ShapeDtypeStruct(value.shape, jnp.bfloat16),
    )(half.T, value, order)


def body(coeffs, seg_count, seg_lines, potential):
    orbs, slot_count, depth = coeffs.shape
    cells_x, cells_y, _ = potential.shape
    n_orb, n_seg = lax.axis_size("orb"), lax.axis_size("seg")
    ends = n_seg - 1
    norb = n_orb * orbs
    lines = seg_lines[0]
    edge_lines = RADIUS * cells_y
    weight_sum = 2.0 / (n_seg * slot_count * depth)

    most = seg_count + swapped(seg_count, "seg", 1)
    for distance in bits("seg")[1:]:
        most = jnp.maximum(most, swapped(most, "seg", distance))
    rows, turned = pack(coeffs, seg_count)
    live = jnp.arange(slot_count) < seg_count[0]
    tail = lines - (cells_x * cells_y - 2 * edge_lines)
    on_edge = jnp.where(lines < edge_lines, lines, jnp.where(tail >= edge_lines, tail, 2 * edge_lines))
    on_edge = jnp.where(live, on_edge, 2 * edge_lines)
    dump = cells_y + 2 * RADIUS
    places = lines + (lines // cells_y) * PITCH_PAD + RADIUS
    places = jnp.where(live, places, dump)

    def rest(used, operands):
        rows, turned, on_edge, places = operands
        moved = slot_count - used

        def spread(value):
            value = lax.all_to_all(value, "orb", split_axis=0, concat_axis=0, tiled=True)
            return value.reshape(n_orb, used // n_orb, orbs, depth)

        def to_partner(value, turned, order=None):
            if not moved:
                return value
            received = swapped(turned[:moved], "seg", 1)
            return merge(value, received, seg_count, used, order)

        def gather(value):
            value = value.reshape(used, orbs, depth)
            return lax.all_to_all(value, "orb", split_axis=0, concat_axis=0, tiled=True)

        def collect(value, order):
            returned = swapped(tail_rows(value, moved, order), "seg", 1) if moved else value
            return unpack(value, returned, seg_count, slot_count)

        merged = to_partner(rows, turned)
        slot_orbitals = spread(merged)

        edges = edges_of(rows, seg_count, on_edge, merged, edge_lines)
        low = lax.ppermute(
            edges[edge_lines : 2 * edge_lines], "seg", [(i, i + 1) for i in range(ends)]
        )
        high = lax.ppermute(edges[:edge_lines], "seg", [(i + 1, i) for i in range(ends)])
        intersection = total(gram(slot_orbitals, slot_orbitals, (low, high)), 2) * weight_sum
        rotation = inverse_root(intersection)
        half = rotation.astype(jnp.bfloat16)
        turned_orbitals = turn(half, slot_orbitals, half)

        applied, reversed_applied = apply_rows(
            rows, seg_count, lines, places, low, high, potential, turned_orbitals
        )
        arrived_orbitals = gather(turned_orbitals)
        slot_applied = spread(to_partner(applied, reversed_applied, arrived_orbitals))
        rotated_orbitals = collect(arrived_orbitals, (half,))

        turned_applied = turn(half, slot_applied, rotated_orbitals)
        energy = gram(slot_orbitals, slot_applied, (turned_applied,))
        hamiltonian = total(energy, 3) * weight_sum
        precise = lax.Precision.HIGHEST
        rotated_hamiltonian = jnp.dot(
            jnp.dot(rotation.T, hamiltonian, precision=precise), rotation, precision=precise
        )
        rotated_applied = collect(gather(turned_applied), (rotated_hamiltonian,))
        return rotated_orbitals, rotated_applied, rotated_hamiltonian

    first = slot_count // 2
    classes = [first + TILE * (i + 1) for i in range((slot_count - first) // TILE)]
    chosen = jnp.clip(((most[0] + 1) // 2 - first + TILE - 1) // TILE - 1, 0, len(classes) - 1)
    return lax.switch(chosen, [functools.partial(rest, used) for used in classes], (rows, turned, on_edge, places))


def solution(mesh):
    in_specs = (P("orb", "seg", None), P("seg"), P("seg", None), P("seg", None, None))
    out_specs = (P("orb", "seg", None), P("orb", "seg", None), P())
    return jax.shard_map(body, mesh=mesh, in_specs=in_specs, out_specs=out_specs, check_vma=False)
```

```python
import functools
import math

import jax
import jax.numpy as jnp
import ml_dtypes
import numpy as np
from jax import lax
from jax.experimental import pallas as pl
from jax.experimental.pallas import tpu as pltpu
from jax.sharding import PartitionSpec as P

SWEEPS = 6
RADIUS = 7
KINETIC = -0.5 / 2.25
TILE = 128
APPLY_TILE = 256
BIG = 512
GROUP = 8
SLOTS = 16
PITCH_PAD = 16
VMEM = 60 * 1024 * 1024


def tap_values():
    exact = [-math.pi * math.pi / 3.0]
    exact += [2.0 * (1.0 if k % 2 else -1.0) / (k * k) for k in range(1, RADIUS + 1)]
    return [float(np.float32(v).astype(ml_dtypes.bfloat16)) for v in exact]


TAPS = tap_values()


def band_matrix(n):
    table = np.zeros((n, n), np.float32)
    for i in range(n):
        for j in range(n):
            if abs(i - j) <= RADIUS:
                table[i, j] = TAPS[abs(i - j)]
    return table.astype(ml_dtypes.bfloat16)


def inverse_root(intersection):
    high = lax.Precision.HIGHEST
    norm_scale = jnp.sqrt(jnp.sum(intersection * intersection) + 1e-06)
    identity = jnp.eye(intersection.shape[0], dtype=jnp.float32)
    upper = intersection / norm_scale
    lower = identity
    for sweep_id in range(SWEEPS):
        middle = 0.5 * (3.0 * identity - jnp.dot(lower, upper, precision=high))
        upper = jnp.dot(upper, middle, precision=high)
        lower = jnp.dot(middle, lower, precision=high)
    return lower / jnp.sqrt(norm_scale)


def swapped(value, axis, distance):
    size = lax.axis_size(axis)
    return lax.ppermute(value, axis, [(i, i ^ distance) for i in range(size)])


def bits(axis):
    size = lax.axis_size(axis)
    return [1 << b for b in range(size.bit_length() - 1)]


def terms_of(value, axis, now):
    masks = [0]
    for bit in now:
        masks += [mask | bit for mask in masks]
    return [swapped(value, axis, mask) if mask else value for mask in masks]


def added(terms):
    while len(terms) > 1:
        terms = [p + q for p, q in zip(terms[::2], terms[1::2])]
    return terms[0]


def total(value, axes):
    for axis in axes:
        left = bits(axis)
        while left:
            now, left = left[-2:], left[:-2]
            value = added(terms_of(value, axis, now))
    return value


def call(kernel, name, cost, **kwargs):
    flops, megabytes = cost
    return pl.pallas_call(
        kernel,
        name=name,
        compiler_params=pltpu.CompilerParams(vmem_limit_bytes=VMEM),
        cost_estimate=pl.CostEstimate(
            flops=flops, bytes_accessed=megabytes << 20, transcendentals=0
        ),
        **kwargs,
    )


def smem():
    return pl.BlockSpec(memory_space=pltpu.SMEM)


def untouched():
    return pl.BlockSpec(memory_space=pl.ANY)


def whole_vmem(pieces=1):
    return pl.BlockSpec(memory_space=pltpu.VMEM)


def pack_kernel(first_turned, count_ref, coeffs_ref, rows_ref, turned_ref):
    step = pl.program_id(0)
    tile_rows = rows_ref.shape[0]
    live = count_ref[0] - step * tile_rows
    tile = jnp.swapaxes(coeffs_ref[...].astype(jnp.float32), 0, 1)
    row = lax.broadcasted_iota(jnp.int32, tile.shape, 0)
    rows_ref[...] = jnp.where(row < live, tile, 0.0).astype(jnp.bfloat16)

    @pl.when(step >= first_turned)
    def _():
        @pl.loop(0, tile_rows // 16)
        def _(block):
            for u in range(16):
                j = block * 16 + u
                turned_ref[tile_rows - 1 - j] = rows_ref[j]


def pack(coeffs, seg_count):
    orbs, slot_count, depth = coeffs.shape
    steps = slot_count // BIG
    half = steps // 2
    return call(
        functools.partial(pack_kernel, half),
        "pack_slots",
        (0, 10),
        grid=(steps,),
        in_specs=[smem(), pl.BlockSpec((orbs, BIG, depth), lambda i: (0, i, 0))],
        out_specs=[
            pl.BlockSpec((BIG, orbs, depth), lambda i: (i, 0, 0)),
            pl.BlockSpec(
                (BIG, orbs, depth), lambda i: (jnp.minimum(steps - 1 - i, half - 1), 0, 0)
            ),
        ],
        out_shape=[
            jax.ShapeDtypeStruct((slot_count, orbs, depth), jnp.bfloat16),
            jax.ShapeDtypeStruct((slot_count // 2, orbs, depth), jnp.bfloat16),
        ],
    )(seg_count, coeffs)


def after(value, order):
    def kernel(value_ref, order_ref, out_ref):
        pass

    return call(
        kernel,
        "after",
        (0, 0),
        in_specs=[untouched(), untouched()],
        out_specs=untouched(),
        out_shape=jax.ShapeDtypeStruct(value.shape, value.dtype),
        input_output_aliases={0: 0},
    )(value, order)


def merge(rows, received, seg_count, used):
    slot_count, orbs, depth = rows.shape
    if used == slot_count:
        return rows
    moved = received.shape[0]
    first = used - moved

    def kernel(count_ref, own_ref, other_ref, out_ref, tail_ref, sem_in, sem_out):
        load = pltpu.make_async_copy(own_ref.at[pl.ds(first, moved)], tail_ref, sem_in)
        load.start()
        load.wait()

        @pl.loop(0, moved // TILE)
        def _(block):
            at = pl.ds(block * TILE, TILE)
            live = count_ref[0] - (first + block * TILE)

            @pl.when(live <= 0)
            def _():
                tail_ref[at] = other_ref[at]

            @pl.when((live > 0) & (live < TILE))
            def _():
                row = lax.broadcasted_iota(jnp.int32, (TILE, orbs, depth), 0)
                own, other = tail_ref[at].astype(jnp.float32), other_ref[at].astype(jnp.float32)
                tail_ref[at] = jnp.where(row < live, own, other).astype(jnp.bfloat16)

        store = pltpu.make_async_copy(tail_ref, out_ref.at[pl.ds(first, moved)], sem_out)
        store.start()
        store.wait()

    return call(
        kernel,
        "merge_rows",
        (0, 4),
        in_specs=[smem(), untouched(), whole_vmem()],
        out_specs=untouched(),
        out_shape=jax.ShapeDtypeStruct((used, orbs, depth), jnp.bfloat16),
        scratch_shapes=[
            pltpu.VMEM((moved, orbs, depth), jnp.bfloat16),
            pltpu.SemaphoreType.DMA,
            pltpu.SemaphoreType.DMA,
        ],
        input_output_aliases={1: 0},
    )(seg_count, rows[:used], received)


def edge_kernel(count_ref, place_ref, rows_ref, order_ref, edge_ref):
    count = count_ref[0]

    @pl.loop(0, edge_ref.shape[0] // 8)
    def _(block):
        edge_ref[pl.ds(block * 8, 8)] = jnp.zeros((8,) + edge_ref.shape[1:], edge_ref.dtype)

    @pl.loop(0, lax.div(count + GROUP - 1, GROUP))
    def _(group):
        for u in range(GROUP):
            j = group * GROUP + u
            edge_ref[place_ref[j]] = rows_ref[j]


def edges_of(rows, seg_count, places, order, edge_lines):
    _, orbs, depth = rows.shape
    return call(
        edge_kernel,
        "edge_planes",
        (0, 8),
        in_specs=[smem(), smem(), whole_vmem(), untouched()],
        out_specs=whole_vmem(),
        out_shape=jax.ShapeDtypeStruct((2 * edge_lines + 8, orbs, depth), jnp.bfloat16),
    )(seg_count, places, rows, order)


def apply_kernel(
    cells_x,
    cells_y,
    count_ref,
    lines_ref,
    place_ref,
    rows_ref,
    low_ref,
    high_ref,
    potential_ref,
    band_ref,
    order_ref,
    applied_ref,
    turned_ref,
    grid_ref,
    zsum_ref,
):
    step = pl.program_id(0)
    pitch = cells_y + PITCH_PAD
    count = count_ref[0]
    base = step * APPLY_TILE
    live = jnp.minimum(count - base, APPLY_TILE)
    reach = RADIUS * pitch

    @pl.when(step == 0)
    def _():
        @pl.loop(0, grid_ref.shape[0] // 16)
        def _(block):
            grid_ref[pl.ds(block * 16, 16)] = jnp.zeros((16,) + grid_ref.shape[1:], jnp.float32)

        blocks = cells_y // 16

        @pl.loop(0, RADIUS * blocks)
        def _(index):
            plane = lax.div(index, blocks)
            inside = RADIUS + (index - plane * blocks) * 16
            source = pl.ds(index * 16, 16)
            grid_ref[pl.ds(plane * pitch + inside, 16)] = low_ref[source].astype(jnp.float32)
            above = (plane + RADIUS + cells_x) * pitch + inside
            grid_ref[pl.ds(above, 16)] = high_ref[source].astype(jnp.float32)

        @pl.loop(0, lax.div(count + GROUP - 1, GROUP))
        def _(group):
            first = group * GROUP
            tiles = [(place_ref[first + u], rows_ref[first + u]) for u in range(GROUP)]
            for place, tile in tiles:
                grid_ref[place + reach] = tile.astype(jnp.float32)

    applied_ref[...] = jnp.zeros_like(applied_ref)

    @pl.when(live > 0)
    def _():
        part = APPLY_TILE // 4

        @pl.loop(0, 4)
        def _(block):
            tile = rows_ref[pl.ds(base + block * part, part)].astype(jnp.float32)
            flat = tile.reshape(part * tile.shape[1], tile.shape[2]).astype(jnp.bfloat16)
            zsum = jnp.dot(flat, band_ref[...], preferred_element_type=jnp.float32)
            zsum_ref[pl.ds(block * part, part)] = (KINETIC * zsum).reshape(tile.shape)

        @pl.loop(0, lax.div(live + GROUP - 1, GROUP))
        def _(group):
            values = []
            for u in range(GROUP):
                j = group * GROUP + u
                line = lines_ref[base + j]
                near = grid_ref.at[pl.ds(place_ref[base + j], 2 * reach + 1)]
                terms = [
                    near[reach] * (potential_ref[pl.ds(line, 1), :] + (2.0 * KINETIC * TAPS[0]))
                ]
                for k in range(1, RADIUS + 1):
                    pair = near[reach - k] + near[reach + k]
                    pair = pair + (near[reach - k * pitch] + near[reach + k * pitch])
                    terms.append((KINETIC * TAPS[k]) * pair)
                while len(terms) > 1:
                    terms = [p + q for p, q in zip(terms[::2], terms[1::2])]
                value = terms[0] + zsum_ref[j]
                values.append(jnp.where(j < live, value, 0.0).astype(jnp.bfloat16))
            for u in range(GROUP):
                applied_ref[group * GROUP + u] = values[u]

    @pl.when(step >= pl.num_programs(0) // 2)
    def _():
        @pl.loop(0, APPLY_TILE // 16)
        def _(block):
            for u in range(16):
                j = block * 16 + u
                turned_ref[APPLY_TILE - 1 - j] = applied_ref[j]


def apply_rows(rows, seg_count, lines, places, low, high, potential, order):
    slot_count, orbs, depth = rows.shape
    cells_x, cells_y, _ = potential.shape
    edge_lines = RADIUS * cells_y
    grid_rows = (cells_x + 2 * RADIUS) * (cells_y + PITCH_PAD)
    once = pl.Buffered(1)
    whole = lambda i: (0, 0, 0)
    steps = slot_count // APPLY_TILE
    half = steps // 2
    return call(
        functools.partial(apply_kernel, cells_x, cells_y),
        "apply_rows",
        (2 << 30, 80),
        grid=(steps,),
        in_specs=[
            smem(),
            smem(),
            smem(),
            pl.BlockSpec((slot_count, orbs, depth), whole, pipeline_mode=once),
            pl.BlockSpec((edge_lines, orbs, depth), whole, pipeline_mode=once),
            pl.BlockSpec((edge_lines, orbs, depth), whole, pipeline_mode=once),
            pl.BlockSpec((cells_x * cells_y, depth), lambda i: (0, 0), pipeline_mode=once),
            pl.BlockSpec((depth, depth), lambda i: (0, 0), pipeline_mode=once),
            untouched(),
        ],
        out_specs=[
            pl.BlockSpec((APPLY_TILE, orbs, depth), lambda i: (i, 0, 0)),
            pl.BlockSpec(
                (APPLY_TILE, orbs, depth), lambda i: (jnp.minimum(steps - 1 - i, half - 1), 0, 0)
            ),
        ],
        out_shape=[
            jax.ShapeDtypeStruct((slot_count, orbs, depth), jnp.bfloat16),
            jax.ShapeDtypeStruct((slot_count // 2, orbs, depth), jnp.bfloat16),
        ],
        scratch_shapes=[
            pltpu.VMEM((grid_rows, orbs, depth), jnp.float32),
            pltpu.VMEM((APPLY_TILE, orbs, depth), jnp.float32),
        ],
    )(
        seg_count,
        lines,
        places,
        rows,
        low,
        high,
        potential.reshape(cells_x * cells_y, depth),
        jnp.asarray(band_matrix(depth)),
        order,
    )


def tail_rows(rows, moved, order):
    used, orbs, depth = rows.shape

    def kernel(rows_ref, *refs):
        out_ref, tail_ref, sem = refs[-3:]
        copy = pltpu.make_async_copy(rows_ref.at[pl.ds(used - moved, moved)], tail_ref, sem)
        copy.start()
        copy.wait()

        @pl.loop(0, moved // 16)
        def _(block):
            for u in range(16):
                out_ref[moved - 1 - (block * 16 + u)] = tail_ref[block * 16 + u]

    return call(
        kernel,
        "tail_rows",
        (0, 4),
        in_specs=[untouched()] * (1 + len(order)),
        out_specs=whole_vmem(),
        out_shape=jax.ShapeDtypeStruct((moved, orbs, depth), jnp.bfloat16),
        scratch_shapes=[pltpu.VMEM((moved, orbs, depth), jnp.bfloat16), pltpu.SemaphoreType.DMA],
    )(rows, *order)


def unpack(rows, returned, seg_count, slot_count):
    used, orbs, depth = rows.shape
    steps = slot_count // BIG
    pieces = BIG // TILE
    kept = used // TILE

    def kernel(count_ref, rows_ref, returned_ref, out_ref):
        step = pl.program_id(0)

        @pl.loop(0, pieces)
        def _(piece):
            block = step * pieces + piece
            live = count_ref[0] - block * TILE

            def put(tile):
                row = lax.broadcasted_iota(jnp.int32, tile.shape, 0)
                tile = jnp.where(row < live, tile.astype(jnp.float32), 0.0)
                at = pl.ds(pl.multiple_of(piece * TILE, TILE), TILE)
                out_ref[:, at, :] = jnp.swapaxes(tile, 0, 1).astype(jnp.bfloat16)

            @pl.when(block < kept)
            def _():
                put(rows_ref[pl.ds(block * TILE, TILE)])

            if kept * TILE < slot_count:

                @pl.when(block >= kept)
                def _():
                    put(returned_ref[pl.ds((block - kept) * TILE, TILE)])

    return call(
        kernel,
        "unpack_slots",
        (0, 10),
        grid=(steps,),
        in_specs=[smem(), whole_vmem(), whole_vmem()],
        out_specs=pl.BlockSpec((orbs, BIG, depth), lambda i: (0, i, 0)),
        out_shape=jax.ShapeDtypeStruct((orbs, slot_count, depth), jnp.bfloat16),
    )(seg_count, rows, returned)


def stacked(ref, start, depth):
    value = ref[:, pl.ds(start, SLOTS)].astype(jnp.float32)
    norb = value.shape[0] * value.shape[2]
    tiles = [value[:, u].reshape(norb, depth) for u in range(SLOTS)]
    return jnp.concatenate(tiles, axis=1).astype(jnp.bfloat16)


def gram(left, right, order):
    parts, slots, orbs, depth = left.shape
    norb = parts * orbs
    if orbs % 8 or slots % SLOTS:
        product = jnp.einsum("asoz,bspz->aobp", left, right, preferred_element_type=jnp.float32)
        return product.reshape(norb, norb)
    same = left is right

    def kernel(*refs):
        out_ref = refs[-1]
        out_ref[...] = jnp.zeros_like(out_ref)

        @pl.loop(0, slots // SLOTS)
        def _(block):
            one = stacked(refs[0], block * SLOTS, depth)
            two = one if same else stacked(refs[1], block * SLOTS, depth)
            out_ref[...] += lax.dot_general(
                one, two, (((1,), (1,)), ((), ())), preferred_element_type=jnp.float32
            )

    given = (left,) if same else (left, right)
    return call(
        kernel,
        "gram",
        (1 << 28, 4 * len(given)),
        in_specs=[whole_vmem()] * len(given) + [untouched()] * len(order),
        out_specs=whole_vmem(),
        out_shape=jax.ShapeDtypeStruct((norb, norb), jnp.float32),
    )(*given, *order)


def turn(half, value, order):
    parts, slots, orbs, depth = value.shape
    norb = parts * orbs
    if orbs % 8 or slots % SLOTS:
        blocks = half.reshape(parts, orbs, parts, orbs)
        turned = jnp.einsum("aobp,asoz->bspz", blocks, value, preferred_element_type=jnp.float32)
        return turned.astype(jnp.bfloat16)

    def kernel(half_ref, value_ref, order_ref, out_ref):
        @pl.loop(0, slots // SLOTS)
        def _(block):
            rows = stacked(value_ref, block * SLOTS, depth)
            product = jnp.dot(half_ref[...], rows, preferred_element_type=jnp.float32)
            for u in range(SLOTS):
                tile = product[:, u * depth : (u + 1) * depth].reshape(parts, orbs, depth)
                out_ref[:, block * SLOTS + u] = tile.astype(jnp.bfloat16)

    return call(
        kernel,
        "turn_rows",
        (1 << 28, 8),
        in_specs=[whole_vmem(), whole_vmem(), untouched()],
        out_specs=whole_vmem(),
        out_shape=jax.ShapeDtypeStruct(value.shape, jnp.bfloat16),
    )(half.T, value, order)


def finish(terms, rotation, weight_sum, order):
    def kernel(*refs):
        rotation_ref, transposed_ref = refs[len(terms) : len(terms) + 2]
        hamiltonian = added([ref[...] for ref in refs[: len(terms)]]) * weight_sum
        precise = dict(precision=lax.Precision.HIGHEST, preferred_element_type=jnp.float32)
        left = jnp.dot(transposed_ref[...], hamiltonian, **precise)
        refs[-1][...] = jnp.dot(left, rotation_ref[...], **precise)

    return call(
        kernel,
        "finish_hamiltonian",
        (1 << 20, 1),
        in_specs=[whole_vmem()] * (len(terms) + 2) + [untouched()],
        out_specs=whole_vmem(),
        out_shape=jax.ShapeDtypeStruct(rotation.shape, jnp.float32),
    )(*terms, rotation, rotation.T, order)


def body(coeffs, seg_count, seg_lines, potential):
    orbs, slot_count, depth = coeffs.shape
    cells_x, cells_y, _ = potential.shape
    n_orb, n_seg = lax.axis_size("orb"), lax.axis_size("seg")
    ends = n_seg - 1
    norb = n_orb * orbs
    lines = seg_lines[0]
    edge_lines = RADIUS * cells_y
    weight_sum = 2.0 / (n_seg * slot_count * depth)

    first_bits, more_bits = bits("seg")[:2], bits("seg")[2:]
    most = seg_count + swapped(seg_count, "seg", 1)
    if len(first_bits) > 1:
        other = swapped(seg_count, "seg", 2) + swapped(seg_count, "seg", 3)
        most = jnp.maximum(most, other)
    for distance in more_bits:
        most = jnp.maximum(most, swapped(most, "seg", distance))
    rows, turned = pack(coeffs, seg_count)
    live = jnp.arange(slot_count) < seg_count[0]
    tail = lines - (cells_x * cells_y - 2 * edge_lines)
    on_edge = jnp.where(lines < edge_lines, lines, jnp.where(tail >= edge_lines, tail, 2 * edge_lines))
    on_edge = jnp.where(live, on_edge, 2 * edge_lines)
    dump = cells_y + 2 * RADIUS
    places = lines + (lines // cells_y) * PITCH_PAD + RADIUS
    places = jnp.where(live, places, dump)

    def rest(used, operands):
        rows, turned, on_edge, places = operands
        moved = slot_count - used

        def spread(value):
            value = lax.all_to_all(value, "orb", split_axis=0, concat_axis=0, tiled=True)
            return value.reshape(n_orb, used // n_orb, orbs, depth)

        def to_partner(value, turned):
            if not moved:
                return value
            received = swapped(turned[:moved], "seg", 1)
            return merge(value, received, seg_count, used)

        def gather(value):
            value = value.reshape(used, orbs, depth)
            return lax.all_to_all(value, "orb", split_axis=0, concat_axis=0, tiled=True)

        def collect(value, order):
            returned = swapped(tail_rows(value, moved, order), "seg", 1) if moved else value
            return unpack(value, returned, seg_count, slot_count)

        merged = to_partner(rows, turned)
        slot_orbitals = spread(merged)

        edges = edges_of(rows, seg_count, on_edge, merged, edge_lines)
        low = lax.ppermute(
            edges[edge_lines : 2 * edge_lines], "seg", [(i, i + 1) for i in range(ends)]
        )
        high = lax.ppermute(edges[:edge_lines], "seg", [(i + 1, i) for i in range(ends)])
        intersection = total(gram(slot_orbitals, slot_orbitals, (low, high)), ("seg", "orb")) * weight_sum
        rotation = inverse_root(intersection)
        half = rotation.astype(jnp.bfloat16)
        turned_orbitals = turn(half, slot_orbitals, half)

        applied, reversed_applied = apply_rows(
            rows, seg_count, lines, places, low, high, potential, turned_orbitals
        )
        arrived_orbitals = gather(turned_orbitals)
        slot_applied = spread(after(to_partner(applied, reversed_applied), arrived_orbitals))
        rotated_orbitals = collect(arrived_orbitals, (half,))

        turned_applied = turn(half, slot_applied, rotated_orbitals)
        energy = gram(slot_orbitals, slot_applied, (turned_applied,))
        left = bits("orb")
        value = total(energy, ("seg",))
        while len(left) > 3:
            value, left = added(terms_of(value, "orb", left[-2:])), left[:-2]
        terms = terms_of(value, "orb", left)
        arrived_applied = gather(turned_applied)
        tail = tail_rows(arrived_applied, moved, (half,)) if moved else arrived_applied
        returned = swapped(tail, "seg", 1) if moved else tail
        rotated_hamiltonian = finish(terms, rotation, weight_sum, tail)
        rotated_applied = unpack(arrived_applied, returned, seg_count, slot_count)
        return rotated_orbitals, rotated_applied, rotated_hamiltonian

    first = slot_count // 2
    classes = [first + TILE * (i + 1) for i in range((slot_count - first) // TILE)]
    chosen = jnp.clip(((most[0] + 1) // 2 - first + TILE - 1) // TILE - 1, 0, len(classes) - 1)
    return lax.switch(chosen, [functools.partial(rest, used) for used in classes], (rows, turned, on_edge, places))


def solution(mesh):
    in_specs = (P("orb", "seg", None), P("seg"), P("seg", None), P("seg", None, None))
    out_specs = (P("orb", "seg", None), P("orb", "seg", None), P())
    return jax.shard_map(body, mesh=mesh, in_specs=in_specs, out_specs=out_specs, check_vma=False)
```

```python
import functools
import math

import jax
import jax.numpy as jnp
import ml_dtypes
import numpy as np
from jax import lax
from jax.experimental import pallas as pl
from jax.experimental.pallas import tpu as pltpu
from jax.sharding import PartitionSpec as P

SWEEPS = 6
RADIUS = 7
KINETIC = -0.5 / 2.25
TILE = 128
APPLY_TILE = 256
BIG = 512
GROUP = 8
SLOTS = 16
PITCH_PAD = 16
VMEM = 60 * 1024 * 1024


def tap_values():
    exact = [-math.pi * math.pi / 3.0]
    exact += [2.0 * (1.0 if k % 2 else -1.0) / (k * k) for k in range(1, RADIUS + 1)]
    return [float(np.float32(v).astype(ml_dtypes.bfloat16)) for v in exact]


TAPS = tap_values()


def band_matrix(n):
    table = np.zeros((n, n), np.float32)
    for i in range(n):
        for j in range(n):
            if abs(i - j) <= RADIUS:
                table[i, j] = TAPS[abs(i - j)]
    return table.astype(ml_dtypes.bfloat16)


def inverse_root(intersection):
    high = lax.Precision.HIGHEST
    norm_scale = jnp.sqrt(jnp.sum(intersection * intersection) + 1e-06)
    identity = jnp.eye(intersection.shape[0], dtype=jnp.float32)
    upper = intersection / norm_scale
    lower = identity
    for sweep_id in range(SWEEPS):
        middle = 0.5 * (3.0 * identity - jnp.dot(lower, upper, precision=high))
        upper = jnp.dot(upper, middle, precision=high)
        lower = jnp.dot(middle, lower, precision=high)
    return lower / jnp.sqrt(norm_scale)


def swapped(value, axis, distance):
    size = lax.axis_size(axis)
    return lax.ppermute(value, axis, [(i, i ^ distance) for i in range(size)])


def bits(axis):
    size = lax.axis_size(axis)
    return [1 << b for b in range(size.bit_length() - 1)]


def terms_of(value, axis, now):
    masks = [0]
    for bit in now:
        masks += [mask | bit for mask in masks]
    return [swapped(value, axis, mask) if mask else value for mask in masks]


def added(terms):
    while len(terms) > 1:
        terms = [p + q for p, q in zip(terms[::2], terms[1::2])]
    return terms[0]


def total(value, axes):
    for axis in axes:
        left = bits(axis)
        while left:
            now, left = left[-2:], left[:-2]
            value = added(terms_of(value, axis, now))
    return value


def call(kernel, name, cost, **kwargs):
    flops, megabytes = cost
    return pl.pallas_call(
        kernel,
        name=name,
        compiler_params=pltpu.CompilerParams(vmem_limit_bytes=VMEM),
        cost_estimate=pl.CostEstimate(
            flops=flops, bytes_accessed=megabytes << 20, transcendentals=0
        ),
        **kwargs,
    )


def smem():
    return pl.BlockSpec(memory_space=pltpu.SMEM)


def untouched():
    return pl.BlockSpec(memory_space=pl.ANY)


def whole_vmem(pieces=1):
    return pl.BlockSpec(memory_space=pltpu.VMEM)


def pack_kernel(first_turned, count_ref, coeffs_ref, rows_ref, turned_ref):
    step = pl.program_id(0)
    tile_rows = rows_ref.shape[0]
    live = count_ref[0] - step * tile_rows
    tile = jnp.swapaxes(coeffs_ref[...].astype(jnp.float32), 0, 1)
    row = lax.broadcasted_iota(jnp.int32, tile.shape, 0)
    rows_ref[...] = jnp.where(row < live, tile, 0.0).astype(jnp.bfloat16)

    @pl.when(step >= first_turned)
    def _():
        @pl.loop(0, tile_rows // 16)
        def _(block):
            for u in range(16):
                j = block * 16 + u
                turned_ref[tile_rows - 1 - j] = rows_ref[j]


def pack(coeffs, seg_count):
    orbs, slot_count, depth = coeffs.shape
    steps = slot_count // BIG
    half = steps // 2
    return call(
        functools.partial(pack_kernel, half),
        "pack_slots",
        (0, 10),
        grid=(steps,),
        in_specs=[smem(), pl.BlockSpec((orbs, BIG, depth), lambda i: (0, i, 0))],
        out_specs=[
            pl.BlockSpec((BIG, orbs, depth), lambda i: (i, 0, 0)),
            pl.BlockSpec(
                (BIG, orbs, depth), lambda i: (jnp.minimum(steps - 1 - i, half - 1), 0, 0)
            ),
        ],
        out_shape=[
            jax.ShapeDtypeStruct((slot_count, orbs, depth), jnp.bfloat16),
            jax.ShapeDtypeStruct((slot_count // 2, orbs, depth), jnp.bfloat16),
        ],
    )(seg_count, coeffs)


def after(value, order):
    def kernel(value_ref, order_ref, out_ref):
        pass

    return call(
        kernel,
        "after",
        (0, 0),
        in_specs=[untouched(), untouched()],
        out_specs=untouched(),
        out_shape=jax.ShapeDtypeStruct(value.shape, value.dtype),
        input_output_aliases={0: 0},
    )(value, order)


def merge(rows, received, seg_count, used):
    slot_count, orbs, depth = rows.shape
    if used == slot_count:
        return rows
    moved = received.shape[0]
    first = used - moved

    def kernel(count_ref, own_ref, other_ref, out_ref, tail_ref, sem_in, sem_out):
        load = pltpu.make_async_copy(own_ref.at[pl.ds(first, moved)], tail_ref, sem_in)
        load.start()
        load.wait()

        @pl.loop(0, moved // TILE)
        def _(block):
            at = pl.ds(block * TILE, TILE)
            live = count_ref[0] - (first + block * TILE)

            @pl.when(live <= 0)
            def _():
                tail_ref[at] = other_ref[at]

            @pl.when((live > 0) & (live < TILE))
            def _():
                row = lax.broadcasted_iota(jnp.int32, (TILE, orbs, depth), 0)
                own, other = tail_ref[at].astype(jnp.float32), other_ref[at].astype(jnp.float32)
                tail_ref[at] = jnp.where(row < live, own, other).astype(jnp.bfloat16)

        store = pltpu.make_async_copy(tail_ref, out_ref.at[pl.ds(first, moved)], sem_out)
        store.start()
        store.wait()

    return call(
        kernel,
        "merge_rows",
        (0, 4),
        in_specs=[smem(), untouched(), whole_vmem()],
        out_specs=untouched(),
        out_shape=jax.ShapeDtypeStruct((used, orbs, depth), jnp.bfloat16),
        scratch_shapes=[
            pltpu.VMEM((moved, orbs, depth), jnp.bfloat16),
            pltpu.SemaphoreType.DMA,
            pltpu.SemaphoreType.DMA,
        ],
        input_output_aliases={1: 0},
    )(seg_count, rows[:used], received)


def edge_kernel(count_ref, place_ref, rows_ref, order_ref, edge_ref):
    count = count_ref[0]

    @pl.loop(0, edge_ref.shape[0] // 8)
    def _(block):
        edge_ref[pl.ds(block * 8, 8)] = jnp.zeros((8,) + edge_ref.shape[1:], edge_ref.dtype)

    @pl.loop(0, lax.div(count + GROUP - 1, GROUP))
    def _(group):
        for u in range(GROUP):
            j = group * GROUP + u
            edge_ref[place_ref[j]] = rows_ref[j]


def edges_of(rows, seg_count, places, order, edge_lines):
    _, orbs, depth = rows.shape
    return call(
        edge_kernel,
        "edge_planes",
        (0, 8),
        in_specs=[smem(), smem(), whole_vmem(), untouched()],
        out_specs=whole_vmem(),
        out_shape=jax.ShapeDtypeStruct((2 * edge_lines + 8, orbs, depth), jnp.bfloat16),
    )(seg_count, places, rows, order)


def apply_kernel(
    cells_x,
    cells_y,
    count_ref,
    lines_ref,
    place_ref,
    rows_ref,
    low_ref,
    high_ref,
    potential_ref,
    band_ref,
    order_ref,
    applied_ref,
    turned_ref,
    grid_ref,
    zsum_ref,
):
    step = pl.program_id(0)
    pitch = cells_y + PITCH_PAD
    count = count_ref[0]
    base = step * APPLY_TILE
    live = jnp.minimum(count - base, APPLY_TILE)
    reach = RADIUS * pitch

    @pl.when(step == 0)
    def _():
        @pl.loop(0, grid_ref.shape[0] // 16)
        def _(block):
            grid_ref[pl.ds(block * 16, 16)] = jnp.zeros((16,) + grid_ref.shape[1:], jnp.float32)

        blocks = cells_y // 16

        @pl.loop(0, RADIUS * blocks)
        def _(index):
            plane = lax.div(index, blocks)
            inside = RADIUS + (index - plane * blocks) * 16
            source = pl.ds(index * 16, 16)
            grid_ref[pl.ds(plane * pitch + inside, 16)] = low_ref[source].astype(jnp.float32)
            above = (plane + RADIUS + cells_x) * pitch + inside
            grid_ref[pl.ds(above, 16)] = high_ref[source].astype(jnp.float32)

        @pl.loop(0, lax.div(count + GROUP - 1, GROUP))
        def _(group):
            first = group * GROUP
            tiles = [(place_ref[first + u], rows_ref[first + u]) for u in range(GROUP)]
            for place, tile in tiles:
                grid_ref[place + reach] = tile.astype(jnp.float32)

    applied_ref[...] = jnp.zeros_like(applied_ref)

    @pl.when(live > 0)
    def _():
        part = APPLY_TILE // 4

        @pl.loop(0, 4)
        def _(block):
            tile = rows_ref[pl.ds(base + block * part, part)].astype(jnp.float32)
            flat = tile.reshape(part * tile.shape[1], tile.shape[2]).astype(jnp.bfloat16)
            zsum = jnp.dot(flat, band_ref[...], preferred_element_type=jnp.float32)
            zsum_ref[pl.ds(block * part, part)] = (KINETIC * zsum).reshape(tile.shape)

        @pl.loop(0, lax.div(live + GROUP - 1, GROUP))
        def _(group):
            values = []
            for u in range(GROUP):
                j = group * GROUP + u
                line = lines_ref[base + j]
                near = grid_ref.at[pl.ds(place_ref[base + j], 2 * reach + 1)]
                terms = [
                    near[reach] * (potential_ref[pl.ds(line, 1), :] + (2.0 * KINETIC * TAPS[0]))
                ]
                for k in range(1, RADIUS + 1):
                    pair = near[reach - k] + near[reach + k]
                    pair = pair + (near[reach - k * pitch] + near[reach + k * pitch])
                    terms.append((KINETIC * TAPS[k]) * pair)
                while len(terms) > 1:
                    terms = [p + q for p, q in zip(terms[::2], terms[1::2])]
                value = terms[0] + zsum_ref[j]
                values.append(jnp.where(j < live, value, 0.0).astype(jnp.bfloat16))
            for u in range(GROUP):
                applied_ref[group * GROUP + u] = values[u]

    @pl.when(step >= pl.num_programs(0) // 2)
    def _():
        @pl.loop(0, APPLY_TILE // 16)
        def _(block):
            for u in range(16):
                j = block * 16 + u
                turned_ref[APPLY_TILE - 1 - j] = applied_ref[j]


def apply_rows(rows, seg_count, lines, places, low, high, potential, order):
    slot_count, orbs, depth = rows.shape
    cells_x, cells_y, _ = potential.shape
    edge_lines = RADIUS * cells_y
    grid_rows = (cells_x + 2 * RADIUS) * (cells_y + PITCH_PAD)
    once = pl.Buffered(1)
    whole = lambda i: (0, 0, 0)
    steps = slot_count // APPLY_TILE
    half = steps // 2
    return call(
        functools.partial(apply_kernel, cells_x, cells_y),
        "apply_rows",
        (2 << 30, 80),
        grid=(steps,),
        in_specs=[
            smem(),
            smem(),
            smem(),
            pl.BlockSpec((slot_count, orbs, depth), whole, pipeline_mode=once),
            pl.BlockSpec((edge_lines, orbs, depth), whole, pipeline_mode=once),
            pl.BlockSpec((edge_lines, orbs, depth), whole, pipeline_mode=once),
            pl.BlockSpec((cells_x * cells_y, depth), lambda i: (0, 0), pipeline_mode=once),
            pl.BlockSpec((depth, depth), lambda i: (0, 0), pipeline_mode=once),
            untouched(),
        ],
        out_specs=[
            pl.BlockSpec((APPLY_TILE, orbs, depth), lambda i: (i, 0, 0)),
            pl.BlockSpec(
                (APPLY_TILE, orbs, depth), lambda i: (jnp.minimum(steps - 1 - i, half - 1), 0, 0)
            ),
        ],
        out_shape=[
            jax.ShapeDtypeStruct((slot_count, orbs, depth), jnp.bfloat16),
            jax.ShapeDtypeStruct((slot_count // 2, orbs, depth), jnp.bfloat16),
        ],
        scratch_shapes=[
            pltpu.VMEM((grid_rows, orbs, depth), jnp.float32),
            pltpu.VMEM((APPLY_TILE, orbs, depth), jnp.float32),
        ],
    )(
        seg_count,
        lines,
        places,
        rows,
        low,
        high,
        potential.reshape(cells_x * cells_y, depth),
        jnp.asarray(band_matrix(depth)),
        order,
    )


def tail_rows(rows, moved, order):
    used, orbs, depth = rows.shape

    def kernel(rows_ref, *refs):
        out_ref, tail_ref, sem = refs[-3:]
        copy = pltpu.make_async_copy(rows_ref.at[pl.ds(used - moved, moved)], tail_ref, sem)
        copy.start()
        copy.wait()

        @pl.loop(0, moved // 16)
        def _(block):
            for u in range(16):
                out_ref[moved - 1 - (block * 16 + u)] = tail_ref[block * 16 + u]

    return call(
        kernel,
        "tail_rows",
        (0, 4),
        in_specs=[untouched()] * (1 + len(order)),
        out_specs=whole_vmem(),
        out_shape=jax.ShapeDtypeStruct((moved, orbs, depth), jnp.bfloat16),
        scratch_shapes=[pltpu.VMEM((moved, orbs, depth), jnp.bfloat16), pltpu.SemaphoreType.DMA],
    )(rows, *order)


def unpack(rows, returned, seg_count, slot_count):
    used, orbs, depth = rows.shape
    steps = slot_count // BIG
    pieces = BIG // TILE
    kept = used // TILE

    def kernel(count_ref, rows_ref, returned_ref, out_ref):
        step = pl.program_id(0)

        @pl.loop(0, pieces)
        def _(piece):
            block = step * pieces + piece
            live = count_ref[0] - block * TILE

            def put(tile):
                row = lax.broadcasted_iota(jnp.int32, tile.shape, 0)
                tile = jnp.where(row < live, tile.astype(jnp.float32), 0.0)
                at = pl.ds(pl.multiple_of(piece * TILE, TILE), TILE)
                out_ref[:, at, :] = jnp.swapaxes(tile, 0, 1).astype(jnp.bfloat16)

            @pl.when(block < kept)
            def _():
                put(rows_ref[pl.ds(block * TILE, TILE)])

            if kept * TILE < slot_count:

                @pl.when(block >= kept)
                def _():
                    put(returned_ref[pl.ds((block - kept) * TILE, TILE)])

    return call(
        kernel,
        "unpack_slots",
        (0, 10),
        grid=(steps,),
        in_specs=[smem(), whole_vmem(), whole_vmem()],
        out_specs=pl.BlockSpec((orbs, BIG, depth), lambda i: (0, i, 0)),
        out_shape=jax.ShapeDtypeStruct((orbs, slot_count, depth), jnp.bfloat16),
    )(seg_count, rows, returned)


def stacked(ref, start, depth):
    value = ref[:, pl.ds(start, SLOTS)].astype(jnp.float32)
    norb = value.shape[0] * value.shape[2]
    tiles = [value[:, u].reshape(norb, depth) for u in range(SLOTS)]
    return jnp.concatenate(tiles, axis=1).astype(jnp.bfloat16)


def gram(left, right, order):
    parts, slots, orbs, depth = left.shape
    norb = parts * orbs
    if orbs % 8 or slots % SLOTS:
        product = jnp.einsum("asoz,bspz->aobp", left, right, preferred_element_type=jnp.float32)
        return product.reshape(norb, norb)
    same = left is right

    def kernel(*refs):
        out_ref = refs[-1]
        out_ref[...] = jnp.zeros_like(out_ref)

        @pl.loop(0, slots // SLOTS)
        def _(block):
            one = stacked(refs[0], block * SLOTS, depth)
            two = one if same else stacked(refs[1], block * SLOTS, depth)
            out_ref[...] += lax.dot_general(
                one, two, (((1,), (1,)), ((), ())), preferred_element_type=jnp.float32
            )

    given = (left,) if same else (left, right)
    return call(
        kernel,
        "gram",
        (1 << 28, 4 * len(given)),
        in_specs=[whole_vmem()] * len(given) + [untouched()] * len(order),
        out_specs=whole_vmem(),
        out_shape=jax.ShapeDtypeStruct((norb, norb), jnp.float32),
    )(*given, *order)


def turn(half, value, order):
    parts, slots, orbs, depth = value.shape
    norb = parts * orbs
    if orbs % 8 or slots % SLOTS:
        blocks = half.reshape(parts, orbs, parts, orbs)
        turned = jnp.einsum("aobp,asoz->bspz", blocks, value, preferred_element_type=jnp.float32)
        return turned.astype(jnp.bfloat16)

    def kernel(half_ref, value_ref, order_ref, out_ref):
        @pl.loop(0, slots // SLOTS)
        def _(block):
            rows = stacked(value_ref, block * SLOTS, depth)
            product = jnp.dot(half_ref[...], rows, preferred_element_type=jnp.float32)
            for u in range(SLOTS):
                tile = product[:, u * depth : (u + 1) * depth].reshape(parts, orbs, depth)
                out_ref[:, block * SLOTS + u] = tile.astype(jnp.bfloat16)

    return call(
        kernel,
        "turn_rows",
        (1 << 28, 8),
        in_specs=[whole_vmem(), whole_vmem(), untouched()],
        out_specs=whole_vmem(),
        out_shape=jax.ShapeDtypeStruct(value.shape, jnp.bfloat16),
    )(half.T, value, order)


def finish(terms, rotation, order):
    def kernel(*refs):
        rotation_ref, transposed_ref = refs[len(terms) : len(terms) + 2]
        hamiltonian = added([ref[...] for ref in refs[: len(terms)]])
        precise = dict(precision=lax.Precision.HIGHEST, preferred_element_type=jnp.float32)
        left = jnp.dot(transposed_ref[...], hamiltonian, **precise)
        refs[-1][...] = jnp.dot(left, rotation_ref[...], **precise)

    return call(
        kernel,
        "finish_hamiltonian",
        (1 << 20, 1),
        in_specs=[whole_vmem()] * (len(terms) + 2) + [untouched()],
        out_specs=whole_vmem(),
        out_shape=jax.ShapeDtypeStruct(rotation.shape, jnp.float32),
    )(*terms, rotation, rotation.T, order)


def body(coeffs, seg_count, seg_lines, potential):
    orbs, slot_count, depth = coeffs.shape
    cells_x, cells_y, _ = potential.shape
    n_orb, n_seg = lax.axis_size("orb"), lax.axis_size("seg")
    ends = n_seg - 1
    norb = n_orb * orbs
    lines = seg_lines[0]
    edge_lines = RADIUS * cells_y
    weight_sum = 2.0 / (n_seg * slot_count * depth)

    first_bits, more_bits = bits("seg")[:2], bits("seg")[2:]
    most = seg_count + swapped(seg_count, "seg", 1)
    if len(first_bits) > 1:
        other = swapped(seg_count, "seg", 2) + swapped(seg_count, "seg", 3)
        most = jnp.maximum(most, other)
    for distance in more_bits:
        most = jnp.maximum(most, swapped(most, "seg", distance))
    rows, turned = pack(coeffs, seg_count)
    live = jnp.arange(slot_count) < seg_count[0]
    tail = lines - (cells_x * cells_y - 2 * edge_lines)
    on_edge = jnp.where(lines < edge_lines, lines, jnp.where(tail >= edge_lines, tail, 2 * edge_lines))
    on_edge = jnp.where(live, on_edge, 2 * edge_lines)
    dump = cells_y + 2 * RADIUS
    places = lines + (lines // cells_y) * PITCH_PAD + RADIUS
    places = jnp.where(live, places, dump)

    def rest(used, operands):
        rows, turned, on_edge, places = operands
        moved = slot_count - used

        def spread(value):
            value = lax.all_to_all(value, "orb", split_axis=0, concat_axis=0, tiled=True)
            return value.reshape(n_orb, used // n_orb, orbs, depth)

        def to_partner(value, turned):
            if not moved:
                return value
            received = swapped(turned[:moved], "seg", 1)
            return merge(value, received, seg_count, used)

        def gather(value):
            value = value.reshape(used, orbs, depth)
            return lax.all_to_all(value, "orb", split_axis=0, concat_axis=0, tiled=True)

        def collect(value, order):
            returned = swapped(tail_rows(value, moved, order), "seg", 1) if moved else value
            return unpack(value, returned, seg_count, slot_count)

        merged = to_partner(rows, turned)
        slot_orbitals = spread(merged)

        edges = edges_of(rows, seg_count, on_edge, merged, edge_lines)
        low = lax.ppermute(
            edges[edge_lines : 2 * edge_lines], "seg", [(i, i + 1) for i in range(ends)]
        )
        high = lax.ppermute(edges[:edge_lines], "seg", [(i + 1, i) for i in range(ends)])
        intersection = total(gram(slot_orbitals, slot_orbitals, (low, high)), ("seg", "orb")) * weight_sum
        rotation = inverse_root(intersection)
        half = rotation.astype(jnp.bfloat16)
        turned_orbitals = turn(half, slot_orbitals, half)

        applied, reversed_applied = apply_rows(
            rows, seg_count, lines, places, low, high, potential, turned_orbitals
        )
        arrived_orbitals = gather(turned_orbitals)
        slot_applied = spread(after(to_partner(applied, reversed_applied), arrived_orbitals))
        rotated_orbitals = collect(arrived_orbitals, (half,))

        turned_applied = turn(half, slot_applied, rotated_orbitals)
        energy = gram(slot_orbitals, slot_applied, (turned_applied,))
        left = bits("orb")
        value = total(energy, ("seg",))
        while len(left) > 1:
            now, left = (left[-2:], left[:-2]) if len(left) > 2 else (left[1:], left[:1])
            value = added(terms_of(value, "orb", now))
        arrived_applied = gather(turned_applied)
        tail = tail_rows(arrived_applied, moved, (value,)) if moved else arrived_applied
        returned = swapped(tail, "seg", 1) if moved else tail
        rotated_hamiltonian = finish(terms_of(value, "orb", left), rotation, tail)
        rotated_applied = unpack(arrived_applied, returned, seg_count, slot_count)
        return rotated_orbitals, rotated_applied, rotated_hamiltonian

    first = slot_count // 2
    classes = [first + TILE * (i + 1) for i in range((slot_count - first) // TILE)]
    chosen = jnp.clip(((most[0] + 1) // 2 - first + TILE - 1) // TILE - 1, 0, len(classes) - 1)
    rotated_orbitals, rotated_applied, rotated_hamiltonian = lax.switch(
        chosen, [functools.partial(rest, used) for used in classes], (rows, turned, on_edge, places)
    )
    return rotated_orbitals, rotated_applied, rotated_hamiltonian * weight_sum


def solution(mesh):
    in_specs = (P("orb", "seg", None), P("seg"), P("seg", None), P("seg", None, None))
    out_specs = (P("orb", "seg", None), P("orb", "seg", None), P())
    return jax.shard_map(body, mesh=mesh, in_specs=in_specs, out_specs=out_specs, check_vma=False)
```

```python
import functools
import math

import jax
import jax.numpy as jnp
import ml_dtypes
import numpy as np
from jax import lax
from jax.experimental import pallas as pl
from jax.experimental.pallas import tpu as pltpu
from jax.sharding import PartitionSpec as P

SWEEPS = 6
RADIUS = 7
KINETIC = -0.5 / 2.25
TILE = 128
APPLY_TILE = 256
BIG = 512
GROUP = 8
SLOTS = 16
PITCH_PAD = 16
VMEM = 60 * 1024 * 1024


def tap_values():
    exact = [-math.pi * math.pi / 3.0]
    exact += [2.0 * (1.0 if k % 2 else -1.0) / (k * k) for k in range(1, RADIUS + 1)]
    return [float(np.float32(v).astype(ml_dtypes.bfloat16)) for v in exact]


TAPS = tap_values()


def band_matrix(n):
    table = np.zeros((n, n), np.float32)
    for i in range(n):
        for j in range(n):
            if abs(i - j) <= RADIUS:
                table[i, j] = TAPS[abs(i - j)]
    return table.astype(ml_dtypes.bfloat16)


def inverse_root(intersection):
    high = lax.Precision.HIGHEST
    norm_scale = jnp.sqrt(jnp.sum(intersection * intersection) + 1e-06)
    identity = jnp.eye(intersection.shape[0], dtype=jnp.float32)
    upper = intersection / norm_scale
    lower = identity
    for sweep_id in range(SWEEPS):
        middle = 0.5 * (3.0 * identity - jnp.dot(lower, upper, precision=high))
        upper = jnp.dot(upper, middle, precision=high)
        lower = jnp.dot(middle, lower, precision=high)
    return lower / jnp.sqrt(norm_scale)


def swapped(value, axis, distance):
    size = lax.axis_size(axis)
    return lax.ppermute(value, axis, [(i, i ^ distance) for i in range(size)])


def bits(axis):
    size = lax.axis_size(axis)
    return [1 << b for b in range(size.bit_length() - 1)]


def terms_of(value, axis, now):
    masks = [0]
    for bit in now:
        masks += [mask | bit for mask in masks]
    return [swapped(value, axis, mask) if mask else value for mask in masks]


def added(terms):
    while len(terms) > 1:
        terms = [p + q for p, q in zip(terms[::2], terms[1::2])]
    return terms[0]


def total(value, axes):
    for axis in axes:
        left = bits(axis)
        while left:
            now, left = left[-2:], left[:-2]
            value = added(terms_of(value, axis, now))
    return value


def call(kernel, name, cost, **kwargs):
    flops, megabytes = cost
    return pl.pallas_call(
        kernel,
        name=name,
        compiler_params=pltpu.CompilerParams(vmem_limit_bytes=VMEM),
        cost_estimate=pl.CostEstimate(
            flops=flops, bytes_accessed=megabytes << 20, transcendentals=0
        ),
        **kwargs,
    )


def smem():
    return pl.BlockSpec(memory_space=pltpu.SMEM)


def untouched():
    return pl.BlockSpec(memory_space=pl.ANY)


def whole_vmem(pieces=1):
    return pl.BlockSpec(memory_space=pltpu.VMEM)


def pack_kernel(first_turned, count_ref, coeffs_ref, rows_ref, turned_ref):
    step = pl.program_id(0)
    tile_rows = rows_ref.shape[0]
    live = count_ref[0] - step * tile_rows
    tile = jnp.swapaxes(coeffs_ref[...].astype(jnp.float32), 0, 1)
    row = lax.broadcasted_iota(jnp.int32, tile.shape, 0)
    rows_ref[...] = jnp.where(row < live, tile, 0.0).astype(jnp.bfloat16)

    @pl.when(step >= first_turned)
    def _():
        @pl.loop(0, tile_rows // 16)
        def _(block):
            for u in range(16):
                j = block * 16 + u
                turned_ref[tile_rows - 1 - j] = rows_ref[j]


def pack(coeffs, seg_count):
    orbs, slot_count, depth = coeffs.shape
    steps = slot_count // BIG
    half = steps // 2
    return call(
        functools.partial(pack_kernel, half),
        "pack_slots",
        (0, 10),
        grid=(steps,),
        in_specs=[smem(), pl.BlockSpec((orbs, BIG, depth), lambda i: (0, i, 0))],
        out_specs=[
            pl.BlockSpec((BIG, orbs, depth), lambda i: (i, 0, 0)),
            pl.BlockSpec(
                (BIG, orbs, depth), lambda i: (jnp.minimum(steps - 1 - i, half - 1), 0, 0)
            ),
        ],
        out_shape=[
            jax.ShapeDtypeStruct((slot_count, orbs, depth), jnp.bfloat16),
            jax.ShapeDtypeStruct((slot_count // 2, orbs, depth), jnp.bfloat16),
        ],
    )(seg_count, coeffs)


def after(value, order):
    def kernel(value_ref, order_ref, out_ref):
        pass

    return call(
        kernel,
        "after",
        (0, 0),
        in_specs=[untouched(), untouched()],
        out_specs=untouched(),
        out_shape=jax.ShapeDtypeStruct(value.shape, value.dtype),
        input_output_aliases={0: 0},
    )(value, order)


def merge(rows, received, seg_count, used):
    slot_count, orbs, depth = rows.shape
    if used == slot_count:
        return rows
    moved = received.shape[0]
    first = used - moved

    def kernel(count_ref, own_ref, other_ref, out_ref, tail_ref, sem_in, sem_out):
        load = pltpu.make_async_copy(own_ref.at[pl.ds(first, moved)], tail_ref, sem_in)
        load.start()
        load.wait()

        @pl.loop(0, moved // TILE)
        def _(block):
            at = pl.ds(block * TILE, TILE)
            live = count_ref[0] - (first + block * TILE)

            @pl.when(live <= 0)
            def _():
                tail_ref[at] = other_ref[at]

            @pl.when((live > 0) & (live < TILE))
            def _():
                row = lax.broadcasted_iota(jnp.int32, (TILE, orbs, depth), 0)
                own, other = tail_ref[at].astype(jnp.float32), other_ref[at].astype(jnp.float32)
                tail_ref[at] = jnp.where(row < live, own, other).astype(jnp.bfloat16)

        store = pltpu.make_async_copy(tail_ref, out_ref.at[pl.ds(first, moved)], sem_out)
        store.start()
        store.wait()

    return call(
        kernel,
        "merge_rows",
        (0, 4),
        in_specs=[smem(), untouched(), whole_vmem()],
        out_specs=untouched(),
        out_shape=jax.ShapeDtypeStruct((used, orbs, depth), jnp.bfloat16),
        scratch_shapes=[
            pltpu.VMEM((moved, orbs, depth), jnp.bfloat16),
            pltpu.SemaphoreType.DMA,
            pltpu.SemaphoreType.DMA,
        ],
        input_output_aliases={1: 0},
    )(seg_count, rows[:used], received)


def edge_kernel(count_ref, place_ref, rows_ref, order_ref, edge_ref):
    count = count_ref[0]

    @pl.loop(0, edge_ref.shape[0] // 8)
    def _(block):
        edge_ref[pl.ds(block * 8, 8)] = jnp.zeros((8,) + edge_ref.shape[1:], edge_ref.dtype)

    @pl.loop(0, lax.div(count + GROUP - 1, GROUP))
    def _(group):
        for u in range(GROUP):
            j = group * GROUP + u
            edge_ref[place_ref[j]] = rows_ref[j]


def edges_of(rows, seg_count, places, order, edge_lines):
    _, orbs, depth = rows.shape
    return call(
        edge_kernel,
        "edge_planes",
        (0, 8),
        in_specs=[smem(), smem(), whole_vmem(), untouched()],
        out_specs=whole_vmem(),
        out_shape=jax.ShapeDtypeStruct((2 * edge_lines + 8, orbs, depth), jnp.bfloat16),
    )(seg_count, places, rows, order)


def apply_kernel(
    cells_x,
    cells_y,
    count_ref,
    lines_ref,
    place_ref,
    rows_ref,
    low_ref,
    high_ref,
    potential_ref,
    band_ref,
    order_ref,
    applied_ref,
    turned_ref,
    grid_ref,
    zsum_ref,
):
    step = pl.program_id(0)
    pitch = cells_y + PITCH_PAD
    count = count_ref[0]
    base = step * APPLY_TILE
    live = jnp.minimum(count - base, APPLY_TILE)
    reach = RADIUS * pitch

    @pl.when(step == 0)
    def _():
        @pl.loop(0, grid_ref.shape[0] // 16)
        def _(block):
            grid_ref[pl.ds(block * 16, 16)] = jnp.zeros((16,) + grid_ref.shape[1:], jnp.float32)

        blocks = cells_y // 16

        @pl.loop(0, RADIUS * blocks)
        def _(index):
            plane = lax.div(index, blocks)
            inside = RADIUS + (index - plane * blocks) * 16
            source = pl.ds(index * 16, 16)
            grid_ref[pl.ds(plane * pitch + inside, 16)] = low_ref[source].astype(jnp.float32)
            above = (plane + RADIUS + cells_x) * pitch + inside
            grid_ref[pl.ds(above, 16)] = high_ref[source].astype(jnp.float32)

        @pl.loop(0, lax.div(count + GROUP - 1, GROUP))
        def _(group):
            first = group * GROUP
            tiles = [(place_ref[first + u], rows_ref[first + u]) for u in range(GROUP)]
            for place, tile in tiles:
                grid_ref[place + reach] = tile.astype(jnp.float32)

    applied_ref[...] = jnp.zeros_like(applied_ref)

    @pl.when(live > 0)
    def _():
        part = APPLY_TILE // 4

        @pl.loop(0, 4)
        def _(block):
            tile = rows_ref[pl.ds(base + block * part, part)].astype(jnp.float32)
            flat = tile.reshape(part * tile.shape[1], tile.shape[2]).astype(jnp.bfloat16)
            zsum = jnp.dot(flat, band_ref[...], preferred_element_type=jnp.float32)
            zsum_ref[pl.ds(block * part, part)] = (KINETIC * zsum).reshape(tile.shape)

        @pl.loop(0, lax.div(live + GROUP - 1, GROUP))
        def _(group):
            values = []
            for u in range(GROUP):
                j = group * GROUP + u
                line = lines_ref[base + j]
                near = grid_ref.at[pl.ds(place_ref[base + j], 2 * reach + 1)]
                terms = [
                    near[reach] * (potential_ref[pl.ds(line, 1), :] + (2.0 * KINETIC * TAPS[0]))
                ]
                for k in range(1, RADIUS + 1):
                    pair = near[reach - k] + near[reach + k]
                    pair = pair + (near[reach - k * pitch] + near[reach + k * pitch])
                    terms.append((KINETIC * TAPS[k]) * pair)
                while len(terms) > 1:
                    terms = [p + q for p, q in zip(terms[::2], terms[1::2])]
                value = terms[0] + zsum_ref[j]
                values.append(jnp.where(j < live, value, 0.0).astype(jnp.bfloat16))
            for u in range(GROUP):
                applied_ref[group * GROUP + u] = values[u]

    @pl.when(step >= pl.num_programs(0) // 2)
    def _():
        @pl.loop(0, APPLY_TILE // 16)
        def _(block):
            for u in range(16):
                j = block * 16 + u
                turned_ref[APPLY_TILE - 1 - j] = applied_ref[j]


def apply_rows(rows, seg_count, lines, places, low, high, potential, order):
    slot_count, orbs, depth = rows.shape
    cells_x, cells_y, _ = potential.shape
    edge_lines = RADIUS * cells_y
    grid_rows = (cells_x + 2 * RADIUS) * (cells_y + PITCH_PAD)
    once = pl.Buffered(1)
    whole = lambda i: (0, 0, 0)
    steps = slot_count // APPLY_TILE
    half = steps // 2
    return call(
        functools.partial(apply_kernel, cells_x, cells_y),
        "apply_rows",
        (2 << 30, 80),
        grid=(steps,),
        in_specs=[
            smem(),
            smem(),
            smem(),
            pl.BlockSpec((slot_count, orbs, depth), whole, pipeline_mode=once),
            pl.BlockSpec((edge_lines, orbs, depth), whole, pipeline_mode=once),
            pl.BlockSpec((edge_lines, orbs, depth), whole, pipeline_mode=once),
            pl.BlockSpec((cells_x * cells_y, depth), lambda i: (0, 0), pipeline_mode=once),
            pl.BlockSpec((depth, depth), lambda i: (0, 0), pipeline_mode=once),
            untouched(),
        ],
        out_specs=[
            pl.BlockSpec((APPLY_TILE, orbs, depth), lambda i: (i, 0, 0)),
            pl.BlockSpec(
                (APPLY_TILE, orbs, depth), lambda i: (jnp.minimum(steps - 1 - i, half - 1), 0, 0)
            ),
        ],
        out_shape=[
            jax.ShapeDtypeStruct((slot_count, orbs, depth), jnp.bfloat16),
            jax.ShapeDtypeStruct((slot_count // 2, orbs, depth), jnp.bfloat16),
        ],
        scratch_shapes=[
            pltpu.VMEM((grid_rows, orbs, depth), jnp.float32),
            pltpu.VMEM((APPLY_TILE, orbs, depth), jnp.float32),
        ],
    )(
        seg_count,
        lines,
        places,
        rows,
        low,
        high,
        potential.reshape(cells_x * cells_y, depth),
        jnp.asarray(band_matrix(depth)),
        order,
    )


def tail_rows(rows, moved, order):
    used, orbs, depth = rows.shape

    def kernel(rows_ref, *refs):
        out_ref, tail_ref, sem = refs[-3:]
        copy = pltpu.make_async_copy(rows_ref.at[pl.ds(used - moved, moved)], tail_ref, sem)
        copy.start()
        copy.wait()

        @pl.loop(0, moved // 16)
        def _(block):
            for u in range(16):
                out_ref[moved - 1 - (block * 16 + u)] = tail_ref[block * 16 + u]

    return call(
        kernel,
        "tail_rows",
        (0, 4),
        in_specs=[untouched()] * (1 + len(order)),
        out_specs=whole_vmem(),
        out_shape=jax.ShapeDtypeStruct((moved, orbs, depth), jnp.bfloat16),
        scratch_shapes=[pltpu.VMEM((moved, orbs, depth), jnp.bfloat16), pltpu.SemaphoreType.DMA],
    )(rows, *order)


def unpack(rows, seg_count, slot_count, first=0, into=None):
    length, orbs, depth = rows.shape
    block_rows = math.gcd(math.gcd(length, first), BIG)
    pieces = block_rows // TILE
    skipped = first // block_rows

    def kernel(count_ref, rows_ref, *refs):
        out_ref = refs[-1]
        step = pl.program_id(0)

        @pl.loop(0, pieces)
        def _(piece):
            live = count_ref[0] - (first + (step * pieces + piece) * TILE)
            at = pl.ds(pl.multiple_of(piece * TILE, TILE), TILE)
            tile = rows_ref[at].astype(jnp.float32)
            row = lax.broadcasted_iota(jnp.int32, tile.shape, 0)
            tile = jnp.where(row < live, tile, 0.0)
            out_ref[:, at, :] = jnp.swapaxes(tile, 0, 1).astype(jnp.bfloat16)

    given = () if into is None else (into,)
    return call(
        kernel,
        "unpack_slots",
        (0, 8),
        grid=(length // block_rows,),
        in_specs=[smem(), pl.BlockSpec((block_rows, orbs, depth), lambda i: (i, 0, 0))]
        + [untouched()] * len(given),
        out_specs=pl.BlockSpec((orbs, block_rows, depth), lambda i: (0, i + skipped, 0)),
        out_shape=jax.ShapeDtypeStruct((orbs, slot_count, depth), jnp.bfloat16),
        input_output_aliases={2: 0} if given else {},
    )(seg_count, rows, *given)


def stacked(ref, start, depth):
    value = ref[:, pl.ds(start, SLOTS)].astype(jnp.float32)
    norb = value.shape[0] * value.shape[2]
    tiles = [value[:, u].reshape(norb, depth) for u in range(SLOTS)]
    return jnp.concatenate(tiles, axis=1).astype(jnp.bfloat16)


def gram(left, right, order):
    parts, slots, orbs, depth = left.shape
    norb = parts * orbs
    if orbs % 8 or slots % SLOTS:
        product = jnp.einsum("asoz,bspz->aobp", left, right, preferred_element_type=jnp.float32)
        return product.reshape(norb, norb)
    same = left is right

    def kernel(*refs):
        out_ref = refs[-1]
        out_ref[...] = jnp.zeros_like(out_ref)

        @pl.loop(0, slots // SLOTS)
        def _(block):
            one = stacked(refs[0], block * SLOTS, depth)
            two = one if same else stacked(refs[1], block * SLOTS, depth)
            out_ref[...] += lax.dot_general(
                one, two, (((1,), (1,)), ((), ())), preferred_element_type=jnp.float32
            )

    given = (left,) if same else (left, right)
    return call(
        kernel,
        "gram",
        (1 << 28, 4 * len(given)),
        in_specs=[whole_vmem()] * len(given) + [untouched()] * len(order),
        out_specs=whole_vmem(),
        out_shape=jax.ShapeDtypeStruct((norb, norb), jnp.float32),
    )(*given, *order)


def turn(half, value, order):
    parts, slots, orbs, depth = value.shape
    norb = parts * orbs
    if orbs % 8 or slots % SLOTS:
        blocks = half.reshape(parts, orbs, parts, orbs)
        turned = jnp.einsum("aobp,asoz->bspz", blocks, value, preferred_element_type=jnp.float32)
        return turned.astype(jnp.bfloat16)

    def kernel(half_ref, value_ref, order_ref, out_ref):
        @pl.loop(0, slots // SLOTS)
        def _(block):
            rows = stacked(value_ref, block * SLOTS, depth)
            product = jnp.dot(half_ref[...], rows, preferred_element_type=jnp.float32)
            for u in range(SLOTS):
                tile = product[:, u * depth : (u + 1) * depth].reshape(parts, orbs, depth)
                out_ref[:, block * SLOTS + u] = tile.astype(jnp.bfloat16)

    return call(
        kernel,
        "turn_rows",
        (1 << 28, 8),
        in_specs=[whole_vmem(), whole_vmem(), untouched()],
        out_specs=whole_vmem(),
        out_shape=jax.ShapeDtypeStruct(value.shape, jnp.bfloat16),
    )(half.T, value, order)


def finish(terms, rotation, order):
    def kernel(*refs):
        rotation_ref, transposed_ref = refs[len(terms) : len(terms) + 2]
        hamiltonian = added([ref[...] for ref in refs[: len(terms)]])
        precise = dict(precision=lax.Precision.HIGHEST, preferred_element_type=jnp.float32)
        left = jnp.dot(transposed_ref[...], hamiltonian, **precise)
        refs[-1][...] = jnp.dot(left, rotation_ref[...], **precise)

    return call(
        kernel,
        "finish_hamiltonian",
        (1 << 20, 1),
        in_specs=[whole_vmem()] * (len(terms) + 2) + [untouched()],
        out_specs=whole_vmem(),
        out_shape=jax.ShapeDtypeStruct(rotation.shape, jnp.float32),
    )(*terms, rotation, rotation.T, order)


def body(coeffs, seg_count, seg_lines, potential):
    orbs, slot_count, depth = coeffs.shape
    cells_x, cells_y, _ = potential.shape
    n_orb, n_seg = lax.axis_size("orb"), lax.axis_size("seg")
    ends = n_seg - 1
    norb = n_orb * orbs
    lines = seg_lines[0]
    edge_lines = RADIUS * cells_y
    weight_sum = 2.0 / (n_seg * slot_count * depth)

    first_bits, more_bits = bits("seg")[:2], bits("seg")[2:]
    most = seg_count + swapped(seg_count, "seg", 1)
    if len(first_bits) > 1:
        other = swapped(seg_count, "seg", 2) + swapped(seg_count, "seg", 3)
        most = jnp.maximum(most, other)
    for distance in more_bits:
        most = jnp.maximum(most, swapped(most, "seg", distance))
    rows, turned = pack(coeffs, seg_count)
    live = jnp.arange(slot_count) < seg_count[0]
    tail = lines - (cells_x * cells_y - 2 * edge_lines)
    on_edge = jnp.where(lines < edge_lines, lines, jnp.where(tail >= edge_lines, tail, 2 * edge_lines))
    on_edge = jnp.where(live, on_edge, 2 * edge_lines)
    dump = cells_y + 2 * RADIUS
    places = lines + (lines // cells_y) * PITCH_PAD + RADIUS
    places = jnp.where(live, places, dump)

    def rest(used, operands):
        rows, turned, on_edge, places = operands
        moved = slot_count - used

        def spread(value):
            value = lax.all_to_all(value, "orb", split_axis=0, concat_axis=0, tiled=True)
            return value.reshape(n_orb, used // n_orb, orbs, depth)

        def to_partner(value, turned):
            if not moved:
                return value
            received = swapped(turned[:moved], "seg", 1)
            return merge(value, received, seg_count, used)

        def gather(value):
            value = value.reshape(used, orbs, depth)
            return lax.all_to_all(value, "orb", split_axis=0, concat_axis=0, tiled=True)

        def collect(value, order):
            if not moved:
                return unpack(value, seg_count, slot_count), value
            tail = tail_rows(value, moved, order)
            returned = swapped(tail, "seg", 1)
            front = unpack(value, seg_count, slot_count)
            return unpack(returned, seg_count, slot_count, used, front), tail

        merged = to_partner(rows, turned)
        slot_orbitals = spread(merged)

        edges = edges_of(rows, seg_count, on_edge, merged, edge_lines)
        low = lax.ppermute(
            edges[edge_lines : 2 * edge_lines], "seg", [(i, i + 1) for i in range(ends)]
        )
        high = lax.ppermute(edges[:edge_lines], "seg", [(i + 1, i) for i in range(ends)])
        intersection = total(gram(slot_orbitals, slot_orbitals, (low, high)), ("seg", "orb")) * weight_sum
        rotation = inverse_root(intersection)
        half = rotation.astype(jnp.bfloat16)
        turned_orbitals = turn(half, slot_orbitals, half)

        applied, reversed_applied = apply_rows(
            rows, seg_count, lines, places, low, high, potential, turned_orbitals
        )
        arrived_orbitals = gather(turned_orbitals)
        slot_applied = spread(after(to_partner(applied, reversed_applied), arrived_orbitals))
        rotated_orbitals, _ = collect(arrived_orbitals, (half,))

        turned_applied = turn(half, slot_applied, rotated_orbitals)
        energy = gram(slot_orbitals, slot_applied, (turned_applied,))
        value = total(energy, ("seg",))
        before, last = bits("orb")[:-2], bits("orb")[-2:]
        while before:
            value, before = added(terms_of(value, "orb", before[-2:])), before[:-2]
        rotated_applied, tail = collect(gather(turned_applied), (value,))
        rotated_hamiltonian = finish(terms_of(value, "orb", last), rotation, tail)
        return rotated_orbitals, rotated_applied, rotated_hamiltonian

    first = slot_count // 2
    grain = slot_count // 8
    classes = [first + grain * (i + 1) for i in range(4)]
    chosen = jnp.clip(((most[0] + 1) // 2 - first + grain - 1) // grain - 1, 0, len(classes) - 1)
    rotated_orbitals, rotated_applied, rotated_hamiltonian = lax.switch(
        chosen, [functools.partial(rest, used) for used in classes], (rows, turned, on_edge, places)
    )
    return rotated_orbitals, rotated_applied, rotated_hamiltonian * weight_sum


def solution(mesh):
    in_specs = (P("orb", "seg", None), P("seg"), P("seg", None), P("seg", None, None))
    out_specs = (P("orb", "seg", None), P("orb", "seg", None), P())
    return jax.shard_map(body, mesh=mesh, in_specs=in_specs, out_specs=out_specs, check_vma=False)
```

```python
import functools
import math

import jax
import jax.numpy as jnp
import ml_dtypes
import numpy as np
from jax import lax
from jax.experimental import pallas as pl
from jax.experimental.pallas import tpu as pltpu
from jax.sharding import PartitionSpec as P

SWEEPS = 6
RADIUS = 7
KINETIC = -0.5 / 2.25
TILE = 128
APPLY_TILE = 256
BIG = 512
GROUP = 8
SLOTS = 16
PITCH_PAD = 16
VMEM = 60 * 1024 * 1024


def tap_values():
    exact = [-math.pi * math.pi / 3.0]
    exact += [2.0 * (1.0 if k % 2 else -1.0) / (k * k) for k in range(1, RADIUS + 1)]
    return [float(np.float32(v).astype(ml_dtypes.bfloat16)) for v in exact]


TAPS = tap_values()


def band_matrix(n):
    table = np.zeros((n, n), np.float32)
    for i in range(n):
        for j in range(n):
            if abs(i - j) <= RADIUS:
                table[i, j] = TAPS[abs(i - j)]
    return table.astype(ml_dtypes.bfloat16)


def inverse_root(intersection):
    high = lax.Precision.HIGHEST
    norm_scale = jnp.sqrt(jnp.sum(intersection * intersection) + 1e-06)
    identity = jnp.eye(intersection.shape[0], dtype=jnp.float32)
    upper = intersection / norm_scale
    lower = identity
    for sweep_id in range(SWEEPS):
        middle = 0.5 * (3.0 * identity - jnp.dot(lower, upper, precision=high))
        upper = jnp.dot(upper, middle, precision=high)
        lower = jnp.dot(middle, lower, precision=high)
    return lower / jnp.sqrt(norm_scale)


def swapped(value, axis, distance):
    size = lax.axis_size(axis)
    return lax.ppermute(value, axis, [(i, i ^ distance) for i in range(size)])


def bits(axis):
    size = lax.axis_size(axis)
    return [1 << b for b in range(size.bit_length() - 1)]


def terms_of(value, axis, now):
    masks = [0]
    for bit in now:
        masks += [mask | bit for mask in masks]
    return [swapped(value, axis, mask) if mask else value for mask in masks]


def added(terms):
    while len(terms) > 1:
        terms = [p + q for p, q in zip(terms[::2], terms[1::2])]
    return terms[0]


def total(value, axes):
    for axis in axes:
        left = bits(axis)
        while left:
            now, left = left[-2:], left[:-2]
            value = added(terms_of(value, axis, now))
    return value


def call(kernel, name, cost, **kwargs):
    flops, megabytes = cost
    return pl.pallas_call(
        kernel,
        name=name,
        compiler_params=pltpu.CompilerParams(vmem_limit_bytes=VMEM),
        cost_estimate=pl.CostEstimate(
            flops=flops, bytes_accessed=megabytes << 20, transcendentals=0
        ),
        **kwargs,
    )


def smem():
    return pl.BlockSpec(memory_space=pltpu.SMEM)


def untouched():
    return pl.BlockSpec(memory_space=pl.ANY)


def whole_vmem(pieces=1):
    return pl.BlockSpec(memory_space=pltpu.VMEM)


def pack_kernel(first_turned, count_ref, coeffs_ref, rows_ref, turned_ref):
    step = pl.program_id(0)
    tile_rows = rows_ref.shape[0]
    live = count_ref[0] - step * tile_rows
    tile = jnp.swapaxes(coeffs_ref[...].astype(jnp.float32), 0, 1)
    row = lax.broadcasted_iota(jnp.int32, tile.shape, 0)
    rows_ref[...] = jnp.where(row < live, tile, 0.0).astype(jnp.bfloat16)

    @pl.when(step >= first_turned)
    def _():
        @pl.loop(0, tile_rows // 16)
        def _(block):
            for u in range(16):
                j = block * 16 + u
                turned_ref[tile_rows - 1 - j] = rows_ref[j]


def pack(coeffs, seg_count):
    orbs, slot_count, depth = coeffs.shape
    steps = slot_count // BIG
    half = steps // 2
    return call(
        functools.partial(pack_kernel, half),
        "pack_slots",
        (0, 10),
        grid=(steps,),
        in_specs=[smem(), pl.BlockSpec((orbs, BIG, depth), lambda i: (0, i, 0))],
        out_specs=[
            pl.BlockSpec((BIG, orbs, depth), lambda i: (i, 0, 0)),
            pl.BlockSpec(
                (BIG, orbs, depth), lambda i: (jnp.minimum(steps - 1 - i, half - 1), 0, 0)
            ),
        ],
        out_shape=[
            jax.ShapeDtypeStruct((slot_count, orbs, depth), jnp.bfloat16),
            jax.ShapeDtypeStruct((slot_count // 2, orbs, depth), jnp.bfloat16),
        ],
    )(seg_count, coeffs)


def after(value, order):
    def kernel(value_ref, order_ref, out_ref):
        pass

    return call(
        kernel,
        "after",
        (0, 0),
        in_specs=[untouched(), untouched()],
        out_specs=untouched(),
        out_shape=jax.ShapeDtypeStruct(value.shape, value.dtype),
        input_output_aliases={0: 0},
    )(value, order)


def merge(rows, received, seg_count, used):
    slot_count, orbs, depth = rows.shape
    if used == slot_count:
        return rows
    moved = received.shape[0]
    first = used - moved

    def kernel(count_ref, own_ref, other_ref, out_ref, tail_ref, sem_in, sem_out):
        load = pltpu.make_async_copy(own_ref.at[pl.ds(first, moved)], tail_ref, sem_in)
        load.start()
        load.wait()

        @pl.loop(0, moved // TILE)
        def _(block):
            at = pl.ds(block * TILE, TILE)
            live = count_ref[0] - (first + block * TILE)

            @pl.when(live <= 0)
            def _():
                tail_ref[at] = other_ref[at]

            @pl.when((live > 0) & (live < TILE))
            def _():
                row = lax.broadcasted_iota(jnp.int32, (TILE, orbs, depth), 0)
                own, other = tail_ref[at].astype(jnp.float32), other_ref[at].astype(jnp.float32)
                tail_ref[at] = jnp.where(row < live, own, other).astype(jnp.bfloat16)

        store = pltpu.make_async_copy(tail_ref, out_ref.at[pl.ds(first, moved)], sem_out)
        store.start()
        store.wait()

    return call(
        kernel,
        "merge_rows",
        (0, 4),
        in_specs=[smem(), untouched(), whole_vmem()],
        out_specs=untouched(),
        out_shape=jax.ShapeDtypeStruct((used, orbs, depth), jnp.bfloat16),
        scratch_shapes=[
            pltpu.VMEM((moved, orbs, depth), jnp.bfloat16),
            pltpu.SemaphoreType.DMA,
            pltpu.SemaphoreType.DMA,
        ],
        input_output_aliases={1: 0},
    )(seg_count, rows[:used], received)


def edge_kernel(count_ref, place_ref, rows_ref, order_ref, edge_ref):
    count = count_ref[0]

    @pl.loop(0, edge_ref.shape[0] // 8)
    def _(block):
        edge_ref[pl.ds(block * 8, 8)] = jnp.zeros((8,) + edge_ref.shape[1:], edge_ref.dtype)

    @pl.loop(0, lax.div(count + GROUP - 1, GROUP))
    def _(group):
        for u in range(GROUP):
            j = group * GROUP + u
            edge_ref[place_ref[j]] = rows_ref[j]


def edges_of(rows, seg_count, places, order, edge_lines):
    _, orbs, depth = rows.shape
    return call(
        edge_kernel,
        "edge_planes",
        (0, 8),
        in_specs=[smem(), smem(), whole_vmem(), untouched()],
        out_specs=whole_vmem(),
        out_shape=jax.ShapeDtypeStruct((2 * edge_lines + 8, orbs, depth), jnp.bfloat16),
    )(seg_count, places, rows, order)


def apply_kernel(
    cells_x,
    cells_y,
    count_ref,
    lines_ref,
    place_ref,
    rows_ref,
    low_ref,
    high_ref,
    potential_ref,
    band_ref,
    order_ref,
    applied_ref,
    turned_ref,
    grid_ref,
    zsum_ref,
):
    step = pl.program_id(0)
    pitch = cells_y + PITCH_PAD
    count = count_ref[0]
    base = step * APPLY_TILE
    live = jnp.minimum(count - base, APPLY_TILE)
    reach = RADIUS * pitch

    @pl.when(step == 0)
    def _():
        @pl.loop(0, grid_ref.shape[0] // 16)
        def _(block):
            grid_ref[pl.ds(block * 16, 16)] = jnp.zeros((16,) + grid_ref.shape[1:], jnp.float32)

        blocks = cells_y // 16

        @pl.loop(0, RADIUS * blocks)
        def _(index):
            plane = lax.div(index, blocks)
            inside = RADIUS + (index - plane * blocks) * 16
            source = pl.ds(index * 16, 16)
            grid_ref[pl.ds(plane * pitch + inside, 16)] = low_ref[source].astype(jnp.float32)
            above = (plane + RADIUS + cells_x) * pitch + inside
            grid_ref[pl.ds(above, 16)] = high_ref[source].astype(jnp.float32)

        @pl.loop(0, lax.div(count + GROUP - 1, GROUP))
        def _(group):
            first = group * GROUP
            tiles = [(place_ref[first + u], rows_ref[first + u]) for u in range(GROUP)]
            for place, tile in tiles:
                grid_ref[place + reach] = tile.astype(jnp.float32)

    applied_ref[...] = jnp.zeros_like(applied_ref)

    @pl.when(live > 0)
    def _():
        part = APPLY_TILE // 4

        @pl.loop(0, 4)
        def _(block):
            tile = rows_ref[pl.ds(base + block * part, part)].astype(jnp.float32)
            flat = tile.reshape(part * tile.shape[1], tile.shape[2]).astype(jnp.bfloat16)
            zsum = jnp.dot(flat, band_ref[...], preferred_element_type=jnp.float32)
            zsum_ref[pl.ds(block * part, part)] = (KINETIC * zsum).reshape(tile.shape)

        @pl.loop(0, lax.div(live + GROUP - 1, GROUP))
        def _(group):
            values = []
            for u in range(GROUP):
                j = group * GROUP + u
                line = lines_ref[base + j]
                near = grid_ref.at[pl.ds(place_ref[base + j], 2 * reach + 1)]
                terms = [
                    near[reach] * (potential_ref[pl.ds(line, 1), :] + (2.0 * KINETIC * TAPS[0]))
                ]
                for k in range(1, RADIUS + 1):
                    pair = near[reach - k] + near[reach + k]
                    pair = pair + (near[reach - k * pitch] + near[reach + k * pitch])
                    terms.append((KINETIC * TAPS[k]) * pair)
                while len(terms) > 1:
                    terms = [p + q for p, q in zip(terms[::2], terms[1::2])]
                value = terms[0] + zsum_ref[j]
                values.append(jnp.where(j < live, value, 0.0).astype(jnp.bfloat16))
            for u in range(GROUP):
                applied_ref[group * GROUP + u] = values[u]

    @pl.when(step >= pl.num_programs(0) // 2)
    def _():
        @pl.loop(0, APPLY_TILE // 16)
        def _(block):
            for u in range(16):
                j = block * 16 + u
                turned_ref[APPLY_TILE - 1 - j] = applied_ref[j]


def apply_rows(rows, seg_count, lines, places, low, high, potential, order):
    slot_count, orbs, depth = rows.shape
    cells_x, cells_y, _ = potential.shape
    edge_lines = RADIUS * cells_y
    grid_rows = (cells_x + 2 * RADIUS) * (cells_y + PITCH_PAD)
    once = pl.Buffered(1)
    whole = lambda i: (0, 0, 0)
    steps = slot_count // APPLY_TILE
    half = steps // 2
    return call(
        functools.partial(apply_kernel, cells_x, cells_y),
        "apply_rows",
        (2 << 30, 80),
        grid=(steps,),
        in_specs=[
            smem(),
            smem(),
            smem(),
            pl.BlockSpec((slot_count, orbs, depth), whole, pipeline_mode=once),
            pl.BlockSpec((edge_lines, orbs, depth), whole, pipeline_mode=once),
            pl.BlockSpec((edge_lines, orbs, depth), whole, pipeline_mode=once),
            pl.BlockSpec((cells_x * cells_y, depth), lambda i: (0, 0), pipeline_mode=once),
            pl.BlockSpec((depth, depth), lambda i: (0, 0), pipeline_mode=once),
            untouched(),
        ],
        out_specs=[
            pl.BlockSpec((APPLY_TILE, orbs, depth), lambda i: (i, 0, 0)),
            pl.BlockSpec(
                (APPLY_TILE, orbs, depth), lambda i: (jnp.minimum(steps - 1 - i, half - 1), 0, 0)
            ),
        ],
        out_shape=[
            jax.ShapeDtypeStruct((slot_count, orbs, depth), jnp.bfloat16),
            jax.ShapeDtypeStruct((slot_count // 2, orbs, depth), jnp.bfloat16),
        ],
        scratch_shapes=[
            pltpu.VMEM((grid_rows, orbs, depth), jnp.float32),
            pltpu.VMEM((APPLY_TILE, orbs, depth), jnp.float32),
        ],
    )(
        seg_count,
        lines,
        places,
        rows,
        low,
        high,
        potential.reshape(cells_x * cells_y, depth),
        jnp.asarray(band_matrix(depth)),
        order,
    )


def tail_rows(rows, moved, order):
    used, orbs, depth = rows.shape

    def kernel(rows_ref, *refs):
        out_ref, tail_ref, sem = refs[-3:]
        copy = pltpu.make_async_copy(rows_ref.at[pl.ds(used - moved, moved)], tail_ref, sem)
        copy.start()
        copy.wait()

        @pl.loop(0, moved // 16)
        def _(block):
            for u in range(16):
                out_ref[moved - 1 - (block * 16 + u)] = tail_ref[block * 16 + u]

    return call(
        kernel,
        "tail_rows",
        (0, 4),
        in_specs=[untouched()] * (1 + len(order)),
        out_specs=whole_vmem(),
        out_shape=jax.ShapeDtypeStruct((moved, orbs, depth), jnp.bfloat16),
        scratch_shapes=[pltpu.VMEM((moved, orbs, depth), jnp.bfloat16), pltpu.SemaphoreType.DMA],
    )(rows, *order)


def unpack(rows, seg_count, slot_count, first=0, into=None):
    length, orbs, depth = rows.shape
    block_rows = math.gcd(math.gcd(length, first), BIG)
    pieces = block_rows // TILE
    skipped = first // block_rows

    def kernel(count_ref, rows_ref, *refs):
        out_ref = refs[-1]
        step = pl.program_id(0)

        @pl.loop(0, pieces)
        def _(piece):
            live = count_ref[0] - (first + (step * pieces + piece) * TILE)
            at = pl.ds(pl.multiple_of(piece * TILE, TILE), TILE)
            tile = rows_ref[at].astype(jnp.float32)
            row = lax.broadcasted_iota(jnp.int32, tile.shape, 0)
            tile = jnp.where(row < live, tile, 0.0)
            out_ref[:, at, :] = jnp.swapaxes(tile, 0, 1).astype(jnp.bfloat16)

    given = () if into is None else (into,)
    return call(
        kernel,
        "unpack_slots",
        (0, 8),
        grid=(length // block_rows,),
        in_specs=[smem(), pl.BlockSpec((block_rows, orbs, depth), lambda i: (i, 0, 0))]
        + [untouched()] * len(given),
        out_specs=pl.BlockSpec((orbs, block_rows, depth), lambda i: (0, i + skipped, 0)),
        out_shape=jax.ShapeDtypeStruct((orbs, slot_count, depth), jnp.bfloat16),
        input_output_aliases={2: 0} if given else {},
    )(seg_count, rows, *given)


def stacked(ref, start, depth):
    value = ref[:, pl.ds(start, SLOTS)].astype(jnp.float32)
    norb = value.shape[0] * value.shape[2]
    tiles = [value[:, u].reshape(norb, depth) for u in range(SLOTS)]
    return jnp.concatenate(tiles, axis=1).astype(jnp.bfloat16)


def gram(left, right, order):
    parts, slots, orbs, depth = left.shape
    norb = parts * orbs
    if orbs % 8 or slots % SLOTS:
        product = jnp.einsum("asoz,bspz->aobp", left, right, preferred_element_type=jnp.float32)
        return product.reshape(norb, norb)
    same = left is right

    def kernel(*refs):
        out_ref = refs[-1]
        out_ref[...] = jnp.zeros_like(out_ref)

        @pl.loop(0, slots // SLOTS)
        def _(block):
            one = stacked(refs[0], block * SLOTS, depth)
            two = one if same else stacked(refs[1], block * SLOTS, depth)
            out_ref[...] += lax.dot_general(
                one, two, (((1,), (1,)), ((), ())), preferred_element_type=jnp.float32
            )

    given = (left,) if same else (left, right)
    return call(
        kernel,
        "gram",
        (1 << 28, 4 * len(given)),
        in_specs=[whole_vmem()] * len(given) + [untouched()] * len(order),
        out_specs=whole_vmem(),
        out_shape=jax.ShapeDtypeStruct((norb, norb), jnp.float32),
    )(*given, *order)


def turn(half, value, order):
    parts, slots, orbs, depth = value.shape
    norb = parts * orbs
    if orbs % 8 or slots % SLOTS:
        blocks = half.reshape(parts, orbs, parts, orbs)
        turned = jnp.einsum("aobp,asoz->bspz", blocks, value, preferred_element_type=jnp.float32)
        return turned.astype(jnp.bfloat16)

    def kernel(half_ref, value_ref, order_ref, out_ref):
        @pl.loop(0, slots // SLOTS)
        def _(block):
            rows = stacked(value_ref, block * SLOTS, depth)
            product = jnp.dot(half_ref[...], rows, preferred_element_type=jnp.float32)
            for u in range(SLOTS):
                tile = product[:, u * depth : (u + 1) * depth].reshape(parts, orbs, depth)
                out_ref[:, block * SLOTS + u] = tile.astype(jnp.bfloat16)

    return call(
        kernel,
        "turn_rows",
        (1 << 28, 8),
        in_specs=[whole_vmem(), whole_vmem(), untouched()],
        out_specs=whole_vmem(),
        out_shape=jax.ShapeDtypeStruct(value.shape, jnp.bfloat16),
    )(half.T, value, order)


def finish(terms, rotation, order):
    def kernel(*refs):
        rotation_ref, transposed_ref = refs[len(terms) : len(terms) + 2]
        hamiltonian = added([ref[...] for ref in refs[: len(terms)]])
        precise = dict(precision=lax.Precision.HIGHEST, preferred_element_type=jnp.float32)
        left = jnp.dot(transposed_ref[...], hamiltonian, **precise)
        refs[-1][...] = jnp.dot(left, rotation_ref[...], **precise)

    return call(
        kernel,
        "finish_hamiltonian",
        (1 << 20, 1),
        in_specs=[whole_vmem()] * (len(terms) + 2) + [untouched()],
        out_specs=whole_vmem(),
        out_shape=jax.ShapeDtypeStruct(rotation.shape, jnp.float32),
    )(*terms, rotation, rotation.T, order)


def body(coeffs, seg_count, seg_lines, potential):
    orbs, slot_count, depth = coeffs.shape
    cells_x, cells_y, _ = potential.shape
    n_orb, n_seg = lax.axis_size("orb"), lax.axis_size("seg")
    ends = n_seg - 1
    norb = n_orb * orbs
    lines = seg_lines[0]
    edge_lines = RADIUS * cells_y
    weight_sum = 2.0 / (n_seg * slot_count * depth)

    first_bits, more_bits = bits("seg")[:2], bits("seg")[2:]
    most = seg_count + swapped(seg_count, "seg", 1)
    if len(first_bits) > 1:
        other = swapped(seg_count, "seg", 2) + swapped(seg_count, "seg", 3)
        most = jnp.maximum(most, other)
    for distance in more_bits:
        most = jnp.maximum(most, swapped(most, "seg", distance))
    rows, turned = pack(coeffs, seg_count)
    live = jnp.arange(slot_count) < seg_count[0]
    tail = lines - (cells_x * cells_y - 2 * edge_lines)
    on_edge = jnp.where(lines < edge_lines, lines, jnp.where(tail >= edge_lines, tail, 2 * edge_lines))
    on_edge = jnp.where(live, on_edge, 2 * edge_lines)
    dump = cells_y + 2 * RADIUS
    places = lines + (lines // cells_y) * PITCH_PAD + RADIUS
    places = jnp.where(live, places, dump)

    def rest(used, operands):
        rows, turned, on_edge, places = operands
        moved = slot_count - used

        def spread(value):
            value = lax.all_to_all(value, "orb", split_axis=0, concat_axis=0, tiled=True)
            return value.reshape(n_orb, used // n_orb, orbs, depth)

        def to_partner(value, turned):
            if not moved:
                return value
            received = swapped(turned[:moved], "seg", 1)
            return merge(value, received, seg_count, used)

        def gather(value):
            value = value.reshape(used, orbs, depth)
            return lax.all_to_all(value, "orb", split_axis=0, concat_axis=0, tiled=True)

        def collect(value, order):
            if not moved:
                return unpack(value, seg_count, slot_count), value
            tail = tail_rows(value, moved, order)
            returned = swapped(tail, "seg", 1)
            front = unpack(value, seg_count, slot_count)
            return unpack(returned, seg_count, slot_count, used, front), tail

        merged = to_partner(rows, turned)
        slot_orbitals = spread(merged)

        edges = edges_of(rows, seg_count, on_edge, merged, edge_lines)
        low = lax.ppermute(
            edges[edge_lines : 2 * edge_lines], "seg", [(i, i + 1) for i in range(ends)]
        )
        high = lax.ppermute(edges[:edge_lines], "seg", [(i + 1, i) for i in range(ends)])
        intersection = total(gram(slot_orbitals, slot_orbitals, (low, high)), ("seg", "orb")) * weight_sum
        rotation = inverse_root(intersection)
        half = rotation.astype(jnp.bfloat16)
        turned_orbitals = turn(half, slot_orbitals, half)

        applied, reversed_applied = apply_rows(
            rows, seg_count, lines, places, low, high, potential, turned_orbitals
        )
        arrived_orbitals = gather(turned_orbitals)
        slot_applied = spread(after(to_partner(applied, reversed_applied), arrived_orbitals))
        rotated_orbitals, _ = collect(arrived_orbitals, (half,))

        turned_applied = turn(half, slot_applied, rotated_orbitals)
        energy = gram(slot_orbitals, slot_applied, (turned_applied,))
        value = total(energy, ("seg",))
        before, last = bits("orb")[:-2], bits("orb")[-2:]
        while before:
            value, before = added(terms_of(value, "orb", before[-2:])), before[:-2]
        rotated_applied, tail = collect(gather(turned_applied), (value,))
        rotated_hamiltonian = finish(terms_of(value, "orb", last), rotation, tail)
        return rotated_orbitals, rotated_applied, rotated_hamiltonian

    needed = (most[0] + 1) // 2
    classes = [slot_count * part // 16 for part in (9, 10, 11, 12, 14, 16)]
    chosen = sum((needed > used).astype(jnp.int32) for used in classes[:-1])
    rotated_orbitals, rotated_applied, rotated_hamiltonian = lax.switch(
        chosen, [functools.partial(rest, used) for used in classes], (rows, turned, on_edge, places)
    )
    return rotated_orbitals, rotated_applied, rotated_hamiltonian * weight_sum


def solution(mesh):
    in_specs = (P("orb", "seg", None), P("seg"), P("seg", None), P("seg", None, None))
    out_specs = (P("orb", "seg", None), P("orb", "seg", None), P())
    return jax.shard_map(body, mesh=mesh, in_specs=in_specs, out_specs=out_specs, check_vma=False)
```

```python
import functools
import math

import jax
import jax.numpy as jnp
import ml_dtypes
import numpy as np
from jax import lax
from jax.experimental import pallas as pl
from jax.experimental.pallas import tpu as pltpu
from jax.sharding import PartitionSpec as P

SWEEPS = 6
RADIUS = 7
KINETIC = -0.5 / 2.25
TILE = 128
APPLY_TILE = 256
BIG = 512
GROUP = 8
SLOTS = 16
PITCH_PAD = 16
VMEM = 60 * 1024 * 1024


def tap_values():
    exact = [-math.pi * math.pi / 3.0]
    exact += [2.0 * (1.0 if k % 2 else -1.0) / (k * k) for k in range(1, RADIUS + 1)]
    return [float(np.float32(v).astype(ml_dtypes.bfloat16)) for v in exact]


TAPS = tap_values()


def band_matrix(n):
    table = np.zeros((n, n), np.float32)
    for i in range(n):
        for j in range(n):
            if abs(i - j) <= RADIUS:
                table[i, j] = TAPS[abs(i - j)]
    return table.astype(ml_dtypes.bfloat16)


def inverse_root(intersection):
    high = lax.Precision.HIGHEST
    norm_scale = jnp.sqrt(jnp.sum(intersection * intersection) + 1e-06)
    identity = jnp.eye(intersection.shape[0], dtype=jnp.float32)
    upper = intersection / norm_scale
    lower = identity
    for sweep_id in range(SWEEPS):
        middle = 0.5 * (3.0 * identity - jnp.dot(lower, upper, precision=high))
        upper = jnp.dot(upper, middle, precision=high)
        lower = jnp.dot(middle, lower, precision=high)
    return lower / jnp.sqrt(norm_scale)


def swapped(value, axis, distance):
    size = lax.axis_size(axis)
    return lax.ppermute(value, axis, [(i, i ^ distance) for i in range(size)])


def bits(axis):
    size = lax.axis_size(axis)
    return [1 << b for b in range(size.bit_length() - 1)]


def terms_of(value, axis, now):
    masks = [0]
    for bit in now:
        masks += [mask | bit for mask in masks]
    return [swapped(value, axis, mask) if mask else value for mask in masks]


def added(terms):
    while len(terms) > 1:
        terms = [p + q for p, q in zip(terms[::2], terms[1::2])]
    return terms[0]


def total(value, axes):
    for axis in axes:
        left = bits(axis)
        while left:
            now, left = left[-2:], left[:-2]
            value = added(terms_of(value, axis, now))
    return value


def call(kernel, name, cost, **kwargs):
    flops, megabytes = cost
    return pl.pallas_call(
        kernel,
        name=name,
        compiler_params=pltpu.CompilerParams(vmem_limit_bytes=VMEM),
        cost_estimate=pl.CostEstimate(
            flops=flops, bytes_accessed=megabytes << 20, transcendentals=0
        ),
        **kwargs,
    )


def smem():
    return pl.BlockSpec(memory_space=pltpu.SMEM)


def untouched():
    return pl.BlockSpec(memory_space=pl.ANY)


def whole_vmem(pieces=1):
    return pl.BlockSpec(memory_space=pltpu.VMEM)


def pack_kernel(first_turned, count_ref, coeffs_ref, rows_ref, turned_ref):
    step = pl.program_id(0)
    tile_rows = rows_ref.shape[0]
    live = count_ref[0] - step * tile_rows
    tile = jnp.swapaxes(coeffs_ref[...].astype(jnp.float32), 0, 1)
    row = lax.broadcasted_iota(jnp.int32, tile.shape, 0)
    rows_ref[...] = jnp.where(row < live, tile, 0.0).astype(jnp.bfloat16)

    @pl.when(step >= first_turned)
    def _():
        @pl.loop(0, tile_rows // 16)
        def _(block):
            for u in range(16):
                j = block * 16 + u
                turned_ref[tile_rows - 1 - j] = rows_ref[j]


def pack(coeffs, seg_count):
    orbs, slot_count, depth = coeffs.shape
    steps = slot_count // BIG
    half = steps // 2
    return call(
        functools.partial(pack_kernel, half),
        "pack_slots",
        (0, 10),
        grid=(steps,),
        in_specs=[smem(), pl.BlockSpec((orbs, BIG, depth), lambda i: (0, i, 0))],
        out_specs=[
            pl.BlockSpec((BIG, orbs, depth), lambda i: (i, 0, 0)),
            pl.BlockSpec(
                (BIG, orbs, depth), lambda i: (jnp.minimum(steps - 1 - i, half - 1), 0, 0)
            ),
        ],
        out_shape=[
            jax.ShapeDtypeStruct((slot_count, orbs, depth), jnp.bfloat16),
            jax.ShapeDtypeStruct((slot_count // 2, orbs, depth), jnp.bfloat16),
        ],
    )(seg_count, coeffs)


def after(value, order):
    def kernel(value_ref, order_ref, out_ref):
        pass

    return call(
        kernel,
        "after",
        (0, 0),
        in_specs=[untouched(), untouched()],
        out_specs=untouched(),
        out_shape=jax.ShapeDtypeStruct(value.shape, value.dtype),
        input_output_aliases={0: 0},
    )(value, order)


def merge(rows, received, seg_count, used):
    slot_count, orbs, depth = rows.shape
    if used == slot_count:
        return rows
    moved = received.shape[0]
    first = used - moved

    def kernel(count_ref, own_ref, other_ref, out_ref, tail_ref, sem_in, sem_out):
        load = pltpu.make_async_copy(own_ref.at[pl.ds(first, moved)], tail_ref, sem_in)
        load.start()
        load.wait()

        @pl.loop(0, moved // TILE)
        def _(block):
            at = pl.ds(block * TILE, TILE)
            live = count_ref[0] - (first + block * TILE)

            @pl.when(live <= 0)
            def _():
                tail_ref[at] = other_ref[at]

            @pl.when((live > 0) & (live < TILE))
            def _():
                row = lax.broadcasted_iota(jnp.int32, (TILE, orbs, depth), 0)
                own, other = tail_ref[at].astype(jnp.float32), other_ref[at].astype(jnp.float32)
                tail_ref[at] = jnp.where(row < live, own, other).astype(jnp.bfloat16)

        store = pltpu.make_async_copy(tail_ref, out_ref.at[pl.ds(first, moved)], sem_out)
        store.start()
        store.wait()

    return call(
        kernel,
        "merge_rows",
        (0, 4),
        in_specs=[smem(), untouched(), whole_vmem()],
        out_specs=untouched(),
        out_shape=jax.ShapeDtypeStruct((used, orbs, depth), jnp.bfloat16),
        scratch_shapes=[
            pltpu.VMEM((moved, orbs, depth), jnp.bfloat16),
            pltpu.SemaphoreType.DMA,
            pltpu.SemaphoreType.DMA,
        ],
        input_output_aliases={1: 0},
    )(seg_count, rows[:used], received)


def edge_kernel(count_ref, place_ref, rows_ref, order_ref, edge_ref):
    count = count_ref[0]

    @pl.loop(0, edge_ref.shape[0] // 8)
    def _(block):
        edge_ref[pl.ds(block * 8, 8)] = jnp.zeros((8,) + edge_ref.shape[1:], edge_ref.dtype)

    @pl.loop(0, lax.div(count + GROUP - 1, GROUP))
    def _(group):
        for u in range(GROUP):
            j = group * GROUP + u
            edge_ref[place_ref[j]] = rows_ref[j]


def edges_of(rows, seg_count, places, order, edge_lines):
    _, orbs, depth = rows.shape
    return call(
        edge_kernel,
        "edge_planes",
        (0, 8),
        in_specs=[smem(), smem(), whole_vmem(), untouched()],
        out_specs=whole_vmem(),
        out_shape=jax.ShapeDtypeStruct((2 * edge_lines + 8, orbs, depth), jnp.bfloat16),
    )(seg_count, places, rows, order)


def apply_kernel(
    cells_x,
    cells_y,
    count_ref,
    lines_ref,
    place_ref,
    rows_ref,
    low_ref,
    high_ref,
    potential_ref,
    band_ref,
    order_ref,
    applied_ref,
    turned_ref,
    grid_ref,
    zsum_ref,
):
    step = pl.program_id(0)
    pitch = cells_y + PITCH_PAD
    count = count_ref[0]
    base = step * APPLY_TILE
    live = jnp.minimum(count - base, APPLY_TILE)
    reach = RADIUS * pitch

    @pl.when(step == 0)
    def _():
        @pl.loop(0, grid_ref.shape[0] // 16)
        def _(block):
            grid_ref[pl.ds(block * 16, 16)] = jnp.zeros((16,) + grid_ref.shape[1:], jnp.float32)

        blocks = cells_y // 16

        @pl.loop(0, RADIUS * blocks)
        def _(index):
            plane = lax.div(index, blocks)
            inside = RADIUS + (index - plane * blocks) * 16
            source = pl.ds(index * 16, 16)
            grid_ref[pl.ds(plane * pitch + inside, 16)] = low_ref[source].astype(jnp.float32)
            above = (plane + RADIUS + cells_x) * pitch + inside
            grid_ref[pl.ds(above, 16)] = high_ref[source].astype(jnp.float32)

        @pl.loop(0, lax.div(count + GROUP - 1, GROUP))
        def _(group):
            first = group * GROUP
            tiles = [(place_ref[first + u], rows_ref[first + u]) for u in range(GROUP)]
            for place, tile in tiles:
                grid_ref[place + reach] = tile.astype(jnp.float32)

    applied_ref[...] = jnp.zeros_like(applied_ref)

    @pl.when(live > 0)
    def _():
        part = APPLY_TILE // 4

        @pl.loop(0, 4)
        def _(block):
            tile = rows_ref[pl.ds(base + block * part, part)].astype(jnp.float32)
            flat = tile.reshape(part * tile.shape[1], tile.shape[2]).astype(jnp.bfloat16)
            zsum = jnp.dot(flat, band_ref[...], preferred_element_type=jnp.float32)
            zsum_ref[pl.ds(block * part, part)] = (KINETIC * zsum).reshape(tile.shape)

        @pl.loop(0, lax.div(live + GROUP - 1, GROUP))
        def _(group):
            values = []
            for u in range(GROUP):
                j = group * GROUP + u
                line = lines_ref[base + j]
                near = grid_ref.at[pl.ds(place_ref[base + j], 2 * reach + 1)]
                terms = [
                    near[reach] * (potential_ref[pl.ds(line, 1), :] + (2.0 * KINETIC * TAPS[0]))
                ]
                for k in range(1, RADIUS + 1):
                    pair = near[reach - k] + near[reach + k]
                    pair = pair + (near[reach - k * pitch] + near[reach + k * pitch])
                    terms.append((KINETIC * TAPS[k]) * pair)
                while len(terms) > 1:
                    terms = [p + q for p, q in zip(terms[::2], terms[1::2])]
                value = terms[0] + zsum_ref[j]
                values.append(jnp.where(j < live, value, 0.0).astype(jnp.bfloat16))
            for u in range(GROUP):
                applied_ref[group * GROUP + u] = values[u]

    @pl.when(step >= pl.num_programs(0) // 2)
    def _():
        @pl.loop(0, APPLY_TILE // 16)
        def _(block):
            for u in range(16):
                j = block * 16 + u
                turned_ref[APPLY_TILE - 1 - j] = applied_ref[j]


def apply_rows(rows, seg_count, lines, places, low, high, potential, order):
    slot_count, orbs, depth = rows.shape
    cells_x, cells_y, _ = potential.shape
    edge_lines = RADIUS * cells_y
    grid_rows = (cells_x + 2 * RADIUS) * (cells_y + PITCH_PAD)
    once = pl.Buffered(1)
    whole = lambda i: (0, 0, 0)
    steps = slot_count // APPLY_TILE
    half = steps // 2
    return call(
        functools.partial(apply_kernel, cells_x, cells_y),
        "apply_rows",
        (2 << 30, 80),
        grid=(steps,),
        in_specs=[
            smem(),
            smem(),
            smem(),
            pl.BlockSpec((slot_count, orbs, depth), whole, pipeline_mode=once),
            pl.BlockSpec((edge_lines, orbs, depth), whole, pipeline_mode=once),
            pl.BlockSpec((edge_lines, orbs, depth), whole, pipeline_mode=once),
            pl.BlockSpec((cells_x * cells_y, depth), lambda i: (0, 0), pipeline_mode=once),
            pl.BlockSpec((depth, depth), lambda i: (0, 0), pipeline_mode=once),
            untouched(),
        ],
        out_specs=[
            pl.BlockSpec((APPLY_TILE, orbs, depth), lambda i: (i, 0, 0)),
            pl.BlockSpec(
                (APPLY_TILE, orbs, depth), lambda i: (jnp.minimum(steps - 1 - i, half - 1), 0, 0)
            ),
        ],
        out_shape=[
            jax.ShapeDtypeStruct((slot_count, orbs, depth), jnp.bfloat16),
            jax.ShapeDtypeStruct((slot_count // 2, orbs, depth), jnp.bfloat16),
        ],
        scratch_shapes=[
            pltpu.VMEM((grid_rows, orbs, depth), jnp.float32),
            pltpu.VMEM((APPLY_TILE, orbs, depth), jnp.float32),
        ],
    )(
        seg_count,
        lines,
        places,
        rows,
        low,
        high,
        potential.reshape(cells_x * cells_y, depth),
        jnp.asarray(band_matrix(depth)),
        order,
    )


def tail_rows(rows, moved, order):
    used, orbs, depth = rows.shape

    def kernel(rows_ref, *refs):
        out_ref, tail_ref, sem = refs[-3:]
        copy = pltpu.make_async_copy(rows_ref.at[pl.ds(used - moved, moved)], tail_ref, sem)
        copy.start()
        copy.wait()

        @pl.loop(0, moved // 16)
        def _(block):
            for u in range(16):
                out_ref[moved - 1 - (block * 16 + u)] = tail_ref[block * 16 + u]

    return call(
        kernel,
        "tail_rows",
        (0, 4),
        in_specs=[untouched()] * (1 + len(order)),
        out_specs=whole_vmem(),
        out_shape=jax.ShapeDtypeStruct((moved, orbs, depth), jnp.bfloat16),
        scratch_shapes=[pltpu.VMEM((moved, orbs, depth), jnp.bfloat16), pltpu.SemaphoreType.DMA],
    )(rows, *order)


def unpack(rows, seg_count, slot_count, first=0, into=None):
    length, orbs, depth = rows.shape
    block_rows = math.gcd(math.gcd(length, first), BIG)
    pieces = block_rows // TILE
    skipped = first // block_rows

    def kernel(count_ref, rows_ref, *refs):
        out_ref = refs[-1]
        step = pl.program_id(0)

        @pl.loop(0, pieces)
        def _(piece):
            live = count_ref[0] - (first + (step * pieces + piece) * TILE)
            at = pl.ds(pl.multiple_of(piece * TILE, TILE), TILE)
            tile = rows_ref[at].astype(jnp.float32)
            row = lax.broadcasted_iota(jnp.int32, tile.shape, 0)
            tile = jnp.where(row < live, tile, 0.0)
            out_ref[:, at, :] = jnp.swapaxes(tile, 0, 1).astype(jnp.bfloat16)

    given = () if into is None else (into,)
    return call(
        kernel,
        "unpack_slots",
        (0, 8),
        grid=(length // block_rows,),
        in_specs=[smem(), pl.BlockSpec((block_rows, orbs, depth), lambda i: (i, 0, 0))]
        + [untouched()] * len(given),
        out_specs=pl.BlockSpec((orbs, block_rows, depth), lambda i: (0, i + skipped, 0)),
        out_shape=jax.ShapeDtypeStruct((orbs, slot_count, depth), jnp.bfloat16),
        input_output_aliases={2: 0} if given else {},
    )(seg_count, rows, *given)


def stacked(ref, start, depth):
    value = ref[:, pl.ds(start, SLOTS)].astype(jnp.float32)
    norb = value.shape[0] * value.shape[2]
    tiles = [value[:, u].reshape(norb, depth) for u in range(SLOTS)]
    return jnp.concatenate(tiles, axis=1).astype(jnp.bfloat16)


def gram(left, right, order):
    parts, slots, orbs, depth = left.shape
    norb = parts * orbs
    if orbs % 8 or slots % SLOTS:
        product = jnp.einsum("asoz,bspz->aobp", left, right, preferred_element_type=jnp.float32)
        return product.reshape(norb, norb)
    same = left is right

    def kernel(*refs):
        out_ref = refs[-1]
        out_ref[...] = jnp.zeros_like(out_ref)

        @pl.loop(0, slots // SLOTS)
        def _(block):
            one = stacked(refs[0], block * SLOTS, depth)
            two = one if same else stacked(refs[1], block * SLOTS, depth)
            out_ref[...] += lax.dot_general(
                one, two, (((1,), (1,)), ((), ())), preferred_element_type=jnp.float32
            )

    given = (left,) if same else (left, right)
    return call(
        kernel,
        "gram",
        (1 << 28, 4 * len(given)),
        in_specs=[whole_vmem()] * len(given) + [untouched()] * len(order),
        out_specs=whole_vmem(),
        out_shape=jax.ShapeDtypeStruct((norb, norb), jnp.float32),
    )(*given, *order)


def turn(half, value, order):
    parts, slots, orbs, depth = value.shape
    norb = parts * orbs
    if orbs % 8 or slots % SLOTS:
        blocks = half.reshape(parts, orbs, parts, orbs)
        turned = jnp.einsum("aobp,asoz->bspz", blocks, value, preferred_element_type=jnp.float32)
        return turned.astype(jnp.bfloat16)

    def kernel(half_ref, value_ref, order_ref, out_ref):
        @pl.loop(0, slots // SLOTS)
        def _(block):
            rows = stacked(value_ref, block * SLOTS, depth)
            product = jnp.dot(half_ref[...], rows, preferred_element_type=jnp.float32)
            for u in range(SLOTS):
                tile = product[:, u * depth : (u + 1) * depth].reshape(parts, orbs, depth)
                out_ref[:, block * SLOTS + u] = tile.astype(jnp.bfloat16)

    return call(
        kernel,
        "turn_rows",
        (1 << 28, 8),
        in_specs=[whole_vmem(), whole_vmem(), untouched()],
        out_specs=whole_vmem(),
        out_shape=jax.ShapeDtypeStruct(value.shape, jnp.bfloat16),
    )(half.T, value, order)


def finish(terms, rotation, order):
    def kernel(*refs):
        rotation_ref, transposed_ref = refs[len(terms) : len(terms) + 2]
        hamiltonian = added([ref[...] for ref in refs[: len(terms)]])
        precise = dict(precision=lax.Precision.HIGHEST, preferred_element_type=jnp.float32)
        left = jnp.dot(transposed_ref[...], hamiltonian, **precise)
        refs[-1][...] = jnp.dot(left, rotation_ref[...], **precise)

    return call(
        kernel,
        "finish_hamiltonian",
        (1 << 20, 1),
        in_specs=[whole_vmem()] * (len(terms) + 2) + [untouched()],
        out_specs=whole_vmem(),
        out_shape=jax.ShapeDtypeStruct(rotation.shape, jnp.float32),
    )(*terms, rotation, rotation.T, order)


def body(coeffs, seg_count, seg_lines, potential):
    orbs, slot_count, depth = coeffs.shape
    cells_x, cells_y, _ = potential.shape
    n_orb, n_seg = lax.axis_size("orb"), lax.axis_size("seg")
    ends = n_seg - 1
    norb = n_orb * orbs
    lines = seg_lines[0]
    edge_lines = RADIUS * cells_y
    weight_sum = 2.0 / (n_seg * slot_count * depth)

    first_bits, more_bits = bits("seg")[:2], bits("seg")[2:]
    most = seg_count + swapped(seg_count, "seg", 1)
    if len(first_bits) > 1:
        other = swapped(seg_count, "seg", 2) + swapped(seg_count, "seg", 3)
        most = jnp.maximum(most, other)
    for distance in more_bits:
        most = jnp.maximum(most, swapped(most, "seg", distance))
    rows, turned = pack(coeffs, seg_count)
    live = jnp.arange(slot_count) < seg_count[0]
    tail = lines - (cells_x * cells_y - 2 * edge_lines)
    on_edge = jnp.where(lines < edge_lines, lines, jnp.where(tail >= edge_lines, tail, 2 * edge_lines))
    on_edge = jnp.where(live, on_edge, 2 * edge_lines)
    dump = cells_y + 2 * RADIUS
    places = lines + (lines // cells_y) * PITCH_PAD + RADIUS
    places = jnp.where(live, places, dump)

    def rest(used, operands):
        rows, turned, on_edge, places = operands
        moved = slot_count - used

        def spread(value):
            value = lax.all_to_all(value, "orb", split_axis=0, concat_axis=0, tiled=True)
            return value.reshape(n_orb, used // n_orb, orbs, depth)

        def to_partner(value, turned):
            if not moved:
                return value
            received = swapped(turned[:moved], "seg", 1)
            return merge(value, received, seg_count, used)

        def gather(value):
            value = value.reshape(used, orbs, depth)
            return lax.all_to_all(value, "orb", split_axis=0, concat_axis=0, tiled=True)

        def collect(value, order):
            if not moved:
                return unpack(value, seg_count, slot_count), value
            tail = tail_rows(value, moved, order)
            returned = swapped(tail, "seg", 1)
            front = unpack(value, seg_count, slot_count)
            return unpack(returned, seg_count, slot_count, used, front), tail

        merged = to_partner(rows, turned)
        slot_orbitals = spread(merged)

        edges = edges_of(rows, seg_count, on_edge, merged, edge_lines)
        low = lax.ppermute(
            edges[edge_lines : 2 * edge_lines], "seg", [(i, i + 1) for i in range(ends)]
        )
        high = lax.ppermute(edges[:edge_lines], "seg", [(i + 1, i) for i in range(ends)])
        intersection = total(gram(slot_orbitals, slot_orbitals, (low, high)), ("seg", "orb")) * weight_sum
        rotation = inverse_root(intersection)
        half = rotation.astype(jnp.bfloat16)
        turned_orbitals = turn(half, slot_orbitals, half)

        applied, reversed_applied = apply_rows(
            rows, seg_count, lines, places, low, high, potential, turned_orbitals
        )
        arrived_orbitals = gather(turned_orbitals)
        slot_applied = spread(after(to_partner(applied, reversed_applied), arrived_orbitals))
        rotated_orbitals, _ = collect(arrived_orbitals, (half,))

        turned_applied = turn(half, slot_applied, rotated_orbitals)
        energy = gram(slot_orbitals, slot_applied, (turned_applied,))
        value = total(energy, ("seg",))
        before, last = bits("orb")[:-2], bits("orb")[-2:]
        while before:
            value, before = added(terms_of(value, "orb", before[-2:])), before[:-2]
        rotated_applied, tail = collect(gather(turned_applied), (value,))
        rotated_hamiltonian = finish(terms_of(value, "orb", last), rotation, tail)
        return rotated_orbitals, rotated_applied, rotated_hamiltonian

    needed = (most[0] + 1) // 2
    classes = [slot_count * part // 16 for part in (16, 14, 12, 11, 10, 9)]
    chosen = sum((needed <= used).astype(jnp.int32) for used in classes[1:])
    rotated_orbitals, rotated_applied, rotated_hamiltonian = lax.switch(
        chosen, [functools.partial(rest, used) for used in classes], (rows, turned, on_edge, places)
    )
    return rotated_orbitals, rotated_applied, rotated_hamiltonian * weight_sum


def solution(mesh):
    in_specs = (P("orb", "seg", None), P("seg"), P("seg", None), P("seg", None, None))
    out_specs = (P("orb", "seg", None), P("orb", "seg", None), P())
    return jax.shard_map(body, mesh=mesh, in_specs=in_specs, out_specs=out_specs, check_vma=False)
```

```python
import functools
import math

import jax
import jax.numpy as jnp
import ml_dtypes
import numpy as np
from jax import lax
from jax.experimental import pallas as pl
from jax.experimental.pallas import tpu as pltpu
from jax.sharding import PartitionSpec as P

SWEEPS = 6
RADIUS = 7
KINETIC = -0.5 / 2.25
TILE = 128
APPLY_TILE = 256
BIG = 512
GROUP = 8
SLOTS = 16
PITCH_PAD = 16
VMEM = 60 * 1024 * 1024


def tap_values():
    exact = [-math.pi * math.pi / 3.0]
    exact += [2.0 * (1.0 if k % 2 else -1.0) / (k * k) for k in range(1, RADIUS + 1)]
    return [float(np.float32(v).astype(ml_dtypes.bfloat16)) for v in exact]


TAPS = tap_values()


def band_matrix(n):
    table = np.zeros((n, n), np.float32)
    for i in range(n):
        for j in range(n):
            if abs(i - j) <= RADIUS:
                table[i, j] = TAPS[abs(i - j)]
    return table.astype(ml_dtypes.bfloat16)


def inverse_root(intersection):
    high = lax.Precision.HIGHEST
    norm_scale = jnp.sqrt(jnp.sum(intersection * intersection) + 1e-06)
    identity = jnp.eye(intersection.shape[0], dtype=jnp.float32)
    upper = intersection / norm_scale
    lower = identity
    for sweep_id in range(SWEEPS):
        middle = 0.5 * (3.0 * identity - jnp.dot(lower, upper, precision=high))
        upper = jnp.dot(upper, middle, precision=high)
        lower = jnp.dot(middle, lower, precision=high)
    return lower / jnp.sqrt(norm_scale)


def swapped(value, axis, distance):
    size = lax.axis_size(axis)
    return lax.ppermute(value, axis, [(i, i ^ distance) for i in range(size)])


def bits(axis):
    size = lax.axis_size(axis)
    return [1 << b for b in range(size.bit_length() - 1)]


def terms_of(value, axis, now):
    masks = [0]
    for bit in now:
        masks += [mask | bit for mask in masks]
    return [swapped(value, axis, mask) if mask else value for mask in masks]


def added(terms):
    while len(terms) > 1:
        terms = [p + q for p, q in zip(terms[::2], terms[1::2])]
    return terms[0]


def total(value, axes):
    for axis in axes:
        left = bits(axis)
        while left:
            now, left = left[-2:], left[:-2]
            value = added(terms_of(value, axis, now))
    return value


def call(kernel, name, cost, **kwargs):
    flops, megabytes = cost
    return pl.pallas_call(
        kernel,
        name=name,
        compiler_params=pltpu.CompilerParams(vmem_limit_bytes=VMEM),
        cost_estimate=pl.CostEstimate(
            flops=flops, bytes_accessed=megabytes << 20, transcendentals=0
        ),
        **kwargs,
    )


def smem():
    return pl.BlockSpec(memory_space=pltpu.SMEM)


def untouched():
    return pl.BlockSpec(memory_space=pl.ANY)


def whole_vmem(pieces=1):
    return pl.BlockSpec(memory_space=pltpu.VMEM)


def pack_kernel(first_turned, count_ref, coeffs_ref, rows_ref, turned_ref):
    step = pl.program_id(0)
    tile_rows = rows_ref.shape[0]
    live = count_ref[0] - step * tile_rows
    tile = jnp.swapaxes(coeffs_ref[...].astype(jnp.float32), 0, 1)
    row = lax.broadcasted_iota(jnp.int32, tile.shape, 0)
    rows_ref[...] = jnp.where(row < live, tile, 0.0).astype(jnp.bfloat16)

    @pl.when(step >= first_turned)
    def _():
        @pl.loop(0, tile_rows // 16)
        def _(block):
            for u in range(16):
                j = block * 16 + u
                turned_ref[tile_rows - 1 - j] = rows_ref[j]


def pack(coeffs, seg_count):
    orbs, slot_count, depth = coeffs.shape
    steps = slot_count // BIG
    half = steps // 2
    return call(
        functools.partial(pack_kernel, half),
        "pack_slots",
        (0, 10),
        grid=(steps,),
        in_specs=[smem(), pl.BlockSpec((orbs, BIG, depth), lambda i: (0, i, 0))],
        out_specs=[
            pl.BlockSpec((BIG, orbs, depth), lambda i: (i, 0, 0)),
            pl.BlockSpec(
                (BIG, orbs, depth), lambda i: (jnp.minimum(steps - 1 - i, half - 1), 0, 0)
            ),
        ],
        out_shape=[
            jax.ShapeDtypeStruct((slot_count, orbs, depth), jnp.bfloat16),
            jax.ShapeDtypeStruct((slot_count // 2, orbs, depth), jnp.bfloat16),
        ],
    )(seg_count, coeffs)


def after(value, order):
    def kernel(value_ref, order_ref, out_ref):
        pass

    return call(
        kernel,
        "after",
        (0, 0),
        in_specs=[untouched(), untouched()],
        out_specs=untouched(),
        out_shape=jax.ShapeDtypeStruct(value.shape, value.dtype),
        input_output_aliases={0: 0},
    )(value, order)


def merge(rows, received, seg_count, used):
    slot_count, orbs, depth = rows.shape
    if used == slot_count:
        return rows
    moved = received.shape[0]
    first = used - moved

    def kernel(count_ref, own_ref, other_ref, out_ref, tail_ref, sem_in, sem_out):
        load = pltpu.make_async_copy(own_ref.at[pl.ds(first, moved)], tail_ref, sem_in)
        load.start()
        load.wait()

        @pl.loop(0, moved // TILE)
        def _(block):
            at = pl.ds(block * TILE, TILE)
            live = count_ref[0] - (first + block * TILE)

            @pl.when(live <= 0)
            def _():
                tail_ref[at] = other_ref[at]

            @pl.when((live > 0) & (live < TILE))
            def _():
                row = lax.broadcasted_iota(jnp.int32, (TILE, orbs, depth), 0)
                own, other = tail_ref[at].astype(jnp.float32), other_ref[at].astype(jnp.float32)
                tail_ref[at] = jnp.where(row < live, own, other).astype(jnp.bfloat16)

        store = pltpu.make_async_copy(tail_ref, out_ref.at[pl.ds(first, moved)], sem_out)
        store.start()
        store.wait()

    return call(
        kernel,
        "merge_rows",
        (0, 4),
        in_specs=[smem(), untouched(), whole_vmem()],
        out_specs=untouched(),
        out_shape=jax.ShapeDtypeStruct((used, orbs, depth), jnp.bfloat16),
        scratch_shapes=[
            pltpu.VMEM((moved, orbs, depth), jnp.bfloat16),
            pltpu.SemaphoreType.DMA,
            pltpu.SemaphoreType.DMA,
        ],
        input_output_aliases={1: 0},
    )(seg_count, rows[:used], received)


def edge_kernel(count_ref, place_ref, rows_ref, order_ref, edge_ref):
    count = count_ref[0]

    @pl.loop(0, edge_ref.shape[0] // 8)
    def _(block):
        edge_ref[pl.ds(block * 8, 8)] = jnp.zeros((8,) + edge_ref.shape[1:], edge_ref.dtype)

    @pl.loop(0, lax.div(count + GROUP - 1, GROUP))
    def _(group):
        for u in range(GROUP):
            j = group * GROUP + u
            edge_ref[place_ref[j]] = rows_ref[j]


def edges_of(rows, seg_count, places, order, edge_lines):
    _, orbs, depth = rows.shape
    return call(
        edge_kernel,
        "edge_planes",
        (0, 8),
        in_specs=[smem(), smem(), whole_vmem(), untouched()],
        out_specs=whole_vmem(),
        out_shape=jax.ShapeDtypeStruct((2 * edge_lines + 8, orbs, depth), jnp.bfloat16),
    )(seg_count, places, rows, order)


def apply_kernel(
    cells_x,
    cells_y,
    count_ref,
    lines_ref,
    place_ref,
    rows_ref,
    low_ref,
    high_ref,
    potential_ref,
    band_ref,
    order_ref,
    applied_ref,
    turned_ref,
    grid_ref,
    zsum_ref,
):
    step = pl.program_id(0)
    pitch = cells_y + PITCH_PAD
    count = count_ref[0]
    base = step * APPLY_TILE
    live = jnp.minimum(count - base, APPLY_TILE)
    reach = RADIUS * pitch

    @pl.when(step == 0)
    def _():
        @pl.loop(0, grid_ref.shape[0] // 16)
        def _(block):
            grid_ref[pl.ds(block * 16, 16)] = jnp.zeros((16,) + grid_ref.shape[1:], jnp.float32)

        blocks = cells_y // 16

        @pl.loop(0, RADIUS * blocks)
        def _(index):
            plane = lax.div(index, blocks)
            inside = RADIUS + (index - plane * blocks) * 16
            source = pl.ds(index * 16, 16)
            grid_ref[pl.ds(plane * pitch + inside, 16)] = low_ref[source].astype(jnp.float32)
            above = (plane + RADIUS + cells_x) * pitch + inside
            grid_ref[pl.ds(above, 16)] = high_ref[source].astype(jnp.float32)

        @pl.loop(0, lax.div(count + GROUP - 1, GROUP))
        def _(group):
            first = group * GROUP
            tiles = [(place_ref[first + u], rows_ref[first + u]) for u in range(GROUP)]
            for place, tile in tiles:
                grid_ref[place + reach] = tile.astype(jnp.float32)

    applied_ref[...] = jnp.zeros_like(applied_ref)

    @pl.when(live > 0)
    def _():
        part = APPLY_TILE // 4

        @pl.loop(0, 4)
        def _(block):
            tile = rows_ref[pl.ds(base + block * part, part)].astype(jnp.float32)
            flat = tile.reshape(part * tile.shape[1], tile.shape[2]).astype(jnp.bfloat16)
            zsum = jnp.dot(flat, band_ref[...], preferred_element_type=jnp.float32)
            zsum_ref[pl.ds(block * part, part)] = (KINETIC * zsum).reshape(tile.shape)

        @pl.loop(0, lax.div(live + GROUP - 1, GROUP))
        def _(group):
            values = []
            for u in range(GROUP):
                j = group * GROUP + u
                line = lines_ref[base + j]
                near = grid_ref.at[pl.ds(place_ref[base + j], 2 * reach + 1)]
                terms = [
                    near[reach] * (potential_ref[pl.ds(line, 1), :] + (2.0 * KINETIC * TAPS[0]))
                ]
                for k in range(1, RADIUS + 1):
                    pair = near[reach - k] + near[reach + k]
                    pair = pair + (near[reach - k * pitch] + near[reach + k * pitch])
                    terms.append((KINETIC * TAPS[k]) * pair)
                while len(terms) > 1:
                    terms = [p + q for p, q in zip(terms[::2], terms[1::2])]
                value = terms[0] + zsum_ref[j]
                values.append(jnp.where(j < live, value, 0.0).astype(jnp.bfloat16))
            for u in range(GROUP):
                applied_ref[group * GROUP + u] = values[u]

    @pl.when(step >= pl.num_programs(0) // 2)
    def _():
        @pl.loop(0, APPLY_TILE // 16)
        def _(block):
            for u in range(16):
                j = block * 16 + u
                turned_ref[APPLY_TILE - 1 - j] = applied_ref[j]


def apply_rows(rows, seg_count, lines, places, low, high, potential, order):
    slot_count, orbs, depth = rows.shape
    cells_x, cells_y, _ = potential.shape
    edge_lines = RADIUS * cells_y
    grid_rows = (cells_x + 2 * RADIUS) * (cells_y + PITCH_PAD)
    once = pl.Buffered(1)
    whole = lambda i: (0, 0, 0)
    steps = slot_count // APPLY_TILE
    half = steps // 2
    return call(
        functools.partial(apply_kernel, cells_x, cells_y),
        "apply_rows",
        (2 << 30, 80),
        grid=(steps,),
        in_specs=[
            smem(),
            smem(),
            smem(),
            pl.BlockSpec((slot_count, orbs, depth), whole, pipeline_mode=once),
            pl.BlockSpec((edge_lines, orbs, depth), whole, pipeline_mode=once),
            pl.BlockSpec((edge_lines, orbs, depth), whole, pipeline_mode=once),
            pl.BlockSpec((cells_x * cells_y, depth), lambda i: (0, 0), pipeline_mode=once),
            pl.BlockSpec((depth, depth), lambda i: (0, 0), pipeline_mode=once),
            untouched(),
        ],
        out_specs=[
            pl.BlockSpec((APPLY_TILE, orbs, depth), lambda i: (i, 0, 0)),
            pl.BlockSpec(
                (APPLY_TILE, orbs, depth), lambda i: (jnp.minimum(steps - 1 - i, half - 1), 0, 0)
            ),
        ],
        out_shape=[
            jax.ShapeDtypeStruct((slot_count, orbs, depth), jnp.bfloat16),
            jax.ShapeDtypeStruct((slot_count // 2, orbs, depth), jnp.bfloat16),
        ],
        scratch_shapes=[
            pltpu.VMEM((grid_rows, orbs, depth), jnp.float32),
            pltpu.VMEM((APPLY_TILE, orbs, depth), jnp.float32),
        ],
    )(
        seg_count,
        lines,
        places,
        rows,
        low,
        high,
        potential.reshape(cells_x * cells_y, depth),
        jnp.asarray(band_matrix(depth)),
        order,
    )


def tail_rows(rows, moved, order):
    used, orbs, depth = rows.shape

    def kernel(rows_ref, *refs):
        out_ref, tail_ref, sem = refs[-3:]
        copy = pltpu.make_async_copy(rows_ref.at[pl.ds(used - moved, moved)], tail_ref, sem)
        copy.start()
        copy.wait()

        @pl.loop(0, moved // 16)
        def _(block):
            for u in range(16):
                out_ref[moved - 1 - (block * 16 + u)] = tail_ref[block * 16 + u]

    return call(
        kernel,
        "tail_rows",
        (0, 4),
        in_specs=[untouched()] * (1 + len(order)),
        out_specs=whole_vmem(),
        out_shape=jax.ShapeDtypeStruct((moved, orbs, depth), jnp.bfloat16),
        scratch_shapes=[pltpu.VMEM((moved, orbs, depth), jnp.bfloat16), pltpu.SemaphoreType.DMA],
    )(rows, *order)


def unpack(rows, seg_count, slot_count, first=0, into=None):
    length, orbs, depth = rows.shape
    block_rows = math.gcd(math.gcd(length, first), BIG)
    pieces = block_rows // TILE
    skipped = first // block_rows

    def kernel(count_ref, rows_ref, *refs):
        out_ref = refs[-1]
        step = pl.program_id(0)

        @pl.loop(0, pieces)
        def _(piece):
            live = count_ref[0] - (first + (step * pieces + piece) * TILE)
            at = pl.ds(pl.multiple_of(piece * TILE, TILE), TILE)
            tile = rows_ref[at].astype(jnp.float32)
            row = lax.broadcasted_iota(jnp.int32, tile.shape, 0)
            tile = jnp.where(row < live, tile, 0.0)
            out_ref[:, at, :] = jnp.swapaxes(tile, 0, 1).astype(jnp.bfloat16)

    given = () if into is None else (into,)
    return call(
        kernel,
        "unpack_slots",
        (0, 8),
        grid=(length // block_rows,),
        in_specs=[smem(), pl.BlockSpec((block_rows, orbs, depth), lambda i: (i, 0, 0))]
        + [untouched()] * len(given),
        out_specs=pl.BlockSpec((orbs, block_rows, depth), lambda i: (0, i + skipped, 0)),
        out_shape=jax.ShapeDtypeStruct((orbs, slot_count, depth), jnp.bfloat16),
        input_output_aliases={2: 0} if given else {},
    )(seg_count, rows, *given)


def stacked(ref, start, depth):
    value = ref[:, pl.ds(start, SLOTS)].astype(jnp.float32)
    norb = value.shape[0] * value.shape[2]
    tiles = [value[:, u].reshape(norb, depth) for u in range(SLOTS)]
    return jnp.concatenate(tiles, axis=1).astype(jnp.bfloat16)


def gram(left, right, order):
    parts, slots, orbs, depth = left.shape
    norb = parts * orbs
    if orbs % 8 or slots % SLOTS:
        product = jnp.einsum("asoz,bspz->aobp", left, right, preferred_element_type=jnp.float32)
        return product.reshape(norb, norb)
    same = left is right

    def kernel(*refs):
        out_ref = refs[-1]
        out_ref[...] = jnp.zeros_like(out_ref)

        @pl.loop(0, slots // SLOTS)
        def _(block):
            one = stacked(refs[0], block * SLOTS, depth)
            two = one if same else stacked(refs[1], block * SLOTS, depth)
            out_ref[...] += lax.dot_general(
                one, two, (((1,), (1,)), ((), ())), preferred_element_type=jnp.float32
            )

    given = (left,) if same else (left, right)
    return call(
        kernel,
        "gram",
        (1 << 28, 4 * len(given)),
        in_specs=[whole_vmem()] * len(given) + [untouched()] * len(order),
        out_specs=whole_vmem(),
        out_shape=jax.ShapeDtypeStruct((norb, norb), jnp.float32),
    )(*given, *order)


def turn(half, value, order):
    parts, slots, orbs, depth = value.shape
    norb = parts * orbs
    if orbs % 8 or slots % SLOTS:
        blocks = half.reshape(parts, orbs, parts, orbs)
        turned = jnp.einsum("aobp,asoz->bspz", blocks, value, preferred_element_type=jnp.float32)
        return turned.astype(jnp.bfloat16)

    def kernel(half_ref, value_ref, order_ref, out_ref):
        @pl.loop(0, slots // SLOTS)
        def _(block):
            rows = stacked(value_ref, block * SLOTS, depth)
            product = jnp.dot(half_ref[...], rows, preferred_element_type=jnp.float32)
            for u in range(SLOTS):
                tile = product[:, u * depth : (u + 1) * depth].reshape(parts, orbs, depth)
                out_ref[:, block * SLOTS + u] = tile.astype(jnp.bfloat16)

    return call(
        kernel,
        "turn_rows",
        (1 << 28, 8),
        in_specs=[whole_vmem(), whole_vmem(), untouched()],
        out_specs=whole_vmem(),
        out_shape=jax.ShapeDtypeStruct(value.shape, jnp.bfloat16),
    )(half.T, value, order)


def finish(terms, rotation, order):
    def kernel(*refs):
        rotation_ref, transposed_ref = refs[len(terms) : len(terms) + 2]
        hamiltonian = added([ref[...] for ref in refs[: len(terms)]])
        precise = dict(precision=lax.Precision.HIGHEST, preferred_element_type=jnp.float32)
        left = jnp.dot(transposed_ref[...], hamiltonian, **precise)
        refs[-1][...] = jnp.dot(left, rotation_ref[...], **precise)

    return call(
        kernel,
        "finish_hamiltonian",
        (1 << 20, 1),
        in_specs=[whole_vmem()] * (len(terms) + 2) + [untouched()],
        out_specs=whole_vmem(),
        out_shape=jax.ShapeDtypeStruct(rotation.shape, jnp.float32),
    )(*terms, rotation, rotation.T, order)


def body(coeffs, seg_count, seg_lines, potential):
    orbs, slot_count, depth = coeffs.shape
    cells_x, cells_y, _ = potential.shape
    n_orb, n_seg = lax.axis_size("orb"), lax.axis_size("seg")
    ends = n_seg - 1
    norb = n_orb * orbs
    lines = seg_lines[0]
    edge_lines = RADIUS * cells_y
    weight_sum = 2.0 / (n_seg * slot_count * depth)

    first_bits, more_bits = bits("seg")[:2], bits("seg")[2:]
    most = seg_count + swapped(seg_count, "seg", 1)
    if len(first_bits) > 1:
        other = swapped(seg_count, "seg", 2) + swapped(seg_count, "seg", 3)
        most = jnp.maximum(most, other)
    for distance in more_bits:
        most = jnp.maximum(most, swapped(most, "seg", distance))
    rows, turned = pack(coeffs, seg_count)
    live = jnp.arange(slot_count) < seg_count[0]
    tail = lines - (cells_x * cells_y - 2 * edge_lines)
    on_edge = jnp.where(lines < edge_lines, lines, jnp.where(tail >= edge_lines, tail, 2 * edge_lines))
    on_edge = jnp.where(live, on_edge, 2 * edge_lines)
    dump = cells_y + 2 * RADIUS
    places = lines + (lines // cells_y) * PITCH_PAD + RADIUS
    places = jnp.where(live, places, dump)

    def rest(used, operands):
        rows, turned, on_edge, places = operands
        moved = slot_count - used

        def spread(value):
            value = lax.all_to_all(value, "orb", split_axis=0, concat_axis=0, tiled=True)
            return value.reshape(n_orb, used // n_orb, orbs, depth)

        def to_partner(value, turned):
            if not moved:
                return value
            received = swapped(turned[:moved], "seg", 1)
            return merge(value, received, seg_count, used)

        def gather(value):
            value = value.reshape(used, orbs, depth)
            return lax.all_to_all(value, "orb", split_axis=0, concat_axis=0, tiled=True)

        def collect(value, order):
            if not moved:
                return unpack(value, seg_count, slot_count), value, value
            tail = tail_rows(value, moved, order)
            returned = swapped(tail, "seg", 1)
            front = unpack(value, seg_count, slot_count)
            return unpack(returned, seg_count, slot_count, used, front), tail, front

        merged = to_partner(rows, turned)
        slot_orbitals = spread(merged)

        edges = edges_of(rows, seg_count, on_edge, merged, edge_lines)
        low = lax.ppermute(
            edges[edge_lines : 2 * edge_lines], "seg", [(i, i + 1) for i in range(ends)]
        )
        high = lax.ppermute(edges[:edge_lines], "seg", [(i + 1, i) for i in range(ends)])
        intersection = total(gram(slot_orbitals, slot_orbitals, (low, high)), ("seg", "orb")) * weight_sum
        rotation = inverse_root(intersection)
        half = rotation.astype(jnp.bfloat16)
        turned_orbitals = turn(half, slot_orbitals, half)

        applied, reversed_applied = apply_rows(
            rows, seg_count, lines, places, low, high, potential, turned_orbitals
        )
        arrived_orbitals = gather(turned_orbitals)
        slot_applied = spread(after(to_partner(applied, reversed_applied), arrived_orbitals))
        rotated_orbitals, _, _ = collect(arrived_orbitals, (half,))

        turned_applied = turn(half, slot_applied, rotated_orbitals)
        energy = gram(slot_orbitals, slot_applied, (turned_applied,))
        value = total(energy, ("seg",))
        before, last = bits("orb")[:-2], bits("orb")[-2:]
        while before:
            value, before = added(terms_of(value, "orb", before[-2:])), before[:-2]
        rotated_applied, tail, front = collect(gather(turned_applied), (value,))
        value = after(value, front)
        rotated_hamiltonian = finish(terms_of(value, "orb", last), rotation, tail)
        return rotated_orbitals, rotated_applied, rotated_hamiltonian

    first = slot_count // 2
    grain = slot_count // 8
    classes = [first + grain * (i + 1) for i in range(4)]
    chosen = jnp.clip(((most[0] + 1) // 2 - first + grain - 1) // grain - 1, 0, len(classes) - 1)
    rotated_orbitals, rotated_applied, rotated_hamiltonian = lax.switch(
        chosen, [functools.partial(rest, used) for used in classes], (rows, turned, on_edge, places)
    )
    return rotated_orbitals, rotated_applied, rotated_hamiltonian * weight_sum


def solution(mesh):
    in_specs = (P("orb", "seg", None), P("seg"), P("seg", None), P("seg", None, None))
    out_specs = (P("orb", "seg", None), P("orb", "seg", None), P())
    return jax.shard_map(body, mesh=mesh, in_specs=in_specs, out_specs=out_specs, check_vma=False)
```
